512 devices in a mesh: tile: 32 (over x, y), lev: 8 (over z_lo, core), var: 2 (over z_hi).
Axes of the slice: x: 4, y: 8, z: 8 (z_hi: 2, z_lo: 4; z = z_hi * 4 + z_lo), core: 2. Of those that a mesh axis runs over, the one named last changes fastest.
Arguments:
- background: float32 [2, 8, 256, 4096], P('var', 'lev', 'tile'), may hold values from -6 to 6
- norm_factor: float32 [2, 8, 256, 4096], P('var', 'lev', 'tile'), may hold values from 0.05 to 15, as said below
- v_diffusivity: float32 [2, 8, 256, 4096], P('var', None, 'tile', 'lev'), may hold values from 0.5 to 20
- h_diffusivity: float32 [2, 8], P('var', 'lev'), may hold values from 20 to 400
- sea_mask: int32 [8, 256, 4096], P('lev', 'tile'), may hold values 0 or 1
- fold_order: int32 [4096], replicated, may hold values from 0 to 4095, each once
- coupling: float32 [2, 8, 256, 4096], P('var', 'lev', 'tile'), may hold values from -1 to 1
Outputs:
- balanced: float32 [2, 8, 256, 4096], P('var', 'lev', 'tile')
The draws below stay inside these ranges and needn't reach their ends.
Inputs may be any that keep to these rules, and one draw needn't show every extreme that they name: `norm_factor`: positive normalisation factors.
All inputs are finite; a program needn't handle non-finite values. No bound on the sum of `sea_mask` on one device may be relied on, other than what follows from the above.
Results may differ from the reference program's by a relative error of at most 0.00035.
Values sent between devices are 32-bit elements; how exact they have to be, the bound alone decides.
A program may use at most 64 MiB of HBM per device.

```python
import math
import jax
import jax.numpy as jnp
from jax import lax

NX = 4096
ITERS = 10
VARS = 2
LEVELS = 8
NY = 256


def draw_norm_factor(key, part):
    key = jax.random.fold_in(key, 11)
    key_cell, key_row, key_col = jax.random.split(key, 3)
    row_pos = (jnp.arange(NY, dtype=jnp.float32) / NY)[:, None]
    row_noise = jax.random.uniform(key_row, (VARS, LEVELS, NY, 1), jnp.float32)
    col_exponent = jax.random.uniform(key_col, (VARS, LEVELS, 1, NX), jnp.float32)
    cell = jax.random.uniform(key_cell, (VARS, LEVELS, NY, NX), jnp.float32, 0.5, 1.5)
    row_exponent = 0.5 * row_pos + 0.5 * row_noise
    return 0.1 * cell * jnp.power(10.0, row_exponent) * jnp.power(10.0, col_exponent)


def with_ends(drawn, own_key, low, top_value):
    longest = drawn.shape.index(max(drawn.shape))
    spots = []
    for shift in (0, 1):
        where = [jax.random.randint(jax.random.fold_in(own_key, axis), (), 0, length) for axis, length in enumerate(drawn.shape)]
        where[longest] = (where[longest] + shift) % drawn.shape[longest]
        spots.append(tuple(where))
    return drawn.at[spots[0]].set(low).at[spots[1]].set(top_value)


def steps_of(own_key, dims, cuts, low, high):
    factor_of, own = 1.0, jax.random.fold_in(own_key, 6)
    for position, parts in cuts:
        heights = jnp.exp(jax.random.uniform(jax.random.fold_in(own, position), (parts,), jnp.float32, low / len(cuts), high / len(cuts)))
        factor_of = factor_of * jnp.repeat(heights, dims[position] // parts).reshape([-1 if axis == position else 1 for axis in range(len(dims))])
    return factor_of


def bell_draw(own_key, extent, scale, limit, shards=(), kind=jnp.bfloat16):
    loudness = steps_of(own_key, extent, shards, -0.22, 0.18) if shards else 1.0
    result = jax.random.normal(own_key, extent, jnp.float32) * scale * loudness
    return jnp.minimum(jnp.maximum(result, -limit), limit).astype(kind)


def setup_inputs(seed: int = 0) -> dict:
    arg_keys = jax.random.split(jax.random.key(seed), 8)
    return {
        "background": bell_draw(arg_keys[0], (VARS, LEVELS, NY, NX), 1.0, 6.0, ((0, 2), (1, 8), (2, 32)), jnp.float32),
        "norm_factor": draw_norm_factor(jax.random.fold_in(arg_keys[7], 71), 0),
        "v_diffusivity": jnp.clip(jnp.exp(math.log(20.0) - 3.6888795 * jax.random.uniform(arg_keys[2], (VARS, LEVELS, NY, NX), jnp.float32) ** steps_of(arg_keys[2], (VARS, LEVELS, NY, NX), ((0, 2), (2, 32), (3, 8)), -0.2, 0.2)), 0.5, 20.0),
        "h_diffusivity": jnp.clip(jnp.exp(math.log(400.0) - 2.9957323 * jax.random.uniform(arg_keys[3], (VARS, LEVELS), jnp.float32) ** steps_of(arg_keys[3], (VARS, LEVELS), ((0, 2), (1, 8)), -0.2, 0.2)), 20.0, 400.0),
        "sea_mask": with_ends((jax.random.randint(arg_keys[4], (LEVELS, NY, NX), 0, 4) < 3).astype(jnp.int32), jax.random.fold_in(arg_keys[4], 1), 0, 1),
        "fold_order": jax.random.permutation(arg_keys[5], NX).astype(jnp.int32),
        "coupling": jnp.clip(jax.random.uniform(arg_keys[6], (VARS, LEVELS, NY, NX), jnp.float32, -1.0, 1.0) * steps_of(arg_keys[6], (VARS, LEVELS, NY, NX), ((0, 2), (1, 8), (2, 32)), -0.4, 0.0), -1.0, 1.0),
    }


def tridiagonal(rhs, coef):
    def forward(carry, item):
        upper_prev, reduced_prev, coef_prev = carry
        rhs_level, coef_level = item
        pivot = 1.0 + coef_prev + coef_level + coef_prev * upper_prev
        upper_now = -coef_level / pivot
        reduced_now = (rhs_level + coef_prev * reduced_prev) / pivot
        return (upper_now, reduced_now, coef_level), (upper_now, reduced_now)

    zero_level = jnp.zeros_like(rhs[0])
    final_state, (upper, reduced) = lax.scan(forward, (zero_level, zero_level, zero_level), (rhs, coef))

    def backward(following, item):
        upper_now, reduced_now = item
        value = reduced_now - upper_now * following
        return value, value

    last_value, solved = lax.scan(backward, zero_level, (upper, reduced), reverse=True)
    return solved


def partner_columns(fold_order):
    swapped = fold_order.reshape(-1, 2)[:, ::-1].reshape(-1)
    return jnp.zeros_like(fold_order).at[fold_order].set(swapped)


def apply_operator(direction, land_free, h_diffusivity, partner):
    masked = land_free * direction
    padded = jnp.pad(masked, ((0, 0), (0, 0), (1, 1), (0, 0)))
    south = padded[:, :, :-2]
    north = padded[:, :, 2:]
    north = north.at[:, :, -1].set(masked[:, :, -1][..., partner])
    east = jnp.roll(masked, -1, 3)
    west = jnp.roll(masked, 1, 3)
    laplace = 4.0 * masked - north - south - east - west
    return direction + h_diffusivity[:, :, None, None] * land_free * laplace


def reference(background, norm_factor, v_diffusivity, h_diffusivity, sea_mask, fold_order, coupling):
    scaled = norm_factor * background
    columns = jnp.stack([tridiagonal(scaled[index], v_diffusivity[index]) for index in range(VARS)])
    land_free = sea_mask.astype(jnp.float32)[None]
    partner = partner_columns(fold_order)
    solution = jnp.zeros_like(columns)
    residual = columns
    direction = columns
    norm_now = jnp.sum(residual * residual, axis=(2, 3))
    for iteration in range(ITERS):
        image = apply_operator(direction, land_free, h_diffusivity, partner)
        step_size = norm_now / jnp.sum(direction * image, axis=(2, 3))
        solution = solution + step_size[:, :, None, None] * direction
        residual = residual - step_size[:, :, None, None] * image
        norm_next = jnp.sum(residual * residual, axis=(2, 3))
        direction = residual + (norm_next / norm_now)[:, :, None, None] * direction
        norm_now = norm_next
    return solution + coupling * solution[::-1]
```

```python
import functools

import jax
import jax.numpy as jnp
from jax import lax
from jax.experimental import pallas as pl
from jax.experimental.pallas import tpu as pltpu
from jax.sharding import PartitionSpec as P

MESH = pl.DeviceIdType.MESH
STEPS = 5
SHIFTS = (0.0, 6.0, 3.0, 7.0, 1.5)
ROWS = 8
PAD = 128
OWN = slice(16, 24)


def starts_of(chains):
    starts, at = [], 0
    for length in chains:
        starts.append(at)
        at += length
    return starts, at


def gram_message(vectors, columns):
    count = len(vectors)
    pairs = [(i, j) for i in range(count) for j in range(i, count)]
    lane = lax.broadcasted_iota(jnp.int32, (8, 128), 1)
    message = jnp.zeros((8, 128), jnp.float32)
    for at in range(0, len(pairs), 22):
        group = pairs[at : at + 22]
        used = sorted({i for pair in group for i in pair})

        def body(block, sums, group=group, used=used):
            held = {i: vectors[i](block) for i in used}
            return tuple(total + held[i] * held[j] for total, (i, j) in zip(sums, group))

        zeros = tuple(jnp.zeros((8, 128), jnp.float32) for _ in group)
        sums = lax.fori_loop(0, columns // 128, body, zeros, unroll=8)
        for total, (i, j) in zip(sums, group):
            here = (lane == count * i + j) | (lane == count * j + i)
            message = jnp.where(here, jnp.sum(total, axis=1, keepdims=True), message)
    return jnp.sum(message, axis=0, keepdims=True)


def coefficient_cg(totals, chains, diffusivity, steps, last):
    starts, count = starts_of(chains)
    shape = (16, 128)
    row = lax.broadcasted_iota(jnp.int32, shape, 0)
    lane = lax.broadcasted_iota(jnp.int32, shape, 1)
    gram = jnp.zeros(shape, jnp.float32)
    for i in range(count):
        line = totals if i == 0 else pltpu.roll(totals, 128 - count * i, 1)
        gram = jnp.where((row == i) & (lane < count), jnp.broadcast_to(line, shape), gram)

    def coefficients(index):
        same = jnp.zeros(shape, jnp.float32)
        step_up = jnp.zeros(shape, jnp.float32)
        for start, length in zip(starts, chains):
            for j in range(length - 1):
                same = jnp.where(index == start + j, 1.0 + diffusivity * SHIFTS[j], same)
                step_up = jnp.where(index == start + j + 1, 4.0 * diffusivity, step_up)
        return same, step_up

    same_row, up_row = coefficients(lane)
    same_col, up_col = coefficients(row)

    def total(value):
        return jnp.sum(jnp.sum(value, axis=0, keepdims=True), axis=1, keepdims=True)

    one, zero = jnp.ones(shape, jnp.float32), jnp.zeros(shape, jnp.float32)
    d_row, d_col = jnp.where(lane == 0, one, zero), jnp.where(row == 0, one, zero)
    first = starts[-1]
    r_row, r_col = jnp.where(lane == first, one, zero), jnp.where(row == first, one, zero)
    x_col = zero
    norm_now = total(r_col * gram * r_row)
    for step in range(steps):
        image_row = same_row * d_row + up_row * pltpu.roll(d_row, 1, 1)
        energy = total(d_col * gram * image_row)
        size = jnp.where(energy > 0, jnp.minimum(norm_now / energy, 1.0), 0.0)
        x_col = x_col + size * d_col
        if last and step == steps - 1:
            break
        image_col = same_col * d_col + up_col * pltpu.roll(d_col, 1, 0)
        r_row = r_row - size * image_row
        r_col = r_col - size * image_col
        norm_next = jnp.maximum(total(r_col * gram * r_row), 0.0)
        ratio = jnp.where(norm_now > 0, norm_next / norm_now, 0.0)
        d_row = r_row + ratio * d_row
        d_col = r_col + ratio * d_col
        norm_now = norm_next
    return x_col, r_col, d_col


def operator(source, target, quarter_mask, columns, shift, rows, loaded, width=512):
    (low, high), (from_row, to_row) = rows, loaded
    inside = slice(low - from_row, high - from_row)
    span = width + 2 * PAD

    def body(chunk, carry):
        at = pl.multiple_of(chunk * width, width)
        wide = source[from_row:to_row, pl.ds(at, span)]
        center = wide[:, PAD : PAD + width]
        middle = wide[inside]
        east = pltpu.roll(middle, span - 1, 1)[:, PAD : PAD + width]
        west = pltpu.roll(middle, 1, 1)[:, PAD : PAD + width]
        north = pltpu.roll(center, to_row - from_row - 1, 0)[inside]
        south = pltpu.roll(center, 1, 0)[inside]
        here = center[inside]
        laplace = 4.0 * here - ((north + south) + (east + west))
        value = quarter_mask[low:high, pl.ds(at, width)] * laplace
        if shift:
            value = value - (0.25 * shift) * here
        target[low:high, pl.ds(at + PAD, width)] = value
        return carry

    lax.fori_loop(0, columns // width, body, 0, unroll=True)
    wrap(target, rows, columns)


def wrap(target, rows, columns):
    low, high = rows
    target[low:high, 0:PAD] = target[low:high, columns : columns + PAD]
    target[low:high, columns + PAD : columns + 2 * PAD] = target[low:high, PAD : 2 * PAD]


def kernel(
    background, norm_factor, v_diffusivity, h_diffusivity, sea_mask, fold_order,
    solved_out, other_out,
    bg, nf, vd, mask_in, fold_in, scaled, rhs, solved, inverse, below, upper,
    field, quarter_mask, v_chain, p_chain, r_chain, masked_p, masked_r, p_own, r_own,
    partner_row, partner_lane, folded, message, received, result, coef,
    load_sem, there_send, there_recv, back_send, back_recv,
    halo_send, halo_recv, mask_send, mask_recv, sum_send, sum_recv, last_send, last_recv, last_local,
):
    tile, lev, var = (lax.axis_index(a) for a in ("tile", "lev", "var"))
    tiles, levels = lax.axis_size("tile"), lax.axis_size("lev")
    columns = bg.shape[1]
    part = columns // levels
    top = tiles - 1
    blocks = columns // 128
    f32 = jnp.float32

    loads = [
        pltpu.make_async_copy(source, target, load_sem.at[i])
        for i, (source, target) in enumerate(
            ((background, bg), (norm_factor, nf), (sea_mask, mask_in), (v_diffusivity, vd), (fold_order, fold_in))
        )
    ]
    for load in loads:
        load.start()
    for buffer in (field, quarter_mask):
        for low in (0, 8, 24, 32):
            buffer[low : low + 8, :] = jnp.zeros((8, columns), f32)
    barrier = pltpu.get_barrier_semaphore()

    def greet_level(d, carry):
        pl.semaphore_signal(barrier, inc=1, device_id={"lev": lax.rem(lev + d, levels)}, device_id_type=MESH)
        return carry

    def greet_tile(d, carry):
        pl.semaphore_signal(barrier, inc=1, device_id={"tile": lax.rem(tile + d, tiles)}, device_id_type=MESH)
        return carry

    lax.fori_loop(1, levels, greet_level, 0)
    lax.fori_loop(1, tiles, greet_tile, 0)
    pl.semaphore_signal(barrier, inc=1, device_id={"var": 1 - var}, device_id_type=MESH)
    loads[0].wait()
    loads[1].wait()
    scaled[...] = nf[...] * bg[...]
    loads[2].wait()
    quarter_mask[OWN, :] = 0.25 * mask_in[...].astype(f32)
    pl.semaphore_wait(barrier, (levels - 1) + (tiles - 1) + 1)

    def send_there(d, carry):
        to = lax.rem(lev + d, levels)
        pltpu.make_async_remote_copy(
            src_ref=scaled.at[:, pl.ds(pl.multiple_of(to * part, part), part)],
            dst_ref=rhs.at[lev],
            send_sem=there_send,
            recv_sem=there_recv,
            device_id={"lev": to},
            device_id_type=MESH,
        ).start()
        return carry

    lax.fori_loop(1, levels, send_there, 0)
    rhs[lev] = scaled[:, pl.ds(pl.multiple_of(lev * part, part), part)]

    sides = ((16, 24, 8, 1), (16, 24, 24, -1), (22, 24, 6, 2), (16, 18, 32, -2))

    def reached(distance):
        return tile + distance <= top if distance > 0 else tile + distance >= 0

    def halo_copies(buffer, send, recv, at, width):
        for side, (low, high, land, distance) in enumerate(sides):

            @pl.when(reached(distance))
            def _(side=side, low=low, high=high, land=land, distance=distance):
                pltpu.make_async_remote_copy(
                    src_ref=buffer.at[low:high, pl.ds(at, width)],
                    dst_ref=buffer.at[land : land + high - low, pl.ds(at, width)],
                    send_sem=send.at[side],
                    recv_sem=recv.at[side],
                    device_id={"tile": tile + distance},
                    device_id_type=MESH,
                ).start()

    def halo_wait(buffer, sem, receive):
        for side, (low, high, land, distance) in enumerate(sides):

            @pl.when(reached(-distance if receive else distance))
            def _(side=side, low=low, high=high, land=land):
                at = slice(land, land + high - low) if receive else slice(low, high)
                pltpu.make_async_copy(buffer.at[at, :], buffer.at[at, :], sem.at[side]).wait()

    halo_copies(quarter_mask, mask_send, mask_recv, 0, columns)

    loads[3].wait()
    above = jnp.zeros((ROWS, part), f32)
    upper_now = above
    for level in range(levels):
        coefficient = vd[level]
        inv = 1.0 / (1.0 + above + coefficient + above * upper_now)
        inverse[level] = inv
        below[level] = above * inv
        upper_now = -coefficient * inv
        upper[level] = upper_now
        above = coefficient

    loads[4].wait()

    @pl.when(tile >= top - 1)
    def _():
        order = fold_in[...]
        lane = lax.broadcasted_iota(jnp.int32, (1, columns), 1)
        mate = jnp.where(lane % 2 == 0, pltpu.roll(order, columns - 1, 1), pltpu.roll(order, 1, 1))
        row_hot = lax.broadcasted_iota(jnp.int32, (blocks, columns), 0) == order // 128
        lane_hot = lax.broadcasted_iota(jnp.int32, (128, columns), 0) == order % 128
        high = jnp.where(row_hot, (mate // 64).astype(f32), 0.0)
        low = jnp.where(row_hot, (mate % 64).astype(f32), 0.0)
        left = jnp.concatenate([high, low], axis=0).astype(jnp.bfloat16)
        right = jnp.where(lane_hot, 1.0, 0.0).astype(jnp.bfloat16)
        found = lax.dot_general(left, right, (((1,), (1,)), ((), ())), preferred_element_type=f32)
        partner = 64 * found[:blocks].astype(jnp.int32) + found[blocks:].astype(jnp.int32)
        partner_row[...] = partner // 128
        partner_lane[...] = partner % 128

    pltpu.make_async_copy(rhs.at[0 : levels - 1], rhs.at[0 : levels - 1], there_recv).wait()
    reduced = jnp.zeros((ROWS, part), f32)
    for level in range(levels):
        reduced = rhs[level] * inverse[level] + below[level] * reduced
        solved[level] = reduced
    value = jnp.zeros((ROWS, part), f32)
    for level in reversed(range(levels)):
        value = solved[level] - upper[level] * value
        solved[level] = value

    my_columns = pl.multiple_of(lev * part, part)

    def send_back(d, carry):
        to = lax.rem(lev + d, levels)
        pltpu.make_async_remote_copy(
            src_ref=solved.at[to],
            dst_ref=field.at[OWN, pl.ds(my_columns, part)],
            send_sem=back_send,
            recv_sem=back_recv.at[d],
            device_id={"lev": to},
            device_id_type=MESH,
        ).start()
        return carry

    lax.fori_loop(1, levels, send_back, 0)
    field[OWN, pl.ds(my_columns, part)] = solved[lev]
    halo_copies(field, halo_send, halo_recv, my_columns, part)

    def pass_on(d, carry):
        at = pl.multiple_of(lax.rem(lev + levels - d, levels) * part, part)
        here = field.at[OWN, pl.ds(at, part)]
        pltpu.make_async_copy(here, here, back_recv.at[d]).wait()
        halo_copies(field, halo_send, halo_recv, at, part)
        return carry

    lax.fori_loop(1, levels, pass_on, 0)

    def fold(buffer, last_row):
        sums = tuple(jnp.zeros((8, 128), f32) for _ in range(blocks // 8))

        def pick(block, sums):
            at = pl.multiple_of(PAD + block * 128, 128)
            line = jnp.broadcast_to(buffer[last_row : last_row + 1, pl.ds(at, 128)], (8, 128))
            chosen = []
            for q, now in enumerate(sums):
                rows = slice(8 * q, 8 * q + 8)
                moved = jnp.take_along_axis(line, partner_lane[rows, :], axis=1)
                chosen.append(jnp.where(partner_row[rows, :] == block, moved, now))
            return tuple(chosen)

        sums = lax.fori_loop(0, blocks, pick, sums, unroll=True)
        for q, now in enumerate(sums):
            folded[8 * q : 8 * q + 8, :] = now
        for block in range(blocks):
            buffer[last_row + 1 : last_row + 2, PAD + block * 128 : PAD + block * 128 + 128] = folded[block : block + 1, :]

    def fold_top(buffer):
        @pl.when(tile == top)
        def _():
            fold(buffer, 23)

    def fold_next(buffer):
        @pl.when(tile == top - 1)
        def _():
            fold(buffer, 31)

    halo_wait(quarter_mask, mask_recv, True)
    halo_wait(field, halo_recv, True)
    masked = masked_p

    def apply_mask(chunk, carry):
        at = pl.multiple_of(chunk * 512, 512)
        masked[:, pl.ds(at + PAD, 512)] = 4.0 * quarter_mask[:, pl.ds(at, 512)] * field[:, pl.ds(at, 512)]
        return carry

    lax.fori_loop(0, columns // 512, apply_mask, 0, unroll=True)
    wrap(masked, (0, 40), columns)
    source = masked
    for j in range(STEPS):
        fold_top(source)
        if j < 2:
            fold_next(source)
        rows, loaded = ((0, 40), (0, 40)) if j == 0 else ((8, 32), (0, 40) if j == 1 else (8, 32))
        operator(source, v_chain[j], quarter_mask, columns, SHIFTS[j], rows, loaded)
        source = v_chain[j]

    def own_of(buffer, pad):
        rows = OWN if buffer.shape[0] == 40 else slice(0, 8)
        return lambda block: buffer[rows, pl.ds(pl.multiple_of(block * 128 + pad, 128), 128)]

    def reduce_over_tiles(index):
        def send(d, carry):
            pltpu.make_async_remote_copy(
                src_ref=message.at[index],
                dst_ref=received.at[index, tile],
                send_sem=sum_send.at[index],
                recv_sem=sum_recv.at[index],
                device_id={"tile": lax.rem(tile + d, tiles)},
                device_id_type=MESH,
            ).start()
            return carry

        lax.fori_loop(1, tiles, send, 0)

    def sum_over_tiles(index):
        others = received.at[index, 0 : tiles - 1]
        pltpu.make_async_copy(others, others, sum_recv.at[index]).wait()
        return jnp.sum(received[index], axis=0)

    shared = gram_message([own_of(field, 0)] + [own_of(v, PAD) for v in v_chain], columns)
    message[0] = shared
    received[0, tile] = shared
    reduce_over_tiles(0)
    diffusivity = h_diffusivity[0, 0]
    x_col, r_col, d_col = coefficient_cg(sum_over_tiles(0), (STEPS + 1,), diffusivity, STEPS, False)
    coef[0:16, :] = x_col
    coef[16:32, :] = r_col
    coef[32:48, :] = d_col

    def next_round(block, carry):
        at = pl.multiple_of(block * 128, 128)
        rows = slice(8, 32)
        held = [field[rows, pl.ds(at, 128)]] + [v[rows, pl.ds(at + PAD, 128)] for v in v_chain]
        residual = sum(coef[16 + j : 17 + j, :] * held[j] for j in range(STEPS + 1))
        direction = sum(coef[32 + j : 33 + j, :] * held[j] for j in range(STEPS + 1))
        mask = 4.0 * quarter_mask[rows, pl.ds(at, 128)]
        masked_r[rows, pl.ds(at + PAD, 128)] = mask * residual
        masked_p[rows, pl.ds(at + PAD, 128)] = mask * direction
        r_own[:, pl.ds(at, 128)] = residual[8:16]
        p_own[:, pl.ds(at, 128)] = direction[8:16]
        return carry

    lax.fori_loop(0, blocks, next_round, 0, unroll=8)
    wrap(masked_r, (8, 32), columns)
    wrap(masked_p, (8, 32), columns)

    for first, chain, length in ((masked_p, p_chain, STEPS), (masked_r, r_chain, STEPS - 1)):
        source = first
        for j in range(length):
            fold_top(source)
            rows = (16, 24) if j == length - 1 else (8, 32)
            operator(source, chain[j], quarter_mask, columns, SHIFTS[j], rows, (8, 32))
            source = chain[j]
    shared = gram_message(
        [own_of(p_own, 0)] + [own_of(p, PAD) for p in p_chain] + [own_of(r_own, 0)] + [own_of(r, PAD) for r in r_chain],
        columns,
    )
    message[1] = shared
    received[1, tile] = shared
    reduce_over_tiles(1)

    def part_one(block, carry):
        at = pl.multiple_of(block * 128, 128)
        held = [field[OWN, pl.ds(at, 128)]] + [v[OWN, pl.ds(at + PAD, 128)] for v in v_chain[: STEPS - 1]]
        result[:, pl.ds(at, 128)] = sum(coef[j : j + 1, :] * held[j] for j in range(STEPS))
        return carry

    lax.fori_loop(0, blocks, part_one, 0, unroll=8)
    x_col, r_col, d_col = coefficient_cg(sum_over_tiles(1), (STEPS + 1, STEPS), diffusivity, STEPS, True)
    coef[0:16, :] = x_col

    pieces = 4
    per_piece = blocks // pieces

    def finish(piece, carry):
        def part_two(block, carry):
            at = pl.multiple_of((piece * per_piece + block) * 128, 128)
            held = [p_own[:, pl.ds(at, 128)]] + [p[OWN, pl.ds(at + PAD, 128)] for p in p_chain[: STEPS - 1]]
            value = sum(coef[j : j + 1, :] * held[j] for j in range(STEPS))
            held = [r_own[:, pl.ds(at, 128)]] + [r[OWN, pl.ds(at + PAD, 128)] for r in r_chain[: STEPS - 2]]
            value += sum(coef[STEPS + 1 + j : STEPS + 2 + j, :] * held[j] for j in range(STEPS - 1))
            result[:, pl.ds(at, 128)] += value
            return carry

        lax.fori_loop(0, per_piece, part_two, 0, unroll=True)
        here = pl.ds(pl.multiple_of(piece * per_piece * 128, 128), per_piece * 128)
        pltpu.make_async_remote_copy(
            src_ref=result.at[:, here],
            dst_ref=other_out.at[:, here],
            send_sem=last_send,
            recv_sem=last_recv,
            device_id={"var": 1 - var},
            device_id_type=MESH,
        ).start()
        return carry

    lax.fori_loop(0, pieces, finish, 0)
    keep = pltpu.make_async_copy(result, solved_out, last_local)
    keep.start()

    def sent(buffer, sem):
        pltpu.make_async_copy(buffer, buffer, sem).wait()

    sent(rhs.at[0 : levels - 1], there_send)
    sent(rhs.at[0 : levels - 1], back_send)
    halo_wait(quarter_mask, mask_send, False)
    halo_wait(field, halo_send, False)
    for index in range(2):
        sent(received.at[index, 0 : tiles - 1], sum_send.at[index])
    keep.wait()
    sent(result, last_send)
    pltpu.make_async_copy(other_out, other_out, last_recv).wait()


def per_device(
    background, norm_factor, v_diffusivity, h_diffusivity, sea_mask, fold_order, coupling
):
    rows, columns = background.shape[2:]
    levels, tiles = lax.axis_size("lev"), lax.axis_size("tile")
    part = columns // levels
    f32 = jnp.float32
    strip = jax.ShapeDtypeStruct((rows, columns), f32)
    vmem = pltpu.VMEM
    tall = vmem((40, columns), f32)
    padded = vmem((40, columns + 2 * PAD), f32)
    blocks = columns // 128
    dma = pltpu.SemaphoreType.DMA
    solved, other = pl.pallas_call(
        kernel,
        out_shape=(strip, strip),
        in_specs=[pl.BlockSpec(memory_space=pl.ANY)] * 3
        + [pl.BlockSpec(memory_space=pltpu.SMEM)]
        + [pl.BlockSpec(memory_space=pl.ANY)] * 2,
        out_specs=(pl.BlockSpec(memory_space=pl.ANY),) * 2,
        scratch_shapes=[
            vmem((rows, columns), f32),
            vmem((rows, columns), f32),
            vmem((levels, rows, part), f32),
            vmem((rows, columns), jnp.int32),
            vmem((1, columns), jnp.int32),
            vmem((rows, columns), f32),
            vmem((levels, rows, part), f32),
            vmem((levels, rows, part), f32),
            vmem((levels, rows, part), f32),
            vmem((levels, rows, part), f32),
            vmem((levels, rows, part), f32),
            tall,
            tall,
            [padded] * STEPS,
            [padded] * STEPS,
            [padded] * (STEPS - 1),
            padded,
            padded,
            vmem((rows, columns), f32),
            vmem((rows, columns), f32),
            vmem((blocks, 128), jnp.int32),
            vmem((blocks, 128), jnp.int32),
            vmem((blocks, 128), f32),
            vmem((2, 1, 128), f32),
            vmem((2, tiles, 1, 128), f32),
            vmem((rows, columns), f32),
            vmem((48, 128), f32),
            dma((5,)),
            dma,
            dma,
            dma,
            dma((levels,)),
            dma((4,)),
            dma((4,)),
            dma((4,)),
            dma((4,)),
            dma((2,)),
            dma((2,)),
            dma,
            dma,
            dma,
        ],
        compiler_params=pltpu.CompilerParams(
            collective_id=0, has_side_effects=True, vmem_limit_bytes=40 * 2**20
        ),
    )(
        background.reshape(rows, columns),
        norm_factor.reshape(rows, columns),
        v_diffusivity.reshape(levels, rows, part),
        h_diffusivity,
        sea_mask.reshape(rows, columns),
        fold_order.reshape(1, columns),
    )
    return (solved + coupling[0, 0] * other)[None, None]


def solution(mesh):
    placed = (
        P("var", "lev", "tile", None),
        P("var", "lev", "tile", None),
        P("var", None, "tile", "lev"),
        P("var", "lev"),
        P("lev", "tile", None),
        P(),
        P("var", "lev", "tile", None),
    )
    return jax.shard_map(
        per_device,
        mesh=mesh,
        in_specs=placed,
        out_specs=P("var", "lev", "tile", None),
        check_vma=False,
    )
```

```python
import functools

import jax
import jax.numpy as jnp
from jax import lax
from jax.experimental import pallas as pl
from jax.experimental.pallas import tpu as pltpu
from jax.sharding import PartitionSpec as P

MESH = pl.DeviceIdType.MESH
STEPS = 5
SHIFTS = (0.0, 5.0, 2.0, 7.0, 0.5)
ROWS = 8
PAD = 128
OWN = slice(16, 24)


def starts_of(chains):
    starts, at = [], 0
    for length in chains:
        starts.append(at)
        at += length
    return starts, at


def gram_message(vectors, columns):
    count = len(vectors)
    pairs = [(i, j) for i in range(count) for j in range(i, count)]
    lane = lax.broadcasted_iota(jnp.int32, (8, 128), 1)
    message = jnp.zeros((8, 128), jnp.float32)
    for at in range(0, len(pairs), 22):
        group = pairs[at : at + 22]
        used = sorted({i for pair in group for i in pair})

        def body(block, sums, group=group, used=used):
            held = {i: vectors[i](block) for i in used}
            return tuple(total + held[i] * held[j] for total, (i, j) in zip(sums, group))

        zeros = tuple(jnp.zeros((8, 128), jnp.float32) for _ in group)
        sums = lax.fori_loop(0, columns // 128, body, zeros, unroll=8)
        for total, (i, j) in zip(sums, group):
            here = (lane == count * i + j) | (lane == count * j + i)
            message = jnp.where(here, jnp.sum(total, axis=1, keepdims=True), message)
    return jnp.sum(message, axis=0, keepdims=True)


def coefficient_cg(totals, chains, diffusivity, steps, last):
    starts, count = starts_of(chains)
    shape = (16, 128)
    row = lax.broadcasted_iota(jnp.int32, shape, 0)
    lane = lax.broadcasted_iota(jnp.int32, shape, 1)
    gram = jnp.zeros(shape, jnp.float32)
    for i in range(count):
        line = totals if i == 0 else pltpu.roll(totals, 128 - count * i, 1)
        gram = jnp.where((row == i) & (lane < count), jnp.broadcast_to(line, shape), gram)

    def coefficients(index):
        same = jnp.zeros(shape, jnp.float32)
        step_up = jnp.zeros(shape, jnp.float32)
        for start, length in zip(starts, chains):
            for j in range(length - 1):
                same = jnp.where(index == start + j, 1.0 + diffusivity * SHIFTS[j], same)
                step_up = jnp.where(index == start + j + 1, 4.0 * diffusivity, step_up)
        return same, step_up

    same_row, up_row = coefficients(lane)
    same_col, up_col = coefficients(row)

    def total(value):
        return jnp.sum(jnp.sum(value, axis=0, keepdims=True), axis=1, keepdims=True)

    one, zero = jnp.ones(shape, jnp.float32), jnp.zeros(shape, jnp.float32)
    d_row, d_col = jnp.where(lane == 0, one, zero), jnp.where(row == 0, one, zero)
    first = starts[-1]
    r_row, r_col = jnp.where(lane == first, one, zero), jnp.where(row == first, one, zero)
    x_col = zero
    norm_now = total(r_col * gram * r_row)
    for step in range(steps):
        image_row = same_row * d_row + up_row * pltpu.roll(d_row, 1, 1)
        energy = total(d_col * gram * image_row)
        size = jnp.where(energy > 0, jnp.minimum(norm_now / energy, 1.0), 0.0)
        x_col = x_col + size * d_col
        if last and step == steps - 1:
            break
        image_col = same_col * d_col + up_col * pltpu.roll(d_col, 1, 0)
        r_row = r_row - size * image_row
        r_col = r_col - size * image_col
        norm_next = jnp.maximum(total(r_col * gram * r_row), 0.0)
        ratio = jnp.where(norm_now > 0, norm_next / norm_now, 0.0)
        d_row = r_row + ratio * d_row
        d_col = r_col + ratio * d_col
        norm_now = norm_next
    return x_col, r_col, d_col


def operator(source, target, quarter_mask, columns, shift, rows, loaded, width=512):
    (low, high), (from_row, to_row) = rows, loaded
    inside = slice(low - from_row, high - from_row)
    span = width + 2 * PAD

    def body(chunk, carry):
        at = pl.multiple_of(chunk * width, width)
        wide = source[from_row:to_row, pl.ds(at, span)]
        center = wide[:, PAD : PAD + width]
        middle = wide[inside]
        east = pltpu.roll(middle, span - 1, 1)[:, PAD : PAD + width]
        west = pltpu.roll(middle, 1, 1)[:, PAD : PAD + width]
        north = pltpu.roll(center, to_row - from_row - 1, 0)[inside]
        south = pltpu.roll(center, 1, 0)[inside]
        here = center[inside]
        laplace = 4.0 * here - ((north + south) + (east + west))
        value = quarter_mask[low:high, pl.ds(at, width)] * laplace
        if shift:
            value = value - (0.25 * shift) * here
        target[low:high, pl.ds(at + PAD, width)] = value
        return carry

    lax.fori_loop(0, columns // width, body, 0, unroll=True)
    wrap(target, rows, columns)


def wrap(target, rows, columns):
    low, high = rows
    target[low:high, 0:PAD] = target[low:high, columns : columns + PAD]
    target[low:high, columns + PAD : columns + 2 * PAD] = target[low:high, PAD : 2 * PAD]


def kernel(
    background, norm_factor, v_diffusivity, h_diffusivity, sea_mask, fold_order,
    solved_out, other_out,
    bg, nf, vd, mask_in, fold_in, scaled, rhs, solved, inverse, below, upper,
    field, quarter_mask, v_chain, p_chain, r_chain, masked_p, masked_r, p_own, r_own,
    partner_row, partner_lane, folded, message, received, result, coef,
    load_sem, there_send, there_recv, back_send, back_recv,
    halo_send, halo_recv, mask_send, mask_recv, sum_send, sum_recv, last_send, last_recv, last_local,
):
    tile, lev, var = (lax.axis_index(a) for a in ("tile", "lev", "var"))
    tiles, levels = lax.axis_size("tile"), lax.axis_size("lev")
    columns = bg.shape[1]
    part = columns // levels
    top = tiles - 1
    blocks = columns // 128
    f32 = jnp.float32

    loads = [
        pltpu.make_async_copy(source, target, load_sem.at[i])
        for i, (source, target) in enumerate(
            ((background, bg), (norm_factor, nf), (sea_mask, mask_in), (v_diffusivity, vd), (fold_order, fold_in))
        )
    ]
    for load in loads:
        load.start()
    for buffer in (field, quarter_mask):
        for low in (0, 8, 24, 32):
            buffer[low : low + 8, :] = jnp.zeros((8, columns), f32)
    barrier = pltpu.get_barrier_semaphore()

    def greet_level(d, carry):
        pl.semaphore_signal(barrier, inc=1, device_id={"lev": lax.rem(lev + d, levels)}, device_id_type=MESH)
        return carry

    def greet_tile(d, carry):
        pl.semaphore_signal(barrier, inc=1, device_id={"tile": lax.rem(tile + d, tiles)}, device_id_type=MESH)
        return carry

    lax.fori_loop(1, levels, greet_level, 0, unroll=True)
    lax.fori_loop(1, tiles, greet_tile, 0, unroll=True)
    pl.semaphore_signal(barrier, inc=1, device_id={"var": 1 - var}, device_id_type=MESH)
    loads[0].wait()
    loads[1].wait()
    scaled[...] = nf[...] * bg[...]
    loads[2].wait()
    quarter_mask[OWN, :] = 0.25 * mask_in[...].astype(f32)
    pl.semaphore_wait(barrier, (levels - 1) + (tiles - 1) + 1)

    def send_there(d, carry):
        to = lax.rem(lev + d, levels)
        pltpu.make_async_remote_copy(
            src_ref=scaled.at[:, pl.ds(pl.multiple_of(to * part, part), part)],
            dst_ref=rhs.at[lev],
            send_sem=there_send,
            recv_sem=there_recv,
            device_id={"lev": to},
            device_id_type=MESH,
        ).start()
        return carry

    lax.fori_loop(1, levels, send_there, 0, unroll=True)
    rhs[lev] = scaled[:, pl.ds(pl.multiple_of(lev * part, part), part)]

    sides = ((16, 24, 8, 1), (16, 24, 24, -1), (22, 24, 6, 2), (16, 18, 32, -2))

    def reached(distance):
        return tile + distance <= top if distance > 0 else tile + distance >= 0

    def halo_copies(buffer, send, recv, at, width):
        for side, (low, high, land, distance) in enumerate(sides):

            @pl.when(reached(distance))
            def _(side=side, low=low, high=high, land=land, distance=distance):
                pltpu.make_async_remote_copy(
                    src_ref=buffer.at[low:high, pl.ds(at, width)],
                    dst_ref=buffer.at[land : land + high - low, pl.ds(at, width)],
                    send_sem=send.at[side],
                    recv_sem=recv.at[side],
                    device_id={"tile": tile + distance},
                    device_id_type=MESH,
                ).start()

    def halo_wait(buffer, sem, receive):
        for side, (low, high, land, distance) in enumerate(sides):

            @pl.when(reached(-distance if receive else distance))
            def _(side=side, low=low, high=high, land=land):
                at = slice(land, land + high - low) if receive else slice(low, high)
                pltpu.make_async_copy(buffer.at[at, :], buffer.at[at, :], sem.at[side]).wait()

    halo_copies(quarter_mask, mask_send, mask_recv, 0, columns)

    loads[3].wait()
    above = jnp.zeros((ROWS, part), f32)
    upper_now = above
    for level in range(levels):
        coefficient = vd[level]
        inv = 1.0 / (1.0 + above + coefficient + above * upper_now)
        inverse[level] = inv
        below[level] = above * inv
        upper_now = -coefficient * inv
        upper[level] = upper_now
        above = coefficient

    loads[4].wait()

    @pl.when(tile >= top - 1)
    def _():
        order = fold_in[...]
        lane = lax.broadcasted_iota(jnp.int32, (1, columns), 1)
        mate = jnp.where(lane % 2 == 0, pltpu.roll(order, columns - 1, 1), pltpu.roll(order, 1, 1))
        row_hot = lax.broadcasted_iota(jnp.int32, (blocks, columns), 0) == order // 128
        lane_hot = lax.broadcasted_iota(jnp.int32, (128, columns), 0) == order % 128
        high = jnp.where(row_hot, (mate // 64).astype(f32), 0.0)
        low = jnp.where(row_hot, (mate % 64).astype(f32), 0.0)
        left = jnp.concatenate([high, low], axis=0).astype(jnp.bfloat16)
        right = jnp.where(lane_hot, 1.0, 0.0).astype(jnp.bfloat16)
        found = lax.dot_general(left, right, (((1,), (1,)), ((), ())), preferred_element_type=f32)
        partner = 64 * found[:blocks].astype(jnp.int32) + found[blocks:].astype(jnp.int32)
        partner_row[...] = partner // 128
        partner_lane[...] = partner % 128

    pltpu.make_async_copy(rhs.at[0 : levels - 1], rhs.at[0 : levels - 1], there_recv).wait()
    reduced = jnp.zeros((ROWS, part), f32)
    for level in range(levels):
        reduced = rhs[level] * inverse[level] + below[level] * reduced
        solved[level] = reduced
    value = jnp.zeros((ROWS, part), f32)
    for level in reversed(range(levels)):
        value = solved[level] - upper[level] * value
        solved[level] = value

    my_columns = pl.multiple_of(lev * part, part)

    def send_back(d, carry):
        to = lax.rem(lev + d, levels)
        pltpu.make_async_remote_copy(
            src_ref=solved.at[to],
            dst_ref=field.at[OWN, pl.ds(my_columns, part)],
            send_sem=back_send,
            recv_sem=back_recv.at[d],
            device_id={"lev": to},
            device_id_type=MESH,
        ).start()
        return carry

    lax.fori_loop(1, levels, send_back, 0, unroll=True)
    field[OWN, pl.ds(my_columns, part)] = solved[lev]
    halo_copies(field, halo_send, halo_recv, my_columns, part)

    def pass_on(d, carry):
        at = pl.multiple_of(lax.rem(lev + levels - d, levels) * part, part)
        here = field.at[OWN, pl.ds(at, part)]
        pltpu.make_async_copy(here, here, back_recv.at[d]).wait()
        halo_copies(field, halo_send, halo_recv, at, part)
        return carry

    lax.fori_loop(1, levels, pass_on, 0)

    def fold(buffer, last_row):
        sums = tuple(jnp.zeros((8, 128), f32) for _ in range(blocks // 8))

        def pick(block, sums):
            at = pl.multiple_of(PAD + block * 128, 128)
            line = jnp.broadcast_to(buffer[last_row : last_row + 1, pl.ds(at, 128)], (8, 128))
            chosen = []
            for q, now in enumerate(sums):
                rows = slice(8 * q, 8 * q + 8)
                moved = jnp.take_along_axis(line, partner_lane[rows, :], axis=1)
                chosen.append(jnp.where(partner_row[rows, :] == block, moved, now))
            return tuple(chosen)

        sums = lax.fori_loop(0, blocks, pick, sums, unroll=True)
        for q, now in enumerate(sums):
            folded[8 * q : 8 * q + 8, :] = now
        for block in range(blocks):
            buffer[last_row + 1 : last_row + 2, PAD + block * 128 : PAD + block * 128 + 128] = folded[block : block + 1, :]

    def fold_top(buffer):
        @pl.when(tile == top)
        def _():
            fold(buffer, 23)

    def fold_next(buffer):
        @pl.when(tile == top - 1)
        def _():
            fold(buffer, 31)

    halo_wait(quarter_mask, mask_recv, True)
    halo_wait(field, halo_recv, True)
    masked = masked_p

    def apply_mask(chunk, carry):
        at = pl.multiple_of(chunk * 512, 512)
        masked[:, pl.ds(at + PAD, 512)] = 4.0 * quarter_mask[:, pl.ds(at, 512)] * field[:, pl.ds(at, 512)]
        return carry

    lax.fori_loop(0, columns // 512, apply_mask, 0, unroll=True)
    wrap(masked, (0, 40), columns)
    source = masked
    for j in range(STEPS):
        fold_top(source)
        if j < 2:
            fold_next(source)
        rows, loaded = ((0, 40), (0, 40)) if j == 0 else ((8, 32), (0, 40) if j == 1 else (8, 32))
        operator(source, v_chain[j], quarter_mask, columns, SHIFTS[j], rows, loaded)
        source = v_chain[j]

    def own_of(buffer, pad):
        rows = OWN if buffer.shape[0] == 40 else slice(0, 8)
        return lambda block: buffer[rows, pl.ds(pl.multiple_of(block * 128 + pad, 128), 128)]

    def reduce_over_tiles(index):
        def send(d, carry):
            pltpu.make_async_remote_copy(
                src_ref=message.at[index],
                dst_ref=received.at[index, tile],
                send_sem=sum_send.at[index],
                recv_sem=sum_recv.at[index],
                device_id={"tile": lax.rem(tile + d, tiles)},
                device_id_type=MESH,
            ).start()
            return carry

        lax.fori_loop(1, tiles, send, 0, unroll=True)

    def sum_over_tiles(index):
        others = received.at[index, 0 : tiles - 1]
        pltpu.make_async_copy(others, others, sum_recv.at[index]).wait()
        return jnp.sum(received[index], axis=0)

    shared = gram_message([own_of(field, 0)] + [own_of(v, PAD) for v in v_chain], columns)
    message[0] = shared
    received[0, tile] = shared
    reduce_over_tiles(0)
    diffusivity = h_diffusivity[0, 0]
    x_col, r_col, d_col = coefficient_cg(sum_over_tiles(0), (STEPS + 1,), diffusivity, STEPS, False)
    coef[0:16, :] = x_col
    coef[16:32, :] = r_col
    coef[32:48, :] = d_col

    def next_round(block, carry):
        at = pl.multiple_of(block * 128, 128)
        rows = slice(8, 32)
        held = [field[rows, pl.ds(at, 128)]] + [v[rows, pl.ds(at + PAD, 128)] for v in v_chain]
        residual = sum(coef[16 + j : 17 + j, :] * held[j] for j in range(STEPS + 1))
        direction = sum(coef[32 + j : 33 + j, :] * held[j] for j in range(STEPS + 1))
        mask = 4.0 * quarter_mask[rows, pl.ds(at, 128)]
        masked_r[rows, pl.ds(at + PAD, 128)] = mask * residual
        masked_p[rows, pl.ds(at + PAD, 128)] = mask * direction
        r_own[:, pl.ds(at, 128)] = residual[8:16]
        p_own[:, pl.ds(at, 128)] = direction[8:16]
        return carry

    lax.fori_loop(0, blocks, next_round, 0, unroll=8)
    wrap(masked_r, (8, 32), columns)
    wrap(masked_p, (8, 32), columns)

    for first, chain, length in ((masked_p, p_chain, STEPS), (masked_r, r_chain, STEPS - 1)):
        source = first
        for j in range(length):
            fold_top(source)
            rows = (16, 24) if j == length - 1 else (8, 32)
            operator(source, chain[j], quarter_mask, columns, SHIFTS[j], rows, (8, 32))
            source = chain[j]
    shared = gram_message(
        [own_of(p_own, 0)] + [own_of(p, PAD) for p in p_chain] + [own_of(r_own, 0)] + [own_of(r, PAD) for r in r_chain],
        columns,
    )
    message[1] = shared
    received[1, tile] = shared
    reduce_over_tiles(1)

    def part_one(block, carry):
        at = pl.multiple_of(block * 128, 128)
        held = [field[OWN, pl.ds(at, 128)]] + [v[OWN, pl.ds(at + PAD, 128)] for v in v_chain[: STEPS - 1]]
        result[:, pl.ds(at, 128)] = sum(coef[j : j + 1, :] * held[j] for j in range(STEPS))
        return carry

    lax.fori_loop(0, blocks, part_one, 0, unroll=8)
    x_col, r_col, d_col = coefficient_cg(sum_over_tiles(1), (STEPS + 1, STEPS), diffusivity, STEPS, True)
    coef[0:16, :] = x_col

    pieces = 4
    per_piece = blocks // pieces

    def finish(piece, carry):
        def part_two(block, carry):
            at = pl.multiple_of((piece * per_piece + block) * 128, 128)
            held = [p_own[:, pl.ds(at, 128)]] + [p[OWN, pl.ds(at + PAD, 128)] for p in p_chain[: STEPS - 1]]
            value = sum(coef[j : j + 1, :] * held[j] for j in range(STEPS))
            held = [r_own[:, pl.ds(at, 128)]] + [r[OWN, pl.ds(at + PAD, 128)] for r in r_chain[: STEPS - 2]]
            value += sum(coef[STEPS + 1 + j : STEPS + 2 + j, :] * held[j] for j in range(STEPS - 1))
            result[:, pl.ds(at, 128)] += value
            return carry

        lax.fori_loop(0, per_piece, part_two, 0, unroll=True)
        here = pl.ds(pl.multiple_of(piece * per_piece * 128, 128), per_piece * 128)
        pltpu.make_async_remote_copy(
            src_ref=result.at[:, here],
            dst_ref=other_out.at[:, here],
            send_sem=last_send,
            recv_sem=last_recv,
            device_id={"var": 1 - var},
            device_id_type=MESH,
        ).start()
        return carry

    lax.fori_loop(0, pieces, finish, 0)
    keep = pltpu.make_async_copy(result, solved_out, last_local)
    keep.start()

    def sent(buffer, sem):
        pltpu.make_async_copy(buffer, buffer, sem).wait()

    sent(rhs.at[0 : levels - 1], there_send)
    sent(rhs.at[0 : levels - 1], back_send)
    halo_wait(quarter_mask, mask_send, False)
    halo_wait(field, halo_send, False)
    for index in range(2):
        sent(received.at[index, 0 : tiles - 1], sum_send.at[index])
    keep.wait()
    sent(result, last_send)
    pltpu.make_async_copy(other_out, other_out, last_recv).wait()


def per_device(
    background, norm_factor, v_diffusivity, h_diffusivity, sea_mask, fold_order, coupling
):
    rows, columns = background.shape[2:]
    levels, tiles = lax.axis_size("lev"), lax.axis_size("tile")
    part = columns // levels
    f32 = jnp.float32
    strip = jax.ShapeDtypeStruct((rows, columns), f32)
    vmem = pltpu.VMEM
    tall = vmem((40, columns), f32)
    padded = vmem((40, columns + 2 * PAD), f32)
    blocks = columns // 128
    dma = pltpu.SemaphoreType.DMA
    in_hbm = functools.partial(pltpu.with_memory_space_constraint, memory_space=pltpu.HBM)
    solved, other = pl.pallas_call(
        kernel,
        out_shape=(strip, strip),
        in_specs=[pl.BlockSpec(memory_space=pl.ANY)] * 3
        + [pl.BlockSpec(memory_space=pltpu.SMEM)]
        + [pl.BlockSpec(memory_space=pl.ANY)] * 2,
        out_specs=(pl.BlockSpec(memory_space=pl.ANY),) * 2,
        scratch_shapes=[
            vmem((rows, columns), f32),
            vmem((rows, columns), f32),
            vmem((levels, rows, part), f32),
            vmem((rows, columns), jnp.int32),
            vmem((1, columns), jnp.int32),
            vmem((rows, columns), f32),
            vmem((levels, rows, part), f32),
            vmem((levels, rows, part), f32),
            vmem((levels, rows, part), f32),
            vmem((levels, rows, part), f32),
            vmem((levels, rows, part), f32),
            tall,
            tall,
            [padded] * STEPS,
            [padded] * STEPS,
            [padded] * (STEPS - 1),
            padded,
            padded,
            vmem((rows, columns), f32),
            vmem((rows, columns), f32),
            vmem((blocks, 128), jnp.int32),
            vmem((blocks, 128), jnp.int32),
            vmem((blocks, 128), f32),
            vmem((2, 1, 128), f32),
            vmem((2, tiles, 1, 128), f32),
            vmem((rows, columns), f32),
            vmem((48, 128), f32),
            dma((5,)),
            dma,
            dma,
            dma,
            dma((levels,)),
            dma((4,)),
            dma((4,)),
            dma((4,)),
            dma((4,)),
            dma((2,)),
            dma((2,)),
            dma,
            dma,
            dma,
        ],
        compiler_params=pltpu.CompilerParams(
            collective_id=0, has_side_effects=True, vmem_limit_bytes=40 * 2**20
        ),
    )(
        in_hbm(background.reshape(rows, columns)),
        in_hbm(norm_factor.reshape(rows, columns)),
        in_hbm(v_diffusivity.reshape(levels, rows, part)),
        h_diffusivity,
        in_hbm(sea_mask.reshape(rows, columns)),
        in_hbm(fold_order.reshape(1, columns)),
    )
    return (solved + coupling[0, 0] * other)[None, None]


def solution(mesh):
    placed = (
        P("var", "lev", "tile", None),
        P("var", "lev", "tile", None),
        P("var", None, "tile", "lev"),
        P("var", "lev"),
        P("lev", "tile", None),
        P(),
        P("var", "lev", "tile", None),
    )
    return jax.shard_map(
        per_device,
        mesh=mesh,
        in_specs=placed,
        out_specs=P("var", "lev", "tile", None),
        check_vma=False,
    )
```

```python
import functools

import jax
import jax.numpy as jnp
from jax import lax
from jax.experimental import pallas as pl
from jax.experimental.pallas import tpu as pltpu
from jax.sharding import PartitionSpec as P

MESH = pl.DeviceIdType.MESH
STEPS = 5
SHIFTS = (0.0, 5.0, 2.0, 7.0, 0.5)
ROWS = 8
PAD = 128
OWN = slice(16, 24)


def starts_of(chains):
    starts, at = [], 0
    for length in chains:
        starts.append(at)
        at += length
    return starts, at


def gram_message(vectors, columns):
    count = len(vectors)
    pairs = [(i, j) for i in range(count) for j in range(i, count)]
    lane = lax.broadcasted_iota(jnp.int32, (8, 128), 1)
    message = jnp.zeros((8, 128), jnp.float32)
    for at in range(0, len(pairs), 22):
        group = pairs[at : at + 22]
        used = sorted({i for pair in group for i in pair})

        def body(block, sums, group=group, used=used):
            held = {i: vectors[i](block) for i in used}
            return tuple(total + held[i] * held[j] for total, (i, j) in zip(sums, group))

        zeros = tuple(jnp.zeros((8, 128), jnp.float32) for _ in group)
        sums = lax.fori_loop(0, columns // 128, body, zeros, unroll=8)
        for total, (i, j) in zip(sums, group):
            here = (lane == count * i + j) | (lane == count * j + i)
            message = jnp.where(here, jnp.sum(total, axis=1, keepdims=True), message)
    return jnp.sum(message, axis=0, keepdims=True)


def coefficient_cg(totals, chains, diffusivity, steps, last):
    starts, count = starts_of(chains)
    shape = (16, 128)
    row = lax.broadcasted_iota(jnp.int32, shape, 0)
    lane = lax.broadcasted_iota(jnp.int32, shape, 1)
    gram = jnp.zeros(shape, jnp.float32)
    for i in range(count):
        line = totals if i == 0 else pltpu.roll(totals, 128 - count * i, 1)
        gram = jnp.where((row == i) & (lane < count), jnp.broadcast_to(line, shape), gram)

    def coefficients(index):
        same = jnp.zeros(shape, jnp.float32)
        step_up = jnp.zeros(shape, jnp.float32)
        for start, length in zip(starts, chains):
            for j in range(length - 1):
                same = jnp.where(index == start + j, 1.0 + diffusivity * SHIFTS[j], same)
                step_up = jnp.where(index == start + j + 1, 4.0 * diffusivity, step_up)
        return same, step_up

    same_row, up_row = coefficients(lane)
    same_col, up_col = coefficients(row)

    def total(value):
        return jnp.sum(jnp.sum(value, axis=0, keepdims=True), axis=1, keepdims=True)

    one, zero = jnp.ones(shape, jnp.float32), jnp.zeros(shape, jnp.float32)
    d_row, d_col = jnp.where(lane == 0, one, zero), jnp.where(row == 0, one, zero)
    first = starts[-1]
    r_row, r_col = jnp.where(lane == first, one, zero), jnp.where(row == first, one, zero)
    x_col = zero
    norm_now = total(r_col * gram * r_row)
    for step in range(steps):
        image_row = same_row * d_row + up_row * pltpu.roll(d_row, 1, 1)
        energy = total(d_col * gram * image_row)
        size = jnp.where(energy > 0, jnp.minimum(norm_now / energy, 1.0), 0.0)
        x_col = x_col + size * d_col
        if last and step == steps - 1:
            break
        image_col = same_col * d_col + up_col * pltpu.roll(d_col, 1, 0)
        r_row = r_row - size * image_row
        r_col = r_col - size * image_col
        norm_next = jnp.maximum(total(r_col * gram * r_row), 0.0)
        ratio = jnp.where(norm_now > 0, norm_next / norm_now, 0.0)
        d_row = r_row + ratio * d_row
        d_col = r_col + ratio * d_col
        norm_now = norm_next
    return x_col, r_col, d_col


def operator(source, target, quarter_mask, columns, shift, rows, loaded, width=512):
    (low, high), (from_row, to_row) = rows, loaded
    inside = slice(low - from_row, high - from_row)
    span = width + 2 * PAD

    def body(chunk, carry):
        at = pl.multiple_of(chunk * width, width)
        wide = source[from_row:to_row, pl.ds(at, span)]
        center = wide[:, PAD : PAD + width]
        middle = wide[inside]
        east = pltpu.roll(middle, span - 1, 1)[:, PAD : PAD + width]
        west = pltpu.roll(middle, 1, 1)[:, PAD : PAD + width]
        north = pltpu.roll(center, to_row - from_row - 1, 0)[inside]
        south = pltpu.roll(center, 1, 0)[inside]
        here = center[inside]
        laplace = 4.0 * here - ((north + south) + (east + west))
        value = quarter_mask[low:high, pl.ds(at, width)] * laplace
        if shift:
            value = value - (0.25 * shift) * here
        target[low:high, pl.ds(at + PAD, width)] = value
        return carry

    lax.fori_loop(0, columns // width, body, 0, unroll=True)
    wrap(target, rows, columns)


def wrap(target, rows, columns):
    low, high = rows
    target[low:high, 0:PAD] = target[low:high, columns : columns + PAD]
    target[low:high, columns + PAD : columns + 2 * PAD] = target[low:high, PAD : 2 * PAD]


def kernel(
    background, norm_factor, v_diffusivity, h_diffusivity, sea_mask, fold_order,
    solved_out, other_out,
    bg, nf, vd, mask_in, fold_in, scaled, rhs, solved, inverse, below, upper,
    field, quarter_mask, v_chain, p_chain, r_chain, masked_p, masked_r, p_own, r_own,
    partner_row, partner_lane, folded, message, received, result, halfway, coef,
    load_sem, there_send, there_recv, back_send, back_recv,
    halo_send, halo_recv, mask_send, mask_recv, sum_send, sum_recv, last_send, half_recv, last_recv, last_local,
):
    tile, lev, var = (lax.axis_index(a) for a in ("tile", "lev", "var"))
    tiles, levels = lax.axis_size("tile"), lax.axis_size("lev")
    columns = bg.shape[1]
    part = columns // levels
    top = tiles - 1
    blocks = columns // 128
    f32 = jnp.float32

    loads = [
        pltpu.make_async_copy(source, target, load_sem.at[i])
        for i, (source, target) in enumerate(
            ((background, bg), (norm_factor, nf), (sea_mask, mask_in), (v_diffusivity, vd), (fold_order, fold_in))
        )
    ]
    for load in loads:
        load.start()
    barrier = pltpu.get_barrier_semaphore()
    bits = (lax.rem(lev, 2), lax.rem(lev // 2, 2), lev // 4)

    def peer_level(d):
        return sum(
            (1 - bit if d >> place & 1 else bit) * (1 << place) for place, bit in enumerate(bits)
        )

    peers = [peer_level(d) for d in range(levels)]
    chip = 4 * var + lev // 2

    def along(hops):
        place = lax.rem(chip + hops + 8, 8)
        return {"var": place // 4, "lev": 2 * lax.rem(place, 4) + bits[0]}

    def greet_tile(d, carry):
        pl.semaphore_signal(barrier, inc=1, device_id={"tile": lax.rem(tile + d, tiles)}, device_id_type=MESH)
        return carry

    for d in range(1, levels):
        pl.semaphore_signal(barrier, inc=1, device_id={"lev": peers[d]}, device_id_type=MESH)
    for hops in (2, -2):
        pl.semaphore_signal(barrier, inc=1, device_id=along(hops), device_id_type=MESH)
    lax.fori_loop(1, tiles, greet_tile, 0, unroll=True)
    loads[0].wait()
    loads[1].wait()
    scaled[...] = nf[...] * bg[...]
    loads[2].wait()
    quarter_mask[OWN, :] = 0.25 * mask_in[...].astype(f32)
    pl.semaphore_wait(barrier, (levels - 1) + (tiles - 1) + 2)

    for d in reversed(range(1, levels)):
        pltpu.make_async_remote_copy(
            src_ref=scaled.at[:, pl.ds(pl.multiple_of(peers[d] * part, part), part)],
            dst_ref=rhs.at[lev],
            send_sem=there_send,
            recv_sem=there_recv,
            device_id={"lev": peers[d]},
            device_id_type=MESH,
        ).start()
    rhs[lev] = scaled[:, pl.ds(pl.multiple_of(lev * part, part), part)]

    sides = ((16, 24, 8, 1), (16, 24, 24, -1), (22, 24, 6, 2), (16, 18, 32, -2))

    def reached(distance):
        return tile + distance <= top if distance > 0 else tile + distance >= 0

    def halo_copies(buffer, send, recv, at, width):
        for side, (low, high, land, distance) in enumerate(sides):

            @pl.when(reached(distance))
            def _(side=side, low=low, high=high, land=land, distance=distance):
                pltpu.make_async_remote_copy(
                    src_ref=buffer.at[low:high, pl.ds(at, width)],
                    dst_ref=buffer.at[land : land + high - low, pl.ds(at, width)],
                    send_sem=send.at[side],
                    recv_sem=recv.at[side],
                    device_id={"tile": tile + distance},
                    device_id_type=MESH,
                ).start()

    def halo_wait(buffer, sem, receive):
        for side, (low, high, land, distance) in enumerate(sides):

            @pl.when(reached(-distance if receive else distance))
            def _(side=side, low=low, high=high, land=land):
                at = slice(land, land + high - low) if receive else slice(low, high)
                pltpu.make_async_copy(buffer.at[at, :], buffer.at[at, :], sem.at[side]).wait()

    halo_copies(quarter_mask, mask_send, mask_recv, 0, columns)
    for side, (_, _, land, distance) in enumerate(sides):
        low = land // 8 * 8

        @pl.when(jnp.logical_not(reached(-distance)))
        def _(low=low):
            for buffer in (field, quarter_mask):
                buffer[low : low + 8, :] = jnp.zeros((8, columns), f32)

    loads[3].wait()
    above = jnp.zeros((ROWS, part), f32)
    upper_now = above
    for level in range(levels):
        coefficient = vd[level]
        inv = 1.0 / (1.0 + above + coefficient + above * upper_now)
        inverse[level] = inv
        below[level] = above * inv
        upper_now = -coefficient * inv
        upper[level] = upper_now
        above = coefficient

    loads[4].wait()

    @pl.when(tile >= top - 1)
    def _():
        order = fold_in[...]
        lane = lax.broadcasted_iota(jnp.int32, (1, columns), 1)
        mate = jnp.where(lane % 2 == 0, pltpu.roll(order, columns - 1, 1), pltpu.roll(order, 1, 1))
        row_hot = lax.broadcasted_iota(jnp.int32, (blocks, columns), 0) == order // 128
        lane_hot = lax.broadcasted_iota(jnp.int32, (128, columns), 0) == order % 128
        high = jnp.where(row_hot, (mate // 64).astype(f32), 0.0)
        low = jnp.where(row_hot, (mate % 64).astype(f32), 0.0)
        left = jnp.concatenate([high, low], axis=0).astype(jnp.bfloat16)
        right = jnp.where(lane_hot, 1.0, 0.0).astype(jnp.bfloat16)
        found = lax.dot_general(left, right, (((1,), (1,)), ((), ())), preferred_element_type=f32)
        partner = 64 * found[:blocks].astype(jnp.int32) + found[blocks:].astype(jnp.int32)
        partner_row[...] = partner // 128
        partner_lane[...] = partner % 128

    pltpu.make_async_copy(rhs.at[0 : levels - 1], rhs.at[0 : levels - 1], there_recv).wait()
    reduced = jnp.zeros((ROWS, part), f32)
    for level in range(levels):
        reduced = rhs[level] * inverse[level] + below[level] * reduced
        solved[level] = reduced
    value = jnp.zeros((ROWS, part), f32)
    for level in reversed(range(levels)):
        value = solved[level] - upper[level] * value
        solved[level] = value

    my_columns = pl.multiple_of(lev * part, part)

    for d in reversed(range(1, levels)):
        pltpu.make_async_remote_copy(
            src_ref=solved.at[peers[d]],
            dst_ref=field.at[OWN, pl.ds(my_columns, part)],
            send_sem=back_send,
            recv_sem=back_recv.at[d],
            device_id={"lev": peers[d]},
            device_id_type=MESH,
        ).start()
    field[OWN, pl.ds(my_columns, part)] = solved[lev]
    halo_copies(field, halo_send, halo_recv, my_columns, part)

    for d in range(1, levels):
        at = pl.multiple_of(peers[d] * part, part)
        here = field.at[OWN, pl.ds(at, part)]
        pltpu.make_async_copy(here, here, back_recv.at[d]).wait()
        halo_copies(field, halo_send, halo_recv, at, part)

    def fold(buffer, last_row):
        sums = tuple(jnp.zeros((8, 128), f32) for _ in range(blocks // 8))

        def pick(block, sums):
            at = pl.multiple_of(PAD + block * 128, 128)
            line = jnp.broadcast_to(buffer[last_row : last_row + 1, pl.ds(at, 128)], (8, 128))
            chosen = []
            for q, now in enumerate(sums):
                rows = slice(8 * q, 8 * q + 8)
                moved = jnp.take_along_axis(line, partner_lane[rows, :], axis=1)
                chosen.append(jnp.where(partner_row[rows, :] == block, moved, now))
            return tuple(chosen)

        sums = lax.fori_loop(0, blocks, pick, sums, unroll=True)
        for q, now in enumerate(sums):
            folded[8 * q : 8 * q + 8, :] = now
        for block in range(blocks):
            buffer[last_row + 1 : last_row + 2, PAD + block * 128 : PAD + block * 128 + 128] = folded[block : block + 1, :]

    def fold_top(buffer):
        @pl.when(tile == top)
        def _():
            fold(buffer, 23)

    def fold_next(buffer):
        @pl.when(tile == top - 1)
        def _():
            fold(buffer, 31)

    halo_wait(quarter_mask, mask_recv, True)
    halo_wait(field, halo_recv, True)
    masked = masked_p

    def apply_mask(chunk, carry):
        at = pl.multiple_of(chunk * 512, 512)
        masked[:, pl.ds(at + PAD, 512)] = 4.0 * quarter_mask[:, pl.ds(at, 512)] * field[:, pl.ds(at, 512)]
        return carry

    lax.fori_loop(0, columns // 512, apply_mask, 0, unroll=True)
    wrap(masked, (0, 40), columns)
    source = masked
    for j in range(STEPS):
        fold_top(source)
        if j < 2:
            fold_next(source)
        rows, loaded = ((0, 40), (0, 40)) if j == 0 else ((8, 32), (0, 40) if j == 1 else (8, 32))
        operator(source, v_chain[j], quarter_mask, columns, SHIFTS[j], rows, loaded)
        source = v_chain[j]

    def own_of(buffer, pad):
        rows = OWN if buffer.shape[0] == 40 else slice(0, 8)
        return lambda block: buffer[rows, pl.ds(pl.multiple_of(block * 128 + pad, 128), 128)]

    def reduce_over_tiles(index):
        def send(d, carry):
            pltpu.make_async_remote_copy(
                src_ref=message.at[index],
                dst_ref=received.at[index, tile],
                send_sem=sum_send.at[index],
                recv_sem=sum_recv.at[index],
                device_id={"tile": lax.rem(tile + d, tiles)},
                device_id_type=MESH,
            ).start()
            return carry

        lax.fori_loop(1, tiles, send, 0, unroll=True)

    def sum_over_tiles(index):
        others = received.at[index, 0 : tiles - 1]
        pltpu.make_async_copy(others, others, sum_recv.at[index]).wait()
        return jnp.sum(received[index], axis=0)

    shared = gram_message([own_of(field, 0)] + [own_of(v, PAD) for v in v_chain], columns)
    message[0] = shared
    received[0, tile] = shared
    reduce_over_tiles(0)
    diffusivity = h_diffusivity[0, 0]
    x_col, r_col, d_col = coefficient_cg(sum_over_tiles(0), (STEPS + 1,), diffusivity, STEPS, False)
    coef[0:16, :] = x_col
    coef[16:32, :] = r_col
    coef[32:48, :] = d_col

    def next_round(block, carry):
        at = pl.multiple_of(block * 128, 128)
        rows = slice(8, 32)
        held = [field[rows, pl.ds(at, 128)]] + [v[rows, pl.ds(at + PAD, 128)] for v in v_chain]
        residual = sum(coef[16 + j : 17 + j, :] * held[j] for j in range(STEPS + 1))
        direction = sum(coef[32 + j : 33 + j, :] * held[j] for j in range(STEPS + 1))
        mask = 4.0 * quarter_mask[rows, pl.ds(at, 128)]
        masked_r[rows, pl.ds(at + PAD, 128)] = mask * residual
        masked_p[rows, pl.ds(at + PAD, 128)] = mask * direction
        r_own[:, pl.ds(at, 128)] = residual[8:16]
        p_own[:, pl.ds(at, 128)] = direction[8:16]
        return carry

    lax.fori_loop(0, blocks, next_round, 0, unroll=8)
    wrap(masked_r, (8, 32), columns)
    wrap(masked_p, (8, 32), columns)

    for first, chain, length in ((masked_p, p_chain, STEPS), (masked_r, r_chain, STEPS - 1)):
        source = first
        for j in range(length):
            fold_top(source)
            rows = (16, 24) if j == length - 1 else (8, 32)
            operator(source, chain[j], quarter_mask, columns, SHIFTS[j], rows, (8, 32))
            source = chain[j]
    shared = gram_message(
        [own_of(p_own, 0)] + [own_of(p, PAD) for p in p_chain] + [own_of(r_own, 0)] + [own_of(r, PAD) for r in r_chain],
        columns,
    )
    message[1] = shared
    received[1, tile] = shared
    reduce_over_tiles(1)

    def part_one(block, carry):
        at = pl.multiple_of(block * 128, 128)
        held = [field[OWN, pl.ds(at, 128)]] + [v[OWN, pl.ds(at + PAD, 128)] for v in v_chain[: STEPS - 1]]
        result[:, pl.ds(at, 128)] = sum(coef[j : j + 1, :] * held[j] for j in range(STEPS))
        return carry

    lax.fori_loop(0, blocks, part_one, 0, unroll=8)
    x_col, r_col, d_col = coefficient_cg(sum_over_tiles(1), (STEPS + 1, STEPS), diffusivity, STEPS, True)
    coef[0:16, :] = x_col

    pieces = 8
    width = columns // pieces
    per_piece = width // 128
    ways = (2, -2)

    def leg(source, target, piece, index):
        here = pl.ds(pl.multiple_of(piece * width, width), width)
        return pltpu.make_async_remote_copy(
            src_ref=source.at[:, here],
            dst_ref=target.at[:, here],
            send_sem=last_send.at[index],
            recv_sem=half_recv.at[piece] if index == 0 else last_recv,
            device_id=along(ways[piece % 2]),
            device_id_type=MESH,
        )

    for piece in range(pieces):

        def part_two(block, carry, piece=piece):
            at = pl.multiple_of((piece * per_piece + block) * 128, 128)
            held = [p_own[:, pl.ds(at, 128)]] + [p[OWN, pl.ds(at + PAD, 128)] for p in p_chain[: STEPS - 1]]
            value = sum(coef[j : j + 1, :] * held[j] for j in range(STEPS))
            held = [r_own[:, pl.ds(at, 128)]] + [r[OWN, pl.ds(at + PAD, 128)] for r in r_chain[: STEPS - 2]]
            value += sum(coef[STEPS + 1 + j : STEPS + 2 + j, :] * held[j] for j in range(STEPS - 1))
            result[:, pl.ds(at, 128)] += value
            return carry

        lax.fori_loop(0, per_piece, part_two, 0, unroll=True)
        leg(result, halfway, piece, 0).start()
    for piece in range(pieces):
        arrived = halfway.at[:, piece * width : (piece + 1) * width]
        pltpu.make_async_copy(arrived, arrived, half_recv.at[piece]).wait()
        leg(halfway, other_out, piece, 1).start()
    keep = pltpu.make_async_copy(result, solved_out, last_local)
    keep.start()

    def sent(buffer, sem):
        pltpu.make_async_copy(buffer, buffer, sem).wait()

    sent(rhs.at[0 : levels - 1], there_send)
    sent(rhs.at[0 : levels - 1], back_send)
    halo_wait(quarter_mask, mask_send, False)
    halo_wait(field, halo_send, False)
    for index in range(2):
        sent(received.at[index, 0 : tiles - 1], sum_send.at[index])
    keep.wait()
    sent(result, last_send.at[0])
    sent(result, last_send.at[1])
    pltpu.make_async_copy(other_out, other_out, last_recv).wait()


def per_device(
    background, norm_factor, v_diffusivity, h_diffusivity, sea_mask, fold_order, coupling
):
    rows, columns = background.shape[2:]
    levels, tiles = lax.axis_size("lev"), lax.axis_size("tile")
    part = columns // levels
    f32 = jnp.float32
    strip = jax.ShapeDtypeStruct((rows, columns), f32)
    vmem = pltpu.VMEM
    tall = vmem((40, columns), f32)
    padded = vmem((40, columns + 2 * PAD), f32)
    blocks = columns // 128
    dma = pltpu.SemaphoreType.DMA
    in_hbm = functools.partial(pltpu.with_memory_space_constraint, memory_space=pltpu.HBM)
    solved, other = pl.pallas_call(
        kernel,
        out_shape=(strip, strip),
        in_specs=[pl.BlockSpec(memory_space=pl.ANY)] * 3
        + [pl.BlockSpec(memory_space=pltpu.SMEM)]
        + [pl.BlockSpec(memory_space=pl.ANY)] * 2,
        out_specs=(pl.BlockSpec(memory_space=pl.ANY),) * 2,
        scratch_shapes=[
            vmem((rows, columns), f32),
            vmem((rows, columns), f32),
            vmem((levels, rows, part), f32),
            vmem((rows, columns), jnp.int32),
            vmem((1, columns), jnp.int32),
            vmem((rows, columns), f32),
            vmem((levels, rows, part), f32),
            vmem((levels, rows, part), f32),
            vmem((levels, rows, part), f32),
            vmem((levels, rows, part), f32),
            vmem((levels, rows, part), f32),
            tall,
            tall,
            [padded] * STEPS,
            [padded] * STEPS,
            [padded] * (STEPS - 1),
            padded,
            padded,
            vmem((rows, columns), f32),
            vmem((rows, columns), f32),
            vmem((blocks, 128), jnp.int32),
            vmem((blocks, 128), jnp.int32),
            vmem((blocks, 128), f32),
            vmem((2, 1, 128), f32),
            vmem((2, tiles, 1, 128), f32),
            vmem((rows, columns), f32),
            vmem((rows, columns), f32),
            vmem((48, 128), f32),
            dma((5,)),
            dma,
            dma,
            dma,
            dma((levels,)),
            dma((4,)),
            dma((4,)),
            dma((4,)),
            dma((4,)),
            dma((2,)),
            dma((2,)),
            dma((2,)),
            dma((8,)),
            dma,
            dma,
        ],
        compiler_params=pltpu.CompilerParams(
            collective_id=0, has_side_effects=True, vmem_limit_bytes=40 * 2**20
        ),
    )(
        in_hbm(background.reshape(rows, columns)),
        in_hbm(norm_factor.reshape(rows, columns)),
        in_hbm(v_diffusivity.reshape(levels, rows, part)),
        h_diffusivity,
        in_hbm(sea_mask.reshape(rows, columns)),
        in_hbm(fold_order.reshape(1, columns)),
    )
    return (solved + coupling[0, 0] * other)[None, None]


def solution(mesh):
    placed = (
        P("var", "lev", "tile", None),
        P("var", "lev", "tile", None),
        P("var", None, "tile", "lev"),
        P("var", "lev"),
        P("lev", "tile", None),
        P(),
        P("var", "lev", "tile", None),
    )
    return jax.shard_map(
        per_device,
        mesh=mesh,
        in_specs=placed,
        out_specs=P("var", "lev", "tile", None),
        check_vma=False,
    )
```

```python
import functools

import jax
import jax.numpy as jnp
from jax import lax
from jax.experimental import pallas as pl
from jax.experimental.pallas import tpu as pltpu
from jax.sharding import PartitionSpec as P

MESH = pl.DeviceIdType.MESH
ROUNDS = (5, 5)
SHIFTS = (0.0, 5.0, 2.0, 7.0, 0.5)
ROWS = 8
PAD = 128
OWN = slice(8, 16)


def tree_sum(terms):
    terms = list(terms)
    while len(terms) > 1:
        terms = [sum(terms[i : i + 2]) for i in range(0, len(terms), 2)]
    return terms[0]


def pairs_of(count):
    return [(i, j) for i in range(count) for j in range(i, count)]


def gram_message(vectors, columns):
    pairs = pairs_of(len(vectors))
    lane = lax.broadcasted_iota(jnp.int32, (8, 128), 1)
    message = jnp.zeros((8, 128), jnp.float32)
    for at in range(0, len(pairs), 28):
        group = pairs[at : at + 28]
        used = sorted({i for pair in group for i in pair})

        def body(block, sums, group=group, used=used):
            held = {i: vectors[i](block) for i in used}
            return tuple(total + held[i] * held[j] for total, (i, j) in zip(sums, group))

        zeros = tuple(jnp.zeros((8, 128), jnp.float32) for _ in group)
        sums = lax.fori_loop(0, columns // 128, body, zeros, unroll=8)
        for place, total in enumerate(sums):
            message = jnp.where(lane == at + place, jnp.sum(total, axis=1, keepdims=True), message)
    return jnp.sum(message, axis=0, keepdims=True)


def coefficient_cg(totals, chains, diffusivity, steps, last):
    count = sum(chains)
    first = count - chains[-1]
    totals = jnp.broadcast_to(totals, (8, 128))
    gram = {}
    for place, (i, j) in enumerate(pairs_of(count)):
        gram[i, j] = gram[j, i] = jnp.broadcast_to(totals[:, place : place + 1], (8, 128))
    same, start = {}, 0
    for length in chains:
        for j in range(length - 1):
            same[start + j] = 1.0 + diffusivity * SHIFTS[j]
        start += length
    up = 4.0 * diffusivity

    def image_of(d):
        parts = {}
        for j, value in d.items():
            parts.setdefault(j, []).append(same[j] * value)
            parts.setdefault(j + 1, []).append(up * value)
        return {j: sum(terms) for j, terms in sorted(parts.items())}

    def product(u, v):
        return tree_sum(u[i] * tree_sum(gram[i, j] * v[j] for j in v) for i in u)

    def add(u, factor, v):
        return {j: (u[j] if j in u else 0.0) + (factor * v[j] if j in v else 0.0) for j in sorted({*u, *v})}

    d, r, x = {0: 1.0}, {first: 1.0}, {}
    norm_now = gram[first, first]
    for step in range(steps):
        image = image_of(d)
        energy = product(d, image)
        size = jnp.where(energy > 0, jnp.minimum(norm_now / energy, 1.0), 0.0)
        x = add(x, size, d)
        if last and step == steps - 1:
            break
        r = add(r, -size, image)
        norm_next = jnp.maximum(product(r, r), 0.0)
        d = add(r, jnp.where(norm_now > 0, norm_next / norm_now, 0.0), d)
        norm_now = norm_next
    return x, r, d


def packed(tall):
    upper_half = lax.broadcasted_iota(jnp.int32, (8, 128), 0) < 4
    return jnp.concatenate([tall[8:16], jnp.where(upper_half, tall[16:24], tall[0:8])], axis=0)


def operator(source, target, quarter_mask, columns, shift, rows, loaded, pack=False, group=8):
    lane = lax.broadcasted_iota(jnp.int32, (rows, 128), 1)
    cut = packed if pack else lambda value: value[0:rows]

    def body(chunk, carry):
        at = pl.multiple_of(chunk * (group * 128), 128)
        held, ahead, behind = {}, {}, {}
        for k in range(group + 2):
            held[k] = source[0:loaded, pl.ds(at + 128 * k, 128)]
            ahead[k] = pltpu.roll(cut(held[k]), 127, 1)
            behind[k] = pltpu.roll(cut(held[k]), 1, 1)
            if k < 2:
                continue
            here = held[k - 1]
            east = jnp.where(lane == 127, ahead[k], ahead[k - 1])
            west = jnp.where(lane == 0, behind[k - 2], behind[k - 1])
            north = cut(pltpu.roll(here, loaded - 1, 0))
            south = cut(pltpu.roll(here, 1, 0))
            here = cut(here)
            value = 4.0 * here - ((north + south) + (east + west))
            value = quarter_mask[0:rows, pl.ds(at + 128 * (k - 2), 128)] * value
            if shift:
                value = value - (0.25 * shift) * here
            target[0:rows, pl.ds(at + 128 * (k - 1), 128)] = value
        return carry

    lax.fori_loop(0, columns // (group * 128), body, 0, unroll=True)
    wrap(target, rows, columns)


def wrap(target, rows, columns):
    target[0:rows, 0:PAD] = target[0:rows, columns : columns + PAD]
    target[0:rows, columns + PAD : columns + 2 * PAD] = target[0:rows, PAD : 2 * PAD]


def kernel(
    background, norm_factor, v_diffusivity, h_diffusivity, sea_mask, fold_order,
    solved_out, other_out,
    bg, nf, vd, mask_in, fold_in, scaled, rhs, solved, inverse, below, upper,
    field, quarter_mask, packed_mask, masked, v_chain, p_chain, r_chain, masked_p, masked_r, p_own, r_own,
    partner_row, partner_lane, folded, message, received, result,
    load_sem, there_send, there_recv, back_send, back_recv,
    halo_send, halo_recv, mask_send, mask_recv, sum_send, sum_recv, last_send, last_recv, last_local,
):
    tile, lev, var = (lax.axis_index(a) for a in ("tile", "lev", "var"))
    tiles, levels = lax.axis_size("tile"), lax.axis_size("lev")
    columns = bg.shape[1]
    part = columns // levels
    top = tiles - 1
    blocks = columns // 128
    f32 = jnp.float32

    loads = [
        pltpu.make_async_copy(source, target, load_sem.at[i])
        for i, (source, target) in enumerate(
            ((background, bg), (norm_factor, nf), (sea_mask, mask_in), (v_diffusivity, vd), (fold_order, fold_in))
        )
    ]
    for load in loads:
        load.start()
    barrier = pltpu.get_barrier_semaphore()
    bits = (lax.rem(lev, 2), lax.rem(lev // 2, 2), lev // 4)

    def peer_level(d):
        return sum(
            (1 - bit if d >> place & 1 else bit) * (1 << place) for place, bit in enumerate(bits)
        )

    peers = [peer_level(d) for d in range(levels)]

    def greet_tile(d, carry):
        pl.semaphore_signal(barrier, inc=1, device_id={"tile": lax.rem(tile + d, tiles)}, device_id_type=MESH)
        return carry

    for d in range(1, levels):
        pl.semaphore_signal(barrier, inc=1, device_id={"lev": peers[d]}, device_id_type=MESH)
    pl.semaphore_signal(barrier, inc=1, device_id={"var": 1 - var}, device_id_type=MESH)
    lax.fori_loop(1, tiles, greet_tile, 0, unroll=True)
    loads[0].wait()
    loads[1].wait()
    scaled[...] = nf[...] * bg[...]
    loads[2].wait()
    quarter_mask[OWN, :] = 0.25 * mask_in[...].astype(f32)
    pl.semaphore_wait(barrier, (levels - 1) + (tiles - 1) + 1)

    for d in reversed(range(1, levels)):
        pltpu.make_async_remote_copy(
            src_ref=scaled.at[:, pl.ds(pl.multiple_of(peers[d] * part, part), part)],
            dst_ref=rhs.at[lev],
            send_sem=there_send,
            recv_sem=there_recv,
            device_id={"lev": peers[d]},
            device_id_type=MESH,
        ).start()
    rhs[lev] = scaled[:, pl.ds(pl.multiple_of(lev * part, part), part)]

    sides = ((8, 16, 0, 1), (8, 16, 16, -1), (14, 16, 30, 2), (8, 10, 24, -2))

    def reached(distance):
        return tile + distance <= top if distance > 0 else tile + distance >= 0

    def halo_copies(buffer, send, recv, at, width):
        for side, (low, high, land, distance) in enumerate(sides):

            @pl.when(reached(distance))
            def _(side=side, low=low, high=high, land=land, distance=distance):
                pltpu.make_async_remote_copy(
                    src_ref=buffer.at[low:high, pl.ds(at, width)],
                    dst_ref=buffer.at[land : land + high - low, pl.ds(at, width)],
                    send_sem=send.at[side],
                    recv_sem=recv.at[side],
                    device_id={"tile": tile + distance},
                    device_id_type=MESH,
                ).start()

    def halo_wait(buffer, sem, receive):
        for side, (low, high, land, distance) in enumerate(sides):

            @pl.when(reached(-distance if receive else distance))
            def _(side=side, low=low, high=high, land=land):
                at = slice(land, land + high - low) if receive else slice(low, high)
                pltpu.make_async_copy(buffer.at[at, :], buffer.at[at, :], sem.at[side]).wait()

    halo_copies(quarter_mask, mask_send, mask_recv, 0, columns)
    for low, high, land, distance in sides:

        @pl.when(jnp.logical_not(reached(-distance)))
        def _(land=land, rows=high - low):
            for buffer in (field, quarter_mask):
                buffer[land : land + rows, :] = jnp.zeros((rows, columns), f32)

    loads[3].wait()
    above = jnp.zeros((ROWS, part), f32)
    upper_now = above
    for level in range(levels):
        coefficient = vd[level]
        inv = 1.0 / (1.0 + above + coefficient + above * upper_now)
        inverse[level] = inv
        below[level] = above * inv
        upper_now = -coefficient * inv
        upper[level] = upper_now
        above = coefficient

    loads[4].wait()

    @pl.when(tile >= top - 1)
    def _():
        order = fold_in[...]
        lane = lax.broadcasted_iota(jnp.int32, (1, columns), 1)
        mate = jnp.where(lane % 2 == 0, pltpu.roll(order, columns - 1, 1), pltpu.roll(order, 1, 1))
        row_hot = lax.broadcasted_iota(jnp.int32, (blocks, columns), 0) == order // 128
        lane_hot = lax.broadcasted_iota(jnp.int32, (128, columns), 0) == order % 128
        high = jnp.where(row_hot, (mate // 64).astype(f32), 0.0)
        low = jnp.where(row_hot, (mate % 64).astype(f32), 0.0)
        left = jnp.concatenate([high, low], axis=0).astype(jnp.bfloat16)
        right = jnp.where(lane_hot, 1.0, 0.0).astype(jnp.bfloat16)
        found = lax.dot_general(left, right, (((1,), (1,)), ((), ())), preferred_element_type=f32)
        partner = 64 * found[:blocks].astype(jnp.int32) + found[blocks:].astype(jnp.int32)
        partner_row[...] = partner // 128
        partner_lane[...] = partner % 128

    pltpu.make_async_copy(rhs.at[0 : levels - 1], rhs.at[0 : levels - 1], there_recv).wait()
    reduced = jnp.zeros((ROWS, part), f32)
    for level in range(levels):
        reduced = rhs[level] * inverse[level] + below[level] * reduced
        solved[level] = reduced
    value = jnp.zeros((ROWS, part), f32)
    for level in reversed(range(levels)):
        value = solved[level] - upper[level] * value
        solved[level] = value

    my_columns = pl.multiple_of(lev * part, part)

    for d in reversed(range(1, levels)):
        pltpu.make_async_remote_copy(
            src_ref=solved.at[peers[d]],
            dst_ref=field.at[OWN, pl.ds(my_columns, part)],
            send_sem=back_send,
            recv_sem=back_recv.at[d],
            device_id={"lev": peers[d]},
            device_id_type=MESH,
        ).start()
    field[OWN, pl.ds(my_columns, part)] = solved[lev]
    halo_copies(field, halo_send, halo_recv, my_columns, part)

    for d in range(1, levels):
        at = pl.multiple_of(peers[d] * part, part)
        here = field.at[OWN, pl.ds(at, part)]
        pltpu.make_async_copy(here, here, back_recv.at[d]).wait()
        halo_copies(field, halo_send, halo_recv, at, part)

    def fold(buffer, last_row):
        sums = tuple(jnp.zeros((8, 128), f32) for _ in range(blocks // 8))

        def pick(block, sums):
            at = pl.multiple_of(PAD + block * 128, 128)
            line = jnp.broadcast_to(buffer[last_row : last_row + 1, pl.ds(at, 128)], (8, 128))
            chosen = []
            for q, now in enumerate(sums):
                rows = slice(8 * q, 8 * q + 8)
                moved = jnp.take_along_axis(line, partner_lane[rows, :], axis=1)
                chosen.append(jnp.where(partner_row[rows, :] == block, moved, now))
            return tuple(chosen)

        sums = lax.fori_loop(0, blocks, pick, sums, unroll=True)
        for q, now in enumerate(sums):
            folded[8 * q : 8 * q + 8, :] = now
        for block in range(blocks):
            buffer[last_row + 1 : last_row + 2, PAD + block * 128 : PAD + block * 128 + 128] = folded[block : block + 1, :]

    def fold_at(strip, buffer, last_row):
        @pl.when(tile == strip)
        def _():
            fold(buffer, last_row)

    first, second = ROUNDS
    halo_wait(quarter_mask, mask_recv, True)

    def pack_mask(block, carry):
        at = pl.multiple_of(block * 128, 128)
        packed_mask[:, pl.ds(at, 128)] = packed(quarter_mask[0:24, pl.ds(at, 128)])
        return carry

    lax.fori_loop(0, blocks, pack_mask, 0, unroll=8)
    halo_wait(field, halo_recv, True)

    def apply_mask(block, carry):
        at = pl.multiple_of(block * 128, 128)
        masked[:, pl.ds(at + PAD, 128)] = (4.0 * quarter_mask[:, pl.ds(at, 128)]) * field[:, pl.ds(at, 128)]
        return carry

    lax.fori_loop(0, blocks, apply_mask, 0, unroll=8)
    wrap(masked, 32, columns)
    source = masked
    for j in range(first):
        fold_at(top, source, 15)
        if j < 2:
            fold_at(top - 1, source, 23)
        operator(source, v_chain[j], quarter_mask, columns, SHIFTS[j], 32 if j == 0 else 24, 32 if j < 2 else 24)
        source = v_chain[j]

    def of(buffer, rows, pad):
        return lambda block: buffer[rows, pl.ds(pl.multiple_of(block * 128 + pad, 128), 128)]

    def reduce_over_tiles(index):
        def send(d, carry):
            pltpu.make_async_remote_copy(
                src_ref=message.at[index],
                dst_ref=received.at[index, tile],
                send_sem=sum_send.at[index],
                recv_sem=sum_recv.at[index],
                device_id={"tile": lax.rem(tile + d, tiles)},
                device_id_type=MESH,
            ).start()
            return carry

        lax.fori_loop(1, tiles, send, 0, unroll=True)

    def sum_over_tiles(index):
        others = received.at[index, 0 : tiles - 1]
        pltpu.make_async_copy(others, others, sum_recv.at[index]).wait()
        return jnp.sum(received[index], axis=0)

    shared = gram_message([of(field, OWN, 0)] + [of(v, OWN, PAD) for v in v_chain], columns)
    message[0] = shared
    received[0, tile] = shared
    reduce_over_tiles(0)
    diffusivity = h_diffusivity[0, 0]
    x_first, r_next, d_next = coefficient_cg(sum_over_tiles(0), (first + 1,), diffusivity, first, False)

    def next_round(block, carry):
        at = pl.multiple_of(block * 128, 128)
        rows = slice(0, 24)
        held = [field[rows, pl.ds(at, 128)]] + [v[rows, pl.ds(at + PAD, 128)] for v in v_chain]
        mask = 4.0 * quarter_mask[rows, pl.ds(at, 128)]
        for masked_one, own, numbers in ((masked_r, r_own, r_next), (masked_p, p_own, d_next)):
            tall = [jnp.concatenate([numbers[j]] * 3, axis=0) for j in numbers]
            value = tree_sum(number * held[j] for number, j in zip(tall, numbers))
            masked_one[:, pl.ds(at + PAD, 128)] = mask * value
            own[:, pl.ds(at, 128)] = value[8:16]
        return carry

    lax.fori_loop(0, blocks, next_round, 0, unroll=8)
    wrap(masked_r, 24, columns)
    wrap(masked_p, 24, columns)

    for start, chain, length in ((masked_p, p_chain, second), (masked_r, r_chain, second - 1)):
        source = start
        for j in range(length):
            fold_at(top, source, 15 if j == 0 else 7)
            rows, loaded = 8 if j == length - 1 else 16, 24 if j == 0 else 16
            operator(source, chain[j], packed_mask, columns, SHIFTS[j], rows, loaded, pack=j == 0)
            source = chain[j]
    strip_rows = slice(0, 8)
    p_basis = [of(p_own, strip_rows, 0)] + [of(p, strip_rows, PAD) for p in p_chain]
    r_basis = [of(r_own, strip_rows, 0)] + [of(r, strip_rows, PAD) for r in r_chain]
    shared = gram_message(p_basis + r_basis, columns)
    message[1] = shared
    received[1, tile] = shared
    reduce_over_tiles(1)
    v_basis = [of(field, OWN, 0)] + [of(v, OWN, PAD) for v in v_chain]

    def part_one(block, carry):
        at = pl.multiple_of(block * 128, 128)
        result[:, pl.ds(at, 128)] = tree_sum(x_first[j] * v_basis[j](block) for j in x_first)
        return carry

    lax.fori_loop(0, blocks, part_one, 0, unroll=8)
    x_second, _, _ = coefficient_cg(sum_over_tiles(1), (second + 1, second), diffusivity, second, True)

    basis = p_basis + r_basis
    pieces = 4
    width = columns // pieces
    for piece in range(pieces):

        def part_two(block, carry, piece=piece):
            block = block + piece * (width // 128)
            at = pl.multiple_of(block * 128, 128)
            result[:, pl.ds(at, 128)] += tree_sum(x_second[j] * basis[j](block) for j in x_second)
            return carry

        lax.fori_loop(0, width // 128, part_two, 0, unroll=True)
        here = slice(piece * width, piece * width + width)
        pltpu.make_async_remote_copy(
            src_ref=result.at[:, here],
            dst_ref=other_out.at[:, here],
            send_sem=last_send,
            recv_sem=last_recv,
            device_id={"var": 1 - var},
            device_id_type=MESH,
        ).start()
    keep = pltpu.make_async_copy(result, solved_out, last_local)
    keep.start()

    def sent(buffer, sem):
        pltpu.make_async_copy(buffer, buffer, sem).wait()

    sent(rhs.at[0 : levels - 1], there_send)
    sent(rhs.at[0 : levels - 1], back_send)
    halo_wait(quarter_mask, mask_send, False)
    halo_wait(field, halo_send, False)
    for index in range(2):
        sent(received.at[index, 0 : tiles - 1], sum_send.at[index])
    keep.wait()
    sent(result, last_send)
    pltpu.make_async_copy(other_out, other_out, last_recv).wait()


def per_device(
    background, norm_factor, v_diffusivity, h_diffusivity, sea_mask, fold_order, coupling
):
    rows, columns = background.shape[2:]
    levels, tiles = lax.axis_size("lev"), lax.axis_size("tile")
    part = columns // levels
    f32 = jnp.float32
    strip = jax.ShapeDtypeStruct((rows, columns), f32)
    vmem = pltpu.VMEM
    tall = vmem((32, columns), f32)

    def padded(height):
        return vmem((height, columns + 2 * PAD), f32)

    first, second = ROUNDS
    blocks = columns // 128
    dma = pltpu.SemaphoreType.DMA
    in_hbm = functools.partial(pltpu.with_memory_space_constraint, memory_space=pltpu.HBM)
    solved, other = pl.pallas_call(
        kernel,
        out_shape=(strip, strip),
        in_specs=[pl.BlockSpec(memory_space=pl.ANY)] * 3
        + [pl.BlockSpec(memory_space=pltpu.SMEM)]
        + [pl.BlockSpec(memory_space=pl.ANY)] * 2,
        out_specs=(pl.BlockSpec(memory_space=pl.ANY),) * 2,
        scratch_shapes=[
            vmem((rows, columns), f32),
            vmem((rows, columns), f32),
            vmem((levels, rows, part), f32),
            vmem((rows, columns), jnp.int32),
            vmem((1, columns), jnp.int32),
            vmem((rows, columns), f32),
            vmem((levels, rows, part), f32),
            vmem((levels, rows, part), f32),
            vmem((levels, rows, part), f32),
            vmem((levels, rows, part), f32),
            vmem((levels, rows, part), f32),
            tall,
            tall,
            vmem((16, columns), f32),
            padded(32),
            [padded(32 if j == 0 else 24) for j in range(first)],
            [padded(16)] * second,
            [padded(16)] * (second - 1),
            padded(24),
            padded(24),
            vmem((rows, columns), f32),
            vmem((rows, columns), f32),
            vmem((blocks, 128), jnp.int32),
            vmem((blocks, 128), jnp.int32),
            vmem((blocks, 128), f32),
            vmem((2, 1, 128), f32),
            vmem((2, tiles, 1, 128), f32),
            vmem((rows, columns), f32),
            dma((5,)),
            dma,
            dma,
            dma,
            dma((levels,)),
            dma((4,)),
            dma((4,)),
            dma((4,)),
            dma((4,)),
            dma((2,)),
            dma((2,)),
            dma,
            dma,
            dma,
        ],
        compiler_params=pltpu.CompilerParams(
            collective_id=0, has_side_effects=True, vmem_limit_bytes=40 * 2**20
        ),
    )(
        in_hbm(background.reshape(rows, columns)),
        in_hbm(norm_factor.reshape(rows, columns)),
        in_hbm(v_diffusivity.reshape(levels, rows, part)),
        h_diffusivity,
        in_hbm(sea_mask.reshape(rows, columns)),
        in_hbm(fold_order.reshape(1, columns)),
    )
    return (solved + coupling[0, 0] * other)[None, None]


def solution(mesh):
    placed = (
        P("var", "lev", "tile", None),
        P("var", "lev", "tile", None),
        P("var", None, "tile", "lev"),
        P("var", "lev"),
        P("lev", "tile", None),
        P(),
        P("var", "lev", "tile", None),
    )
    return jax.shard_map(
        per_device,
        mesh=mesh,
        in_specs=placed,
        out_specs=P("var", "lev", "tile", None),
        check_vma=False,
    )
```

```python
import functools

import jax
import jax.numpy as jnp
from jax import lax
from jax.experimental import pallas as pl
from jax.experimental.pallas import tpu as pltpu
from jax.sharding import PartitionSpec as P

MESH = pl.DeviceIdType.MESH
ROUNDS = (5, 5)
SHIFTS = (0.0, 5.0, 2.0, 7.0, 0.5)
ROWS = 8
PAD = 128
OWN = slice(8, 16)


def tree_sum(terms):
    terms = list(terms)
    while len(terms) > 1:
        terms = [sum(terms[i : i + 2]) for i in range(0, len(terms), 2)]
    return terms[0]


def pairs_of(count):
    return [(i, j) for i in range(count) for j in range(i, count)]


def gram_message(vectors, columns):
    pairs = pairs_of(len(vectors))
    lane = lax.broadcasted_iota(jnp.int32, (8, 128), 1)
    message = jnp.zeros((8, 128), jnp.float32)
    for at in range(0, len(pairs), 28):
        group = pairs[at : at + 28]
        used = sorted({i for pair in group for i in pair})

        def body(block, sums, group=group, used=used):
            held = {i: vectors[i](block) for i in used}
            return tuple(total + held[i] * held[j] for total, (i, j) in zip(sums, group))

        zeros = tuple(jnp.zeros((8, 128), jnp.float32) for _ in group)
        sums = lax.fori_loop(0, columns // 128, body, zeros, unroll=8)
        for place, total in enumerate(sums):
            message = jnp.where(lane == at + place, jnp.sum(total, axis=1, keepdims=True), message)
    return jnp.sum(message, axis=0, keepdims=True)


def coefficient_cg(totals, chains, diffusivity, steps, last):
    count = sum(chains)
    first = count - chains[-1]
    totals = jnp.broadcast_to(totals, (8, 128))
    gram = {}
    for place, (i, j) in enumerate(pairs_of(count)):
        gram[i, j] = gram[j, i] = jnp.broadcast_to(totals[:, place : place + 1], (8, 128))
    same, start = {}, 0
    for length in chains:
        for j in range(length - 1):
            same[start + j] = 1.0 + diffusivity * SHIFTS[j]
        start += length
    up = 4.0 * diffusivity

    def image_of(d):
        parts = {}
        for j, value in d.items():
            parts.setdefault(j, []).append(same[j] * value)
            parts.setdefault(j + 1, []).append(up * value)
        return {j: sum(terms) for j, terms in sorted(parts.items())}

    def product(u, v):
        return tree_sum(u[i] * tree_sum(gram[i, j] * v[j] for j in v) for i in u)

    def add(u, factor, v):
        return {j: (u[j] if j in u else 0.0) + (factor * v[j] if j in v else 0.0) for j in sorted({*u, *v})}

    d, r, x = {0: 1.0}, {first: 1.0}, {}
    norm_now = gram[first, first]
    for step in range(steps):
        image = image_of(d)
        energy = product(d, image)
        size = jnp.where(energy > 0, jnp.minimum(norm_now / energy, 1.0), 0.0)
        x = add(x, size, d)
        if last and step == steps - 1:
            break
        r = add(r, -size, image)
        norm_next = jnp.maximum(product(r, r), 0.0)
        d = add(r, jnp.where(norm_now > 0, norm_next / norm_now, 0.0), d)
        norm_now = norm_next
    return x, r, d


def packed(tall):
    upper_half = lax.broadcasted_iota(jnp.int32, (8, 128), 0) < 4
    return jnp.concatenate([tall[8:16], jnp.where(upper_half, tall[16:24], tall[0:8])], axis=0)


def operator(source, target, quarter_mask, columns, shift, rows, loaded, pack=False, group=8):
    lane = lax.broadcasted_iota(jnp.int32, (rows, 128), 1)
    cut = packed if pack else lambda value: value[0:rows]

    def body(chunk, carry):
        at = pl.multiple_of(chunk * (group * 128), 128)
        held, ahead, behind = {}, {}, {}
        for k in range(group + 2):
            held[k] = source[0:loaded, pl.ds(at + 128 * k, 128)]
            ahead[k] = pltpu.roll(cut(held[k]), 127, 1)
            behind[k] = pltpu.roll(cut(held[k]), 1, 1)
            if k < 2:
                continue
            here = held[k - 1]
            east = jnp.where(lane == 127, ahead[k], ahead[k - 1])
            west = jnp.where(lane == 0, behind[k - 2], behind[k - 1])
            north = cut(pltpu.roll(here, loaded - 1, 0))
            south = cut(pltpu.roll(here, 1, 0))
            here = cut(here)
            value = 4.0 * here - ((north + south) + (east + west))
            value = quarter_mask[0:rows, pl.ds(at + 128 * (k - 2), 128)] * value
            if shift:
                value = value - (0.25 * shift) * here
            target[0:rows, pl.ds(at + 128 * (k - 1), 128)] = value
        return carry

    lax.fori_loop(0, columns // (group * 128), body, 0, unroll=True)
    wrap(target, rows, columns)


def wrap(target, rows, columns):
    target[0:rows, 0:PAD] = target[0:rows, columns : columns + PAD]
    target[0:rows, columns + PAD : columns + 2 * PAD] = target[0:rows, PAD : 2 * PAD]


def kernel(
    background, norm_factor, v_diffusivity, h_diffusivity, sea_mask, fold_order,
    solved_out, other_out,
    bg, nf, vd, mask_in, fold_in, scaled, rhs, solved, inverse, below, upper,
    field, quarter_mask, packed_mask, masked, v_chain, p_chain, r_chain, masked_p, masked_r, p_own, r_own,
    partner_row, partner_lane, folded, message, near, total, far, result,
    load_sem, there_send, there_recv, back_send, back_recv,
    halo_send, halo_recv, mask_send, mask_recv, near_send, near_recv, far_send, far_recv, last_send, last_recv, last_local,
):
    tile, lev, var = (lax.axis_index(a) for a in ("tile", "lev", "var"))
    tiles, levels = lax.axis_size("tile"), lax.axis_size("lev")
    columns = bg.shape[1]
    part = columns // levels
    top = tiles - 1
    blocks = columns // 128
    f32 = jnp.float32

    loads = [
        pltpu.make_async_copy(source, target, load_sem.at[i])
        for i, (source, target) in enumerate(
            ((background, bg), (norm_factor, nf), (sea_mask, mask_in), (v_diffusivity, vd), (fold_order, fold_in))
        )
    ]
    for load in loads:
        load.start()
    barrier = pltpu.get_barrier_semaphore()
    bits = (lax.rem(lev, 2), lax.rem(lev // 2, 2), lev // 4)

    def peer_level(d):
        return sum(
            (1 - bit if d >> place & 1 else bit) * (1 << place) for place, bit in enumerate(bits)
        )

    peers = [peer_level(d) for d in range(levels)]

    across = 8
    run, place = tile // across, lax.rem(tile, across)
    in_run = [across * run + lax.rem(place + d, across) for d in range(across)]
    over_runs = [lax.rem(tile + across * d, tiles) for d in range(tiles // across)]
    beside = [lax.rem(tile + d + tiles, tiles) for d in (1, -1, 2, -2)]

    for d in range(1, levels):
        pl.semaphore_signal(barrier, inc=1, device_id={"lev": peers[d]}, device_id_type=MESH)
    pl.semaphore_signal(barrier, inc=1, device_id={"var": 1 - var}, device_id_type=MESH)
    strips = beside + in_run[1:] + over_runs[1:]
    for to in strips:
        pl.semaphore_signal(barrier, inc=1, device_id={"tile": to}, device_id_type=MESH)
    loads[0].wait()
    loads[1].wait()
    scaled[...] = nf[...] * bg[...]
    loads[2].wait()
    quarter_mask[OWN, :] = 0.25 * mask_in[...].astype(f32)
    pl.semaphore_wait(barrier, (levels - 1) + len(strips) + 1)

    for d in reversed(range(1, levels)):
        pltpu.make_async_remote_copy(
            src_ref=scaled.at[:, pl.ds(pl.multiple_of(peers[d] * part, part), part)],
            dst_ref=rhs.at[lev],
            send_sem=there_send,
            recv_sem=there_recv,
            device_id={"lev": peers[d]},
            device_id_type=MESH,
        ).start()
    rhs[lev] = scaled[:, pl.ds(pl.multiple_of(lev * part, part), part)]

    sides = ((8, 16, 0, 1), (8, 16, 16, -1), (14, 16, 30, 2), (8, 10, 24, -2))

    def reached(distance):
        return tile + distance <= top if distance > 0 else tile + distance >= 0

    def halo_copies(buffer, send, recv, at, width):
        for side, (low, high, land, distance) in enumerate(sides):

            @pl.when(reached(distance))
            def _(side=side, low=low, high=high, land=land, distance=distance):
                pltpu.make_async_remote_copy(
                    src_ref=buffer.at[low:high, pl.ds(at, width)],
                    dst_ref=buffer.at[land : land + high - low, pl.ds(at, width)],
                    send_sem=send.at[side],
                    recv_sem=recv.at[side],
                    device_id={"tile": tile + distance},
                    device_id_type=MESH,
                ).start()

    def halo_wait(buffer, sem, receive):
        for side, (low, high, land, distance) in enumerate(sides):

            @pl.when(reached(-distance if receive else distance))
            def _(side=side, low=low, high=high, land=land):
                at = slice(land, land + high - low) if receive else slice(low, high)
                pltpu.make_async_copy(buffer.at[at, :], buffer.at[at, :], sem.at[side]).wait()

    halo_copies(quarter_mask, mask_send, mask_recv, 0, columns)
    for low, high, land, distance in sides:

        @pl.when(jnp.logical_not(reached(-distance)))
        def _(land=land, rows=high - low):
            for buffer in (field, quarter_mask):
                buffer[land : land + rows, :] = jnp.zeros((rows, columns), f32)

    loads[3].wait()
    above = jnp.zeros((ROWS, part), f32)
    upper_now = above
    for level in range(levels):
        coefficient = vd[level]
        inv = 1.0 / (1.0 + above + coefficient + above * upper_now)
        inverse[level] = inv
        below[level] = above * inv
        upper_now = -coefficient * inv
        upper[level] = upper_now
        above = coefficient

    loads[4].wait()

    @pl.when(tile >= top - 1)
    def _():
        order = fold_in[...]
        lane = lax.broadcasted_iota(jnp.int32, (1, columns), 1)
        mate = jnp.where(lane % 2 == 0, pltpu.roll(order, columns - 1, 1), pltpu.roll(order, 1, 1))
        row_hot = lax.broadcasted_iota(jnp.int32, (blocks, columns), 0) == order // 128
        lane_hot = lax.broadcasted_iota(jnp.int32, (128, columns), 0) == order % 128
        high = jnp.where(row_hot, (mate // 64).astype(f32), 0.0)
        low = jnp.where(row_hot, (mate % 64).astype(f32), 0.0)
        left = jnp.concatenate([high, low], axis=0).astype(jnp.bfloat16)
        right = jnp.where(lane_hot, 1.0, 0.0).astype(jnp.bfloat16)
        found = lax.dot_general(left, right, (((1,), (1,)), ((), ())), preferred_element_type=f32)
        partner = 64 * found[:blocks].astype(jnp.int32) + found[blocks:].astype(jnp.int32)
        partner_row[...] = partner // 128
        partner_lane[...] = partner % 128

    pltpu.make_async_copy(rhs.at[0 : levels - 1], rhs.at[0 : levels - 1], there_recv).wait()
    reduced = jnp.zeros((ROWS, part), f32)
    for level in range(levels):
        reduced = rhs[level] * inverse[level] + below[level] * reduced
        solved[level] = reduced
    value = jnp.zeros((ROWS, part), f32)
    for level in reversed(range(levels)):
        value = solved[level] - upper[level] * value
        solved[level] = value

    my_columns = pl.multiple_of(lev * part, part)

    for d in reversed(range(1, levels)):
        pltpu.make_async_remote_copy(
            src_ref=solved.at[peers[d]],
            dst_ref=field.at[OWN, pl.ds(my_columns, part)],
            send_sem=back_send,
            recv_sem=back_recv.at[d],
            device_id={"lev": peers[d]},
            device_id_type=MESH,
        ).start()
    field[OWN, pl.ds(my_columns, part)] = solved[lev]
    halo_copies(field, halo_send, halo_recv, my_columns, part)

    for d in range(1, levels):
        at = pl.multiple_of(peers[d] * part, part)
        here = field.at[OWN, pl.ds(at, part)]
        pltpu.make_async_copy(here, here, back_recv.at[d]).wait()
        halo_copies(field, halo_send, halo_recv, at, part)

    def fold(buffer, last_row):
        sums = tuple(jnp.zeros((8, 128), f32) for _ in range(blocks // 8))

        def pick(block, sums):
            at = pl.multiple_of(PAD + block * 128, 128)
            line = jnp.broadcast_to(buffer[last_row : last_row + 1, pl.ds(at, 128)], (8, 128))
            chosen = []
            for q, now in enumerate(sums):
                rows = slice(8 * q, 8 * q + 8)
                moved = jnp.take_along_axis(line, partner_lane[rows, :], axis=1)
                chosen.append(jnp.where(partner_row[rows, :] == block, moved, now))
            return tuple(chosen)

        sums = lax.fori_loop(0, blocks, pick, sums, unroll=True)
        for q, now in enumerate(sums):
            folded[8 * q : 8 * q + 8, :] = now
        for block in range(blocks):
            buffer[last_row + 1 : last_row + 2, PAD + block * 128 : PAD + block * 128 + 128] = folded[block : block + 1, :]

    def fold_at(strip, buffer, last_row):
        @pl.when(tile == strip)
        def _():
            fold(buffer, last_row)

    first, second = ROUNDS
    halo_wait(quarter_mask, mask_recv, True)

    def pack_mask(block, carry):
        at = pl.multiple_of(block * 128, 128)
        packed_mask[:, pl.ds(at, 128)] = packed(quarter_mask[0:24, pl.ds(at, 128)])
        return carry

    lax.fori_loop(0, blocks, pack_mask, 0, unroll=8)
    halo_wait(field, halo_recv, True)

    def apply_mask(block, carry):
        at = pl.multiple_of(block * 128, 128)
        masked[:, pl.ds(at + PAD, 128)] = (4.0 * quarter_mask[:, pl.ds(at, 128)]) * field[:, pl.ds(at, 128)]
        return carry

    lax.fori_loop(0, blocks, apply_mask, 0, unroll=8)
    wrap(masked, 32, columns)
    source = masked
    for j in range(first):
        fold_at(top, source, 15)
        if j < 2:
            fold_at(top - 1, source, 23)
        operator(source, v_chain[j], quarter_mask, columns, SHIFTS[j], 32 if j == 0 else 24, 32 if j < 2 else 24)
        source = v_chain[j]

    def of(buffer, rows, pad):
        return lambda block: buffer[rows, pl.ds(pl.multiple_of(block * 128 + pad, 128), 128)]

    def send_sums(message, received, peers_here, own_slot, send, recv):
        for to in peers_here[1:]:
            pltpu.make_async_remote_copy(
                src_ref=message,
                dst_ref=received.at[own_slot],
                send_sem=send,
                recv_sem=recv,
                device_id={"tile": to},
                device_id_type=MESH,
            ).start()

    def take_sums(received, recv):
        others = received.at[0 : received.shape[0] - 1]
        pltpu.make_async_copy(others, others, recv).wait()
        return jnp.sum(received[...], axis=0)

    def reduce_over_tiles(index, shared):
        message[index] = shared
        near[index, place] = shared
        send_sums(message.at[index], near.at[index], in_run, place, near_send.at[index], near_recv.at[index])

    def sum_over_tiles(index):
        shared = take_sums(near.at[index], near_recv.at[index])
        total[index] = shared
        far[index, run] = shared
        send_sums(total.at[index], far.at[index], over_runs, run, far_send.at[index], far_recv.at[index])
        return take_sums(far.at[index], far_recv.at[index])

    shared = gram_message([of(field, OWN, 0)] + [of(v, OWN, PAD) for v in v_chain], columns)
    reduce_over_tiles(0, shared)
    diffusivity = h_diffusivity[0, 0]
    x_first, r_next, d_next = coefficient_cg(sum_over_tiles(0), (first + 1,), diffusivity, first, False)

    def next_round(block, carry):
        at = pl.multiple_of(block * 128, 128)
        rows = slice(0, 24)
        held = [field[rows, pl.ds(at, 128)]] + [v[rows, pl.ds(at + PAD, 128)] for v in v_chain]
        mask = 4.0 * quarter_mask[rows, pl.ds(at, 128)]
        for masked_one, own, numbers in ((masked_r, r_own, r_next), (masked_p, p_own, d_next)):
            tall = [jnp.concatenate([numbers[j]] * 3, axis=0) for j in numbers]
            value = tree_sum(number * held[j] for number, j in zip(tall, numbers))
            masked_one[:, pl.ds(at + PAD, 128)] = mask * value
            own[:, pl.ds(at, 128)] = value[8:16]
        return carry

    lax.fori_loop(0, blocks, next_round, 0, unroll=8)
    wrap(masked_r, 24, columns)
    wrap(masked_p, 24, columns)

    for start, chain, length in ((masked_p, p_chain, second), (masked_r, r_chain, second - 1)):
        source = start
        for j in range(length):
            fold_at(top, source, 15 if j == 0 else 7)
            rows, loaded = 8 if j == length - 1 else 16, 24 if j == 0 else 16
            operator(source, chain[j], packed_mask, columns, SHIFTS[j], rows, loaded, pack=j == 0)
            source = chain[j]
    strip_rows = slice(0, 8)
    p_basis = [of(p_own, strip_rows, 0)] + [of(p, strip_rows, PAD) for p in p_chain]
    r_basis = [of(r_own, strip_rows, 0)] + [of(r, strip_rows, PAD) for r in r_chain]
    shared = gram_message(p_basis + r_basis, columns)
    reduce_over_tiles(1, shared)
    v_basis = [of(field, OWN, 0)] + [of(v, OWN, PAD) for v in v_chain]

    def part_one(block, carry):
        at = pl.multiple_of(block * 128, 128)
        result[:, pl.ds(at, 128)] = tree_sum(x_first[j] * v_basis[j](block) for j in x_first)
        return carry

    lax.fori_loop(0, blocks, part_one, 0, unroll=8)
    x_second, _, _ = coefficient_cg(sum_over_tiles(1), (second + 1, second), diffusivity, second, True)

    basis = p_basis + r_basis
    pieces = 4
    width = columns // pieces
    for piece in range(pieces):

        def part_two(block, carry, piece=piece):
            block = block + piece * (width // 128)
            at = pl.multiple_of(block * 128, 128)
            result[:, pl.ds(at, 128)] += tree_sum(x_second[j] * basis[j](block) for j in x_second)
            return carry

        lax.fori_loop(0, width // 128, part_two, 0, unroll=True)
        here = slice(piece * width, piece * width + width)
        pltpu.make_async_remote_copy(
            src_ref=result.at[:, here],
            dst_ref=other_out.at[:, here],
            send_sem=last_send,
            recv_sem=last_recv,
            device_id={"var": 1 - var},
            device_id_type=MESH,
        ).start()
    keep = pltpu.make_async_copy(result, solved_out, last_local)
    keep.start()

    def sent(buffer, sem):
        pltpu.make_async_copy(buffer, buffer, sem).wait()

    sent(rhs.at[0 : levels - 1], there_send)
    sent(rhs.at[0 : levels - 1], back_send)
    halo_wait(quarter_mask, mask_send, False)
    halo_wait(field, halo_send, False)
    for index in range(2):
        sent(near.at[index, 0 : across - 1], near_send.at[index])
        sent(far.at[index, 0 : tiles // across - 1], far_send.at[index])
    keep.wait()
    sent(result, last_send)
    pltpu.make_async_copy(other_out, other_out, last_recv).wait()


def per_device(
    background, norm_factor, v_diffusivity, h_diffusivity, sea_mask, fold_order, coupling
):
    rows, columns = background.shape[2:]
    levels, tiles = lax.axis_size("lev"), lax.axis_size("tile")
    part = columns // levels
    f32 = jnp.float32
    strip = jax.ShapeDtypeStruct((rows, columns), f32)
    vmem = pltpu.VMEM
    tall = vmem((32, columns), f32)

    def padded(height):
        return vmem((height, columns + 2 * PAD), f32)

    first, second = ROUNDS
    blocks = columns // 128
    dma = pltpu.SemaphoreType.DMA
    in_hbm = functools.partial(pltpu.with_memory_space_constraint, memory_space=pltpu.HBM)
    solved, other = pl.pallas_call(
        kernel,
        out_shape=(strip, strip),
        in_specs=[pl.BlockSpec(memory_space=pl.ANY)] * 3
        + [pl.BlockSpec(memory_space=pltpu.SMEM)]
        + [pl.BlockSpec(memory_space=pl.ANY)] * 2,
        out_specs=(pl.BlockSpec(memory_space=pl.ANY),) * 2,
        scratch_shapes=[
            vmem((rows, columns), f32),
            vmem((rows, columns), f32),
            vmem((levels, rows, part), f32),
            vmem((rows, columns), jnp.int32),
            vmem((1, columns), jnp.int32),
            vmem((rows, columns), f32),
            vmem((levels, rows, part), f32),
            vmem((levels, rows, part), f32),
            vmem((levels, rows, part), f32),
            vmem((levels, rows, part), f32),
            vmem((levels, rows, part), f32),
            tall,
            tall,
            vmem((16, columns), f32),
            padded(32),
            [padded(32 if j == 0 else 24) for j in range(first)],
            [padded(16)] * second,
            [padded(16)] * (second - 1),
            padded(24),
            padded(24),
            vmem((rows, columns), f32),
            vmem((rows, columns), f32),
            vmem((blocks, 128), jnp.int32),
            vmem((blocks, 128), jnp.int32),
            vmem((blocks, 128), f32),
            vmem((2, 1, 128), f32),
            vmem((2, 8, 1, 128), f32),
            vmem((2, 1, 128), f32),
            vmem((2, tiles // 8, 1, 128), f32),
            vmem((rows, columns), f32),
            dma((5,)),
            dma,
            dma,
            dma,
            dma((levels,)),
            dma((4,)),
            dma((4,)),
            dma((4,)),
            dma((4,)),
            dma((2,)),
            dma((2,)),
            dma((2,)),
            dma((2,)),
            dma,
            dma,
            dma,
        ],
        compiler_params=pltpu.CompilerParams(
            collective_id=0, has_side_effects=True, vmem_limit_bytes=40 * 2**20
        ),
    )(
        in_hbm(background.reshape(rows, columns)),
        in_hbm(norm_factor.reshape(rows, columns)),
        in_hbm(v_diffusivity.reshape(levels, rows, part)),
        h_diffusivity,
        in_hbm(sea_mask.reshape(rows, columns)),
        in_hbm(fold_order.reshape(1, columns)),
    )
    return (solved + coupling[0, 0] * other)[None, None]


def solution(mesh):
    placed = (
        P("var", "lev", "tile", None),
        P("var", "lev", "tile", None),
        P("var", None, "tile", "lev"),
        P("var", "lev"),
        P("lev", "tile", None),
        P(),
        P("var", "lev", "tile", None),
    )
    return jax.shard_map(
        per_device,
        mesh=mesh,
        in_specs=placed,
        out_specs=P("var", "lev", "tile", None),
        check_vma=False,
    )
```

```python
import functools

import jax
import jax.numpy as jnp
from jax import lax
from jax.experimental import pallas as pl
from jax.experimental.pallas import tpu as pltpu
from jax.sharding import PartitionSpec as P

MESH = pl.DeviceIdType.MESH
ROUNDS = (5, 5)
SHIFTS = (0.0, 5.0, 2.0, 7.0, 0.5)
ROWS = 8
PAD = 128
OWN = slice(8, 16)


def tree_sum(terms):
    terms = list(terms)
    while len(terms) > 1:
        terms = [sum(terms[i : i + 2]) for i in range(0, len(terms), 2)]
    return terms[0]


def pairs_of(count):
    return [(i, j) for i in range(count) for j in range(i, count)]


def gram_message(vectors, columns):
    pairs = pairs_of(len(vectors))
    lane = lax.broadcasted_iota(jnp.int32, (8, 128), 1)
    message = jnp.zeros((8, 128), jnp.float32)
    for at in range(0, len(pairs), 28):
        group = pairs[at : at + 28]
        used = sorted({i for pair in group for i in pair})

        def body(block, sums, group=group, used=used):
            held = {i: vectors[i](block) for i in used}
            return tuple(total + held[i] * held[j] for total, (i, j) in zip(sums, group))

        zeros = tuple(jnp.zeros((8, 128), jnp.float32) for _ in group)
        sums = lax.fori_loop(0, columns // 128, body, zeros, unroll=8)
        for place, total in enumerate(sums):
            message = jnp.where(lane == at + place, jnp.sum(total, axis=1, keepdims=True), message)
    return jnp.sum(message, axis=0, keepdims=True)


def coefficient_cg(totals, chains, diffusivity, steps, last):
    count = sum(chains)
    first = count - chains[-1]
    totals = jnp.broadcast_to(totals, (8, 128))
    gram = {}
    for place, (i, j) in enumerate(pairs_of(count)):
        gram[i, j] = gram[j, i] = jnp.broadcast_to(totals[:, place : place + 1], (8, 128))
    same, start = {}, 0
    for length in chains:
        for j in range(length - 1):
            same[start + j] = 1.0 + diffusivity * SHIFTS[j]
        start += length
    up = 4.0 * diffusivity

    def image_of(d):
        parts = {}
        for j, value in d.items():
            parts.setdefault(j, []).append(same[j] * value)
            parts.setdefault(j + 1, []).append(up * value)
        return {j: sum(terms) for j, terms in sorted(parts.items())}

    def product(u, v):
        return tree_sum(u[i] * tree_sum(gram[i, j] * v[j] for j in v) for i in u)

    def add(u, factor, v):
        return {j: (u[j] if j in u else 0.0) + (factor * v[j] if j in v else 0.0) for j in sorted({*u, *v})}

    d, r, x = {0: 1.0}, {first: 1.0}, {}
    norm_now = gram[first, first]
    for step in range(steps):
        image = image_of(d)
        energy = product(d, image)
        size = jnp.where(energy > 0, jnp.minimum(norm_now / energy, 1.0), 0.0)
        x = add(x, size, d)
        if last and step == steps - 1:
            break
        r = add(r, -size, image)
        norm_next = jnp.maximum(product(r, r), 0.0)
        d = add(r, jnp.where(norm_now > 0, norm_next / norm_now, 0.0), d)
        norm_now = norm_next
    return x, r, d


def packed(tall):
    upper_half = lax.broadcasted_iota(jnp.int32, (8, 128), 0) < 4
    return jnp.concatenate([tall[8:16], jnp.where(upper_half, tall[16:24], tall[0:8])], axis=0)


def operator(source, target, quarter_mask, columns, shift, rows, loaded, pack=False, folded=None, group=8):
    lane = lax.broadcasted_iota(jnp.int32, (rows, 128), 1)
    if folded is not None:
        line, last_row = folded
        is_last = lax.broadcasted_iota(jnp.int32, (rows, 128), 0) == last_row
    cut = packed if pack else lambda value: value[0:rows]

    def body(chunk, carry):
        at = pl.multiple_of(chunk * (group * 128), 128)
        held, ahead, behind = {}, {}, {}
        for k in range(group + 2):
            held[k] = source[0:loaded, pl.ds(at + 128 * k, 128)]
            ahead[k] = pltpu.roll(cut(held[k]), 127, 1)
            behind[k] = pltpu.roll(cut(held[k]), 1, 1)
            if k < 2:
                continue
            here = held[k - 1]
            east = jnp.where(lane == 127, ahead[k], ahead[k - 1])
            west = jnp.where(lane == 0, behind[k - 2], behind[k - 1])
            north = cut(pltpu.roll(here, loaded - 1, 0))
            south = cut(pltpu.roll(here, 1, 0))
            if folded is not None:
                north = jnp.where(is_last, line[pl.ds(chunk * group + k - 2, 1), :], north)
            here = cut(here)
            value = 4.0 * here - ((north + south) + (east + west))
            value = quarter_mask[0:rows, pl.ds(at + 128 * (k - 2), 128)] * value
            if shift:
                value = value - (0.25 * shift) * here
            target[0:rows, pl.ds(at + 128 * (k - 1), 128)] = value
        return carry

    lax.fori_loop(0, columns // (group * 128), body, 0, unroll=True)
    wrap(target, rows, columns)


def wrap(target, rows, columns):
    target[0:rows, 0:PAD] = target[0:rows, columns : columns + PAD]
    target[0:rows, columns + PAD : columns + 2 * PAD] = target[0:rows, PAD : 2 * PAD]


def kernel(
    background, norm_factor, v_diffusivity, h_diffusivity, sea_mask, fold_order,
    solved_out, other_out,
    bg, nf, vd, mask_in, fold_in, scaled, rhs, solved, inverse, below, upper,
    field, quarter_mask, packed_mask, masked, v_chain, p_chain, r_chain, masked_p, masked_r, p_own, r_own,
    partner_row, partner_lane, lines, folded_p, folded_r, message, received, result,
    load_sem, there_send, there_recv, back_send, back_recv,
    halo_send, halo_recv, mask_send, mask_recv, sum_send, sum_recv, last_send, last_recv, last_local,
):
    tile, lev, var = (lax.axis_index(a) for a in ("tile", "lev", "var"))
    tiles, levels = lax.axis_size("tile"), lax.axis_size("lev")
    columns = bg.shape[1]
    part = columns // levels
    top = tiles - 1
    blocks = columns // 128
    f32 = jnp.float32

    loads = [
        pltpu.make_async_copy(source, target, load_sem.at[i])
        for i, (source, target) in enumerate(
            ((background, bg), (norm_factor, nf), (sea_mask, mask_in), (v_diffusivity, vd), (fold_order, fold_in))
        )
    ]
    for load in loads:
        load.start()
    barrier = pltpu.get_barrier_semaphore()
    bits = (lax.rem(lev, 2), lax.rem(lev // 2, 2), lev // 4)

    def peer_level(d):
        return sum(
            (1 - bit if d >> place & 1 else bit) * (1 << place) for place, bit in enumerate(bits)
        )

    peers = [peer_level(d) for d in range(levels)]

    def greet_tile(d, carry):
        pl.semaphore_signal(barrier, inc=1, device_id={"tile": lax.rem(tile + d, tiles)}, device_id_type=MESH)
        return carry

    for d in range(1, levels):
        pl.semaphore_signal(barrier, inc=1, device_id={"lev": peers[d]}, device_id_type=MESH)
    pl.semaphore_signal(barrier, inc=1, device_id={"var": 1 - var}, device_id_type=MESH)
    lax.fori_loop(1, tiles, greet_tile, 0, unroll=True)
    loads[0].wait()
    loads[1].wait()
    scaled[...] = nf[...] * bg[...]
    loads[2].wait()
    quarter_mask[OWN, :] = 0.25 * mask_in[...].astype(f32)
    pl.semaphore_wait(barrier, (levels - 1) + (tiles - 1) + 1)

    for d in reversed(range(1, levels)):
        pltpu.make_async_remote_copy(
            src_ref=scaled.at[:, pl.ds(pl.multiple_of(peers[d] * part, part), part)],
            dst_ref=rhs.at[lev],
            send_sem=there_send,
            recv_sem=there_recv,
            device_id={"lev": peers[d]},
            device_id_type=MESH,
        ).start()
    rhs[lev] = scaled[:, pl.ds(pl.multiple_of(lev * part, part), part)]

    sides = ((8, 16, 0, 1), (8, 16, 16, -1), (14, 16, 30, 2), (8, 10, 24, -2))

    def reached(distance):
        return tile + distance <= top if distance > 0 else tile + distance >= 0

    def halo_copies(buffer, send, recv, at, width):
        for side, (low, high, land, distance) in enumerate(sides):

            @pl.when(reached(distance))
            def _(side=side, low=low, high=high, land=land, distance=distance):
                pltpu.make_async_remote_copy(
                    src_ref=buffer.at[low:high, pl.ds(at, width)],
                    dst_ref=buffer.at[land : land + high - low, pl.ds(at, width)],
                    send_sem=send.at[side],
                    recv_sem=recv.at[side],
                    device_id={"tile": tile + distance},
                    device_id_type=MESH,
                ).start()

    def halo_wait(buffer, sem, receive):
        for side, (low, high, land, distance) in enumerate(sides):

            @pl.when(reached(-distance if receive else distance))
            def _(side=side, low=low, high=high, land=land):
                at = slice(land, land + high - low) if receive else slice(low, high)
                pltpu.make_async_copy(buffer.at[at, :], buffer.at[at, :], sem.at[side]).wait()

    halo_copies(quarter_mask, mask_send, mask_recv, 0, columns)
    for low, high, land, distance in sides:

        @pl.when(jnp.logical_not(reached(-distance)))
        def _(land=land, rows=high - low):
            for buffer in (field, quarter_mask):
                buffer[land : land + rows, :] = jnp.zeros((rows, columns), f32)

    @pl.when(tile == top)
    def _():
        for chain in v_chain[1:]:
            chain[16:24, :] = jnp.zeros((8, chain.shape[1]), f32)

    loads[3].wait()
    above = jnp.zeros((ROWS, part), f32)
    upper_now = above
    for level in range(levels):
        coefficient = vd[level]
        inv = 1.0 / (1.0 + above + coefficient + above * upper_now)
        inverse[level] = inv
        below[level] = above * inv
        upper_now = -coefficient * inv
        upper[level] = upper_now
        above = coefficient

    loads[4].wait()

    @pl.when(tile >= top - 1)
    def _():
        order = fold_in[...]
        lane = lax.broadcasted_iota(jnp.int32, (1, columns), 1)
        mate = jnp.where(lane % 2 == 0, pltpu.roll(order, columns - 1, 1), pltpu.roll(order, 1, 1))
        row_hot = lax.broadcasted_iota(jnp.int32, (blocks, columns), 0) == order // 128
        lane_hot = lax.broadcasted_iota(jnp.int32, (128, columns), 0) == order % 128
        high = jnp.where(row_hot, (mate // 64).astype(f32), 0.0)
        low = jnp.where(row_hot, (mate % 64).astype(f32), 0.0)
        left = jnp.concatenate([high, low], axis=0).astype(jnp.bfloat16)
        right = jnp.where(lane_hot, 1.0, 0.0).astype(jnp.bfloat16)
        found = lax.dot_general(left, right, (((1,), (1,)), ((), ())), preferred_element_type=f32)
        partner = 64 * found[:blocks].astype(jnp.int32) + found[blocks:].astype(jnp.int32)
        partner_row[...] = partner // 128
        partner_lane[...] = partner % 128

    pltpu.make_async_copy(rhs.at[0 : levels - 1], rhs.at[0 : levels - 1], there_recv).wait()
    reduced = jnp.zeros((ROWS, part), f32)
    for level in range(levels):
        reduced = rhs[level] * inverse[level] + below[level] * reduced
        solved[level] = reduced
    value = jnp.zeros((ROWS, part), f32)
    for level in reversed(range(levels)):
        value = solved[level] - upper[level] * value
        solved[level] = value

    my_columns = pl.multiple_of(lev * part, part)

    for d in reversed(range(1, levels)):
        pltpu.make_async_remote_copy(
            src_ref=solved.at[peers[d]],
            dst_ref=field.at[OWN, pl.ds(my_columns, part)],
            send_sem=back_send,
            recv_sem=back_recv.at[d],
            device_id={"lev": peers[d]},
            device_id_type=MESH,
        ).start()
    field[OWN, pl.ds(my_columns, part)] = solved[lev]
    for d in range(1, levels):
        at = pl.multiple_of(peers[d] * part, part)
        here = field.at[OWN, pl.ds(at, part)]
        pltpu.make_async_copy(here, here, back_recv.at[d]).wait()
        if d % 2 == 1:
            at = pl.multiple_of(peers[d] // 2 * (2 * part), 2 * part)
            halo_copies(field, halo_send, halo_recv, at, 2 * part)

    def fold(buffer, last_row, folded):
        def repeat(block, carry):
            at = pl.multiple_of(PAD + block * 128, 128)
            lines[block] = jnp.broadcast_to(buffer[last_row : last_row + 1, pl.ds(at, 128)], (8, 128))
            return carry

        lax.fori_loop(0, blocks, repeat, 0, unroll=True)
        for q in range(blocks // 8):
            rows = slice(8 * q, 8 * q + 8)
            at_lane, at_row = partner_lane[rows, :], partner_row[rows, :]

            def pick(block, now, at_lane=at_lane, at_row=at_row):
                moved = jnp.take_along_axis(lines[block], at_lane, axis=1, mode="promise_in_bounds")
                return jnp.where(at_row == block, moved, now)

            folded[rows, :] = lax.fori_loop(0, blocks, pick, jnp.zeros((8, 128), f32), unroll=True)

    is_top = tile == top

    first, second = ROUNDS
    halo_wait(quarter_mask, mask_recv, True)

    def pack_mask(block, carry):
        at = pl.multiple_of(block * 128, 128)
        packed_mask[:, pl.ds(at, 128)] = packed(quarter_mask[0:24, pl.ds(at, 128)])
        return carry

    lax.fori_loop(0, blocks, pack_mask, 0, unroll=8)
    halo_wait(field, halo_recv, True)

    def apply_mask(block, carry):
        at = pl.multiple_of(block * 128, 128)
        masked[:, pl.ds(at + PAD, 128)] = (4.0 * quarter_mask[:, pl.ds(at, 128)]) * field[:, pl.ds(at, 128)]
        return carry

    lax.fori_loop(0, blocks, apply_mask, 0, unroll=8)
    wrap(masked, 32, columns)
    source = masked
    for j in range(first):
        if j < 2:

            @pl.when(tile == top - 1)
            def _(source=source):
                fold(source, 23, folded_p)
                for block in range(blocks):
                    at = PAD + block * 128
                    source[24:25, at : at + 128] = folded_p[block : block + 1, :]

        @pl.when(is_top)
        def _(source=source, j=j):
            fold(source, 15, folded_p)
            rows, loaded = 32 if j == 0 else 16, 32 if j < 2 else 16
            operator(source, v_chain[j], quarter_mask, columns, SHIFTS[j], rows, loaded, folded=(folded_p, 15))

        @pl.when(jnp.logical_not(is_top))
        def _(source=source, j=j):
            rows, loaded = 32 if j == 0 else 24, 32 if j < 2 else 24
            operator(source, v_chain[j], quarter_mask, columns, SHIFTS[j], rows, loaded)

        source = v_chain[j]

    def of(buffer, rows, pad):
        return lambda block: buffer[rows, pl.ds(pl.multiple_of(block * 128 + pad, 128), 128)]

    def reduce_over_tiles(index):
        def send(d, carry):
            pltpu.make_async_remote_copy(
                src_ref=message.at[index],
                dst_ref=received.at[index, tile],
                send_sem=sum_send.at[index],
                recv_sem=sum_recv.at[index],
                device_id={"tile": lax.rem(tile + d, tiles)},
                device_id_type=MESH,
            ).start()
            return carry

        lax.fori_loop(1, tiles, send, 0, unroll=True)

    def sum_over_tiles(index):
        others = received.at[index, 0 : tiles - 1]
        pltpu.make_async_copy(others, others, sum_recv.at[index]).wait()
        return jnp.sum(received[index], axis=0)

    shared = gram_message([of(field, OWN, 0)] + [of(v, OWN, PAD) for v in v_chain], columns)
    message[0] = shared
    received[0, tile] = shared
    reduce_over_tiles(0)
    diffusivity = h_diffusivity[0, 0]
    x_first, r_next, d_next = coefficient_cg(sum_over_tiles(0), (first + 1,), diffusivity, first, False)

    def next_round(block, carry):
        at = pl.multiple_of(block * 128, 128)
        rows = slice(0, 24)
        held = [field[rows, pl.ds(at, 128)]] + [v[rows, pl.ds(at + PAD, 128)] for v in v_chain]
        mask = 4.0 * quarter_mask[rows, pl.ds(at, 128)]
        for masked_one, own, numbers in ((masked_r, r_own, r_next), (masked_p, p_own, d_next)):
            tall = [jnp.concatenate([numbers[j]] * 3, axis=0) for j in numbers]
            value = tree_sum(number * held[j] for number, j in zip(tall, numbers))
            masked_one[:, pl.ds(at + PAD, 128)] = mask * value
            own[:, pl.ds(at, 128)] = value[8:16]
        return carry

    lax.fori_loop(0, blocks, next_round, 0, unroll=8)
    wrap(masked_r, 24, columns)
    wrap(masked_p, 24, columns)

    p_source, r_source = masked_p, masked_r
    for j in range(second):
        work = [(p_source, p_chain[j], folded_p, 8 if j == second - 1 else 16)]
        if j < second - 1:
            work.append((r_source, r_chain[j], folded_r, 8 if j == second - 2 else 16))

        def both(work, j, at_top):
            if at_top:
                for source, _, folded, _ in work:
                    fold(source, 15 if j == 0 else 7, folded)
            for source, target, folded, rows in work:
                operator(
                    source, target, packed_mask, columns, SHIFTS[j], rows, 24 if j == 0 else 16,
                    pack=j == 0, folded=(folded, 7) if at_top else None,
                )

        pl.when(is_top)(functools.partial(both, work, j, True))
        pl.when(jnp.logical_not(is_top))(functools.partial(both, work, j, False))
        if j < second - 1:
            p_source, r_source = p_chain[j], r_chain[j]
    strip_rows = slice(0, 8)
    p_basis = [of(p_own, strip_rows, 0)] + [of(p, strip_rows, PAD) for p in p_chain]
    r_basis = [of(r_own, strip_rows, 0)] + [of(r, strip_rows, PAD) for r in r_chain]
    shared = gram_message(p_basis + r_basis, columns)
    message[1] = shared
    received[1, tile] = shared
    reduce_over_tiles(1)
    v_basis = [of(field, OWN, 0)] + [of(v, OWN, PAD) for v in v_chain]

    def part_one(block, carry):
        at = pl.multiple_of(block * 128, 128)
        result[:, pl.ds(at, 128)] = tree_sum(x_first[j] * v_basis[j](block) for j in x_first)
        return carry

    lax.fori_loop(0, blocks, part_one, 0, unroll=8)
    x_second, _, _ = coefficient_cg(sum_over_tiles(1), (second + 1, second), diffusivity, second, True)

    basis = p_basis + r_basis
    pieces = 4
    width = columns // pieces
    for piece in range(pieces):

        def part_two(block, carry, piece=piece):
            block = block + piece * (width // 128)
            at = pl.multiple_of(block * 128, 128)
            result[:, pl.ds(at, 128)] += tree_sum(x_second[j] * basis[j](block) for j in x_second)
            return carry

        lax.fori_loop(0, width // 128, part_two, 0, unroll=True)
        here = slice(piece * width, piece * width + width)
        pltpu.make_async_remote_copy(
            src_ref=result.at[:, here],
            dst_ref=other_out.at[:, here],
            send_sem=last_send,
            recv_sem=last_recv,
            device_id={"var": 1 - var},
            device_id_type=MESH,
        ).start()
    keep = pltpu.make_async_copy(result, solved_out, last_local)
    keep.start()

    def sent(buffer, sem):
        pltpu.make_async_copy(buffer, buffer, sem).wait()

    sent(rhs.at[0 : levels - 1], there_send)
    sent(rhs.at[0 : levels - 1], back_send)
    halo_wait(quarter_mask, mask_send, False)
    halo_wait(field, halo_send, False)
    for index in range(2):
        sent(received.at[index, 0 : tiles - 1], sum_send.at[index])
    keep.wait()
    sent(result, last_send)
    pltpu.make_async_copy(other_out, other_out, last_recv).wait()


def per_device(
    background, norm_factor, v_diffusivity, h_diffusivity, sea_mask, fold_order, coupling
):
    rows, columns = background.shape[2:]
    levels, tiles = lax.axis_size("lev"), lax.axis_size("tile")
    part = columns // levels
    f32 = jnp.float32
    strip = jax.ShapeDtypeStruct((rows, columns), f32)
    vmem = pltpu.VMEM
    tall = vmem((32, columns), f32)

    def padded(height):
        return vmem((height, columns + 2 * PAD), f32)

    first, second = ROUNDS
    blocks = columns // 128
    dma = pltpu.SemaphoreType.DMA
    in_hbm = functools.partial(pltpu.with_memory_space_constraint, memory_space=pltpu.HBM)
    solved, other = pl.pallas_call(
        kernel,
        out_shape=(strip, strip),
        in_specs=[pl.BlockSpec(memory_space=pl.ANY)] * 3
        + [pl.BlockSpec(memory_space=pltpu.SMEM)]
        + [pl.BlockSpec(memory_space=pl.ANY)] * 2,
        out_specs=(pl.BlockSpec(memory_space=pl.ANY),) * 2,
        scratch_shapes=[
            vmem((rows, columns), f32),
            vmem((rows, columns), f32),
            vmem((levels, rows, part), f32),
            vmem((rows, columns), jnp.int32),
            vmem((1, columns), jnp.int32),
            vmem((rows, columns), f32),
            vmem((levels, rows, part), f32),
            vmem((levels, rows, part), f32),
            vmem((levels, rows, part), f32),
            vmem((levels, rows, part), f32),
            vmem((levels, rows, part), f32),
            tall,
            tall,
            vmem((16, columns), f32),
            padded(32),
            [padded(32 if j == 0 else 24) for j in range(first)],
            [padded(16)] * second,
            [padded(16)] * (second - 1),
            padded(24),
            padded(24),
            vmem((rows, columns), f32),
            vmem((rows, columns), f32),
            vmem((blocks, 128), jnp.int32),
            vmem((blocks, 128), jnp.int32),
            vmem((blocks, 8, 128), f32),
            vmem((blocks, 128), f32),
            vmem((blocks, 128), f32),
            vmem((2, 1, 128), f32),
            vmem((2, tiles, 1, 128), f32),
            vmem((rows, columns), f32),
            dma((5,)),
            dma,
            dma,
            dma,
            dma((levels,)),
            dma((4,)),
            dma((4,)),
            dma((4,)),
            dma((4,)),
            dma((2,)),
            dma((2,)),
            dma,
            dma,
            dma,
        ],
        compiler_params=pltpu.CompilerParams(
            collective_id=0, has_side_effects=True, vmem_limit_bytes=40 * 2**20
        ),
    )(
        in_hbm(background.reshape(rows, columns)),
        in_hbm(norm_factor.reshape(rows, columns)),
        in_hbm(v_diffusivity.reshape(levels, rows, part)),
        h_diffusivity,
        in_hbm(sea_mask.reshape(rows, columns)),
        in_hbm(fold_order.reshape(1, columns)),
    )
    return (solved + coupling[0, 0] * other)[None, None]


def solution(mesh):
    placed = (
        P("var", "lev", "tile", None),
        P("var", "lev", "tile", None),
        P("var", None, "tile", "lev"),
        P("var", "lev"),
        P("lev", "tile", None),
        P(),
        P("var", "lev", "tile", None),
    )
    return jax.shard_map(
        per_device,
        mesh=mesh,
        in_specs=placed,
        out_specs=P("var", "lev", "tile", None),
        check_vma=False,
    )
```

```python
import functools

import jax
import jax.numpy as jnp
from jax import lax
from jax.experimental import pallas as pl
from jax.experimental.pallas import tpu as pltpu
from jax.sharding import PartitionSpec as P

MESH = pl.DeviceIdType.MESH
ROUNDS = (5, 5)
SHIFTS = (0.0, 5.0, 2.0, 7.0, 0.5)
ROWS = 8
PAD = 128
OWN = slice(8, 16)


def tree_sum(terms):
    terms = list(terms)
    while len(terms) > 1:
        terms = [sum(terms[i : i + 2]) for i in range(0, len(terms), 2)]
    return terms[0]


def pairs_of(count):
    return [(i, j) for i in range(count) for j in range(i, count)]


def gram_message(vectors, columns):
    pairs = pairs_of(len(vectors))
    lane = lax.broadcasted_iota(jnp.int32, (8, 128), 1)
    message = jnp.zeros((8, 128), jnp.float32)
    for at in range(0, len(pairs), 28):
        group = pairs[at : at + 28]
        used = sorted({i for pair in group for i in pair})

        def body(block, sums, group=group, used=used):
            held = {i: vectors[i](block) for i in used}
            return tuple(total + held[i] * held[j] for total, (i, j) in zip(sums, group))

        zeros = tuple(jnp.zeros((8, 128), jnp.float32) for _ in group)
        sums = lax.fori_loop(0, columns // 128, body, zeros, unroll=8)
        for place, total in enumerate(sums):
            message = jnp.where(lane == at + place, jnp.sum(total, axis=1, keepdims=True), message)
    return jnp.sum(message, axis=0, keepdims=True)


def coefficient_cg(totals, chains, diffusivity, steps, last):
    count = sum(chains)
    first = count - chains[-1]
    totals = jnp.broadcast_to(totals, (8, 128))
    gram = {}
    for place, (i, j) in enumerate(pairs_of(count)):
        gram[i, j] = gram[j, i] = jnp.broadcast_to(totals[:, place : place + 1], (8, 128))
    same, start = {}, 0
    for length in chains:
        for j in range(length - 1):
            same[start + j] = 1.0 + diffusivity * SHIFTS[j]
        start += length
    up = 4.0 * diffusivity

    def image_of(d):
        parts = {}
        for j, value in d.items():
            parts.setdefault(j, []).append(same[j] * value)
            parts.setdefault(j + 1, []).append(up * value)
        return {j: sum(terms) for j, terms in sorted(parts.items())}

    def product(u, v):
        return tree_sum(u[i] * tree_sum(gram[i, j] * v[j] for j in v) for i in u)

    def add(u, factor, v):
        return {j: (u[j] if j in u else 0.0) + (factor * v[j] if j in v else 0.0) for j in sorted({*u, *v})}

    d, r, x = {0: 1.0}, {first: 1.0}, {}
    norm_now = gram[first, first]
    for step in range(steps):
        image = image_of(d)
        energy = product(d, image)
        size = jnp.where(energy > 0, jnp.minimum(norm_now / energy, 1.0), 0.0)
        x = add(x, size, d)
        if last and step == steps - 1:
            break
        r = add(r, -size, image)
        norm_next = jnp.maximum(product(r, r), 0.0)
        d = add(r, jnp.where(norm_now > 0, norm_next / norm_now, 0.0), d)
        norm_now = norm_next
    return x, r, d


def packed(tall):
    upper_half = lax.broadcasted_iota(jnp.int32, (8, 128), 0) < 4
    return jnp.concatenate([tall[8:16], jnp.where(upper_half, tall[16:24], tall[0:8])], axis=0)


def operator(source, target, quarter_mask, columns, shift, rows, loaded, pack=False, folded=None, group=8):
    lane = lax.broadcasted_iota(jnp.int32, (rows, 128), 1)
    if folded is not None:
        line, last_row = folded
        is_last = lax.broadcasted_iota(jnp.int32, (rows, 128), 0) == last_row
    cut = packed if pack else lambda value: value[0:rows]

    def body(chunk, carry):
        at = pl.multiple_of(chunk * (group * 128), 128)
        held, ahead, behind = {}, {}, {}
        for k in range(group + 2):
            held[k] = source[0:loaded, pl.ds(at + 128 * k, 128)]
            ahead[k] = pltpu.roll(cut(held[k]), 127, 1)
            behind[k] = pltpu.roll(cut(held[k]), 1, 1)
            if k < 2:
                continue
            here = held[k - 1]
            east = jnp.where(lane == 127, ahead[k], ahead[k - 1])
            west = jnp.where(lane == 0, behind[k - 2], behind[k - 1])
            north = cut(pltpu.roll(here, loaded - 1, 0))
            south = cut(pltpu.roll(here, 1, 0))
            if folded is not None:
                north = jnp.where(is_last, line[pl.ds(chunk * group + k - 2, 1), :], north)
            here = cut(here)
            value = 4.0 * here - ((north + south) + (east + west))
            value = quarter_mask[0:rows, pl.ds(at + 128 * (k - 2), 128)] * value
            if shift:
                value = value - (0.25 * shift) * here
            target[0:rows, pl.ds(at + 128 * (k - 1), 128)] = value
        return carry

    lax.fori_loop(0, columns // (group * 128), body, 0)
    wrap(target, rows, columns)


def wrap(target, rows, columns):
    target[0:rows, 0:PAD] = target[0:rows, columns : columns + PAD]
    target[0:rows, columns + PAD : columns + 2 * PAD] = target[0:rows, PAD : 2 * PAD]


def kernel(
    background, norm_factor, v_diffusivity, h_diffusivity, sea_mask, fold_order,
    solved_out, other_out,
    bg, nf, vd, mask_in, fold_in, scaled, rhs, solved, inverse, below, upper,
    field, quarter_mask, packed_mask, masked, v_chain, p_chain, r_chain, masked_p, masked_r, p_own, r_own,
    partner_row, partner_lane, lines, folded_p, folded_r, message, received, result,
    load_sem, there_send, there_recv, back_send, back_recv,
    halo_send, halo_recv, mask_send, mask_recv, sum_send, sum_recv, last_send, last_recv, last_local,
):
    tile, lev, var = (lax.axis_index(a) for a in ("tile", "lev", "var"))
    tiles, levels = lax.axis_size("tile"), lax.axis_size("lev")
    columns = bg.shape[1]
    part = columns // levels
    top = tiles - 1
    blocks = columns // 128
    f32 = jnp.float32

    loads = [
        pltpu.make_async_copy(source, target, load_sem.at[i])
        for i, (source, target) in enumerate(
            ((background, bg), (norm_factor, nf), (sea_mask, mask_in), (v_diffusivity, vd), (fold_order, fold_in))
        )
    ]
    for load in loads:
        load.start()
    barrier = pltpu.get_barrier_semaphore()
    bits = (lax.rem(lev, 2), lax.rem(lev // 2, 2), lev // 4)

    def peer_level(d):
        return sum(
            (1 - bit if d >> place & 1 else bit) * (1 << place) for place, bit in enumerate(bits)
        )

    peers = [peer_level(d) for d in range(levels)]

    def greet_tile(d, carry):
        pl.semaphore_signal(barrier, inc=1, device_id={"tile": lax.rem(tile + d, tiles)}, device_id_type=MESH)
        return carry

    for d in range(1, levels):
        pl.semaphore_signal(barrier, inc=1, device_id={"lev": peers[d]}, device_id_type=MESH)
    pl.semaphore_signal(barrier, inc=1, device_id={"var": 1 - var}, device_id_type=MESH)
    lax.fori_loop(1, tiles, greet_tile, 0, unroll=True)
    loads[0].wait()
    loads[1].wait()
    scaled[...] = nf[...] * bg[...]
    loads[2].wait()
    quarter_mask[OWN, :] = 0.25 * mask_in[...].astype(f32)
    pl.semaphore_wait(barrier, (levels - 1) + (tiles - 1) + 1)

    for d in reversed(range(1, levels)):
        pltpu.make_async_remote_copy(
            src_ref=scaled.at[:, pl.ds(pl.multiple_of(peers[d] * part, part), part)],
            dst_ref=rhs.at[lev],
            send_sem=there_send,
            recv_sem=there_recv,
            device_id={"lev": peers[d]},
            device_id_type=MESH,
        ).start()
    rhs[lev] = scaled[:, pl.ds(pl.multiple_of(lev * part, part), part)]

    sides = ((8, 16, 0, 1), (8, 16, 16, -1), (14, 16, 30, 2), (8, 10, 24, -2))

    def reached(distance):
        return tile + distance <= top if distance > 0 else tile + distance >= 0

    def halo_copies(buffer, send, recv, at, width):
        for side, (low, high, land, distance) in enumerate(sides):

            @pl.when(reached(distance))
            def _(side=side, low=low, high=high, land=land, distance=distance):
                pltpu.make_async_remote_copy(
                    src_ref=buffer.at[low:high, pl.ds(at, width)],
                    dst_ref=buffer.at[land : land + high - low, pl.ds(at, width)],
                    send_sem=send.at[side],
                    recv_sem=recv.at[side],
                    device_id={"tile": tile + distance},
                    device_id_type=MESH,
                ).start()

    def halo_wait(buffer, sem, receive):
        for side, (low, high, land, distance) in enumerate(sides):

            @pl.when(reached(-distance if receive else distance))
            def _(side=side, low=low, high=high, land=land):
                at = slice(land, land + high - low) if receive else slice(low, high)
                pltpu.make_async_copy(buffer.at[at, :], buffer.at[at, :], sem.at[side]).wait()

    halo_copies(quarter_mask, mask_send, mask_recv, 0, columns)
    for low, high, land, distance in sides:

        @pl.when(jnp.logical_not(reached(-distance)))
        def _(land=land, rows=high - low):
            for buffer in (field, quarter_mask):
                buffer[land : land + rows, :] = jnp.zeros((rows, columns), f32)

    @pl.when(tile == top)
    def _():
        for chain in v_chain[1:]:
            chain[16:24, :] = jnp.zeros((8, chain.shape[1]), f32)

    loads[3].wait()
    above = jnp.zeros((ROWS, part), f32)
    upper_now = above
    for level in range(levels):
        coefficient = vd[level]
        inv = 1.0 / (1.0 + above + coefficient + above * upper_now)
        inverse[level] = inv
        below[level] = above * inv
        upper_now = -coefficient * inv
        upper[level] = upper_now
        above = coefficient

    loads[4].wait()

    @pl.when(tile >= top - 1)
    def _():
        order = fold_in[...]
        lane = lax.broadcasted_iota(jnp.int32, (1, columns), 1)
        mate = jnp.where(lane % 2 == 0, pltpu.roll(order, columns - 1, 1), pltpu.roll(order, 1, 1))
        row_hot = lax.broadcasted_iota(jnp.int32, (blocks, columns), 0) == order // 128
        lane_hot = lax.broadcasted_iota(jnp.int32, (128, columns), 0) == order % 128
        high = jnp.where(row_hot, (mate // 64).astype(f32), 0.0)
        low = jnp.where(row_hot, (mate % 64).astype(f32), 0.0)
        left = jnp.concatenate([high, low], axis=0).astype(jnp.bfloat16)
        right = jnp.where(lane_hot, 1.0, 0.0).astype(jnp.bfloat16)
        found = lax.dot_general(left, right, (((1,), (1,)), ((), ())), preferred_element_type=f32)
        partner = 64 * found[:blocks].astype(jnp.int32) + found[blocks:].astype(jnp.int32)
        partner_row[...] = partner // 128
        partner_lane[...] = partner % 128

    pltpu.make_async_copy(rhs.at[0 : levels - 1], rhs.at[0 : levels - 1], there_recv).wait()
    reduced = jnp.zeros((ROWS, part), f32)
    for level in range(levels):
        reduced = rhs[level] * inverse[level] + below[level] * reduced
        solved[level] = reduced
    value = jnp.zeros((ROWS, part), f32)
    for level in reversed(range(levels)):
        value = solved[level] - upper[level] * value
        solved[level] = value

    my_columns = pl.multiple_of(lev * part, part)

    for d in reversed(range(1, levels)):
        pltpu.make_async_remote_copy(
            src_ref=solved.at[peers[d]],
            dst_ref=field.at[OWN, pl.ds(my_columns, part)],
            send_sem=back_send,
            recv_sem=back_recv.at[d],
            device_id={"lev": peers[d]},
            device_id_type=MESH,
        ).start()
    field[OWN, pl.ds(my_columns, part)] = solved[lev]
    for d in range(1, levels):
        at = pl.multiple_of(peers[d] * part, part)
        here = field.at[OWN, pl.ds(at, part)]
        pltpu.make_async_copy(here, here, back_recv.at[d]).wait()
        if d % 2 == 1:
            at = pl.multiple_of(peers[d] // 2 * (2 * part), 2 * part)
            halo_copies(field, halo_send, halo_recv, at, 2 * part)

    def fold(buffer, last_row, folded):
        def repeat(block, carry):
            at = pl.multiple_of(PAD + block * 128, 128)
            lines[block] = jnp.broadcast_to(buffer[last_row : last_row + 1, pl.ds(at, 128)], (8, 128))
            return carry

        lax.fori_loop(0, blocks, repeat, 0, unroll=True)
        for q in range(blocks // 8):
            rows = slice(8 * q, 8 * q + 8)
            at_lane, at_row = partner_lane[rows, :], partner_row[rows, :]

            def pick(block, now, at_lane=at_lane, at_row=at_row):
                moved = jnp.take_along_axis(lines[block], at_lane, axis=1, mode="promise_in_bounds")
                return jnp.where(at_row == block, moved, now)

            folded[rows, :] = lax.fori_loop(0, blocks, pick, jnp.zeros((8, 128), f32), unroll=True)

    is_top = tile == top

    first, second = ROUNDS
    halo_wait(quarter_mask, mask_recv, True)

    def pack_mask(block, carry):
        at = pl.multiple_of(block * 128, 128)
        packed_mask[:, pl.ds(at, 128)] = packed(quarter_mask[0:24, pl.ds(at, 128)])
        return carry

    lax.fori_loop(0, blocks, pack_mask, 0, unroll=8)
    halo_wait(field, halo_recv, True)

    def apply_mask(block, carry):
        at = pl.multiple_of(block * 128, 128)
        masked[:, pl.ds(at + PAD, 128)] = (4.0 * quarter_mask[:, pl.ds(at, 128)]) * field[:, pl.ds(at, 128)]
        return carry

    lax.fori_loop(0, blocks, apply_mask, 0, unroll=8)
    wrap(masked, 32, columns)
    source = masked
    for j in range(first):
        if j < 2:

            @pl.when(tile == top - 1)
            def _(source=source):
                fold(source, 23, folded_p)
                for block in range(blocks):
                    at = PAD + block * 128
                    source[24:25, at : at + 128] = folded_p[block : block + 1, :]

        @pl.when(is_top)
        def _(source=source, j=j):
            fold(source, 15, folded_p)
            rows, loaded = 32 if j == 0 else 16, 32 if j < 2 else 16
            operator(source, v_chain[j], quarter_mask, columns, SHIFTS[j], rows, loaded, folded=(folded_p, 15))

        @pl.when(jnp.logical_not(is_top))
        def _(source=source, j=j):
            rows, loaded = 32 if j == 0 else 24, 32 if j < 2 else 24
            operator(source, v_chain[j], quarter_mask, columns, SHIFTS[j], rows, loaded)

        source = v_chain[j]

    def of(buffer, rows, pad):
        return lambda block: buffer[rows, pl.ds(pl.multiple_of(block * 128 + pad, 128), 128)]

    def reduce_over_tiles(index):
        def send(d, carry):
            pltpu.make_async_remote_copy(
                src_ref=message.at[index],
                dst_ref=received.at[index, tile],
                send_sem=sum_send.at[index],
                recv_sem=sum_recv.at[index],
                device_id={"tile": lax.rem(tile + d, tiles)},
                device_id_type=MESH,
            ).start()
            return carry

        lax.fori_loop(1, tiles, send, 0, unroll=True)

    def sum_over_tiles(index):
        others = received.at[index, 0 : tiles - 1]
        pltpu.make_async_copy(others, others, sum_recv.at[index]).wait()
        return jnp.sum(received[index], axis=0)

    shared = gram_message([of(field, OWN, 0)] + [of(v, OWN, PAD) for v in v_chain], columns)
    message[0] = shared
    received[0, tile] = shared
    reduce_over_tiles(0)
    diffusivity = h_diffusivity[0, 0]
    x_first, r_next, d_next = coefficient_cg(sum_over_tiles(0), (first + 1,), diffusivity, first, False)

    def next_round(block, carry):
        at = pl.multiple_of(block * 128, 128)
        rows = slice(0, 24)
        held = [field[rows, pl.ds(at, 128)]] + [v[rows, pl.ds(at + PAD, 128)] for v in v_chain]
        mask = 4.0 * quarter_mask[rows, pl.ds(at, 128)]
        for masked_one, own, numbers in ((masked_r, r_own, r_next), (masked_p, p_own, d_next)):
            tall = [jnp.concatenate([numbers[j]] * 3, axis=0) for j in numbers]
            value = tree_sum(number * held[j] for number, j in zip(tall, numbers))
            masked_one[:, pl.ds(at + PAD, 128)] = mask * value
            own[:, pl.ds(at, 128)] = value[8:16]
        return carry

    lax.fori_loop(0, blocks, next_round, 0, unroll=8)
    wrap(masked_r, 24, columns)
    wrap(masked_p, 24, columns)

    p_source, r_source = masked_p, masked_r
    for j in range(second):
        work = [(p_source, p_chain[j], folded_p, 8 if j == second - 1 else 16)]
        if j < second - 1:
            work.append((r_source, r_chain[j], folded_r, 8 if j == second - 2 else 16))

        def both(work, j, at_top):
            if at_top:
                for source, _, folded, _ in work:
                    fold(source, 15 if j == 0 else 7, folded)
            for source, target, folded, rows in work:
                operator(
                    source, target, packed_mask, columns, SHIFTS[j], rows, 24 if j == 0 else 16,
                    pack=j == 0, folded=(folded, 7) if at_top else None,
                )

        pl.when(is_top)(functools.partial(both, work, j, True))
        pl.when(jnp.logical_not(is_top))(functools.partial(both, work, j, False))
        if j < second - 1:
            p_source, r_source = p_chain[j], r_chain[j]
    strip_rows = slice(0, 8)
    p_basis = [of(p_own, strip_rows, 0)] + [of(p, strip_rows, PAD) for p in p_chain]
    r_basis = [of(r_own, strip_rows, 0)] + [of(r, strip_rows, PAD) for r in r_chain]
    shared = gram_message(p_basis + r_basis, columns)
    message[1] = shared
    received[1, tile] = shared
    reduce_over_tiles(1)
    v_basis = [of(field, OWN, 0)] + [of(v, OWN, PAD) for v in v_chain]

    def part_one(block, carry):
        at = pl.multiple_of(block * 128, 128)
        result[:, pl.ds(at, 128)] = tree_sum(x_first[j] * v_basis[j](block) for j in x_first)
        return carry

    lax.fori_loop(0, blocks, part_one, 0, unroll=8)
    x_second, _, _ = coefficient_cg(sum_over_tiles(1), (second + 1, second), diffusivity, second, True)

    basis = p_basis + r_basis
    pieces = 4
    width = columns // pieces
    for piece in range(pieces):

        def part_two(block, carry, piece=piece):
            block = block + piece * (width // 128)
            at = pl.multiple_of(block * 128, 128)
            result[:, pl.ds(at, 128)] += tree_sum(x_second[j] * basis[j](block) for j in x_second)
            return carry

        lax.fori_loop(0, width // 128, part_two, 0, unroll=True)
        here = slice(piece * width, piece * width + width)
        pltpu.make_async_remote_copy(
            src_ref=result.at[:, here],
            dst_ref=other_out.at[:, here],
            send_sem=last_send,
            recv_sem=last_recv,
            device_id={"var": 1 - var},
            device_id_type=MESH,
        ).start()
    keep = pltpu.make_async_copy(result, solved_out, last_local)
    keep.start()

    def sent(buffer, sem):
        pltpu.make_async_copy(buffer, buffer, sem).wait()

    sent(rhs.at[0 : levels - 1], there_send)
    sent(rhs.at[0 : levels - 1], back_send)
    halo_wait(quarter_mask, mask_send, False)
    halo_wait(field, halo_send, False)
    for index in range(2):
        sent(received.at[index, 0 : tiles - 1], sum_send.at[index])
    keep.wait()
    sent(result, last_send)
    pltpu.make_async_copy(other_out, other_out, last_recv).wait()


def per_device(
    background, norm_factor, v_diffusivity, h_diffusivity, sea_mask, fold_order, coupling
):
    rows, columns = background.shape[2:]
    levels, tiles = lax.axis_size("lev"), lax.axis_size("tile")
    part = columns // levels
    f32 = jnp.float32
    strip = jax.ShapeDtypeStruct((rows, columns), f32)
    vmem = pltpu.VMEM
    tall = vmem((32, columns), f32)

    def padded(height):
        return vmem((height, columns + 2 * PAD), f32)

    first, second = ROUNDS
    blocks = columns // 128
    dma = pltpu.SemaphoreType.DMA
    in_hbm = functools.partial(pltpu.with_memory_space_constraint, memory_space=pltpu.HBM)
    solved, other = pl.pallas_call(
        kernel,
        out_shape=(strip, strip),
        in_specs=[pl.BlockSpec(memory_space=pl.ANY)] * 3
        + [pl.BlockSpec(memory_space=pltpu.SMEM)]
        + [pl.BlockSpec(memory_space=pl.ANY)] * 2,
        out_specs=(pl.BlockSpec(memory_space=pl.ANY),) * 2,
        scratch_shapes=[
            vmem((rows, columns), f32),
            vmem((rows, columns), f32),
            vmem((levels, rows, part), f32),
            vmem((rows, columns), jnp.int32),
            vmem((1, columns), jnp.int32),
            vmem((rows, columns), f32),
            vmem((levels, rows, part), f32),
            vmem((levels, rows, part), f32),
            vmem((levels, rows, part), f32),
            vmem((levels, rows, part), f32),
            vmem((levels, rows, part), f32),
            tall,
            tall,
            vmem((16, columns), f32),
            padded(32),
            [padded(32 if j == 0 else 24) for j in range(first)],
            [padded(16)] * second,
            [padded(16)] * (second - 1),
            padded(24),
            padded(24),
            vmem((rows, columns), f32),
            vmem((rows, columns), f32),
            vmem((blocks, 128), jnp.int32),
            vmem((blocks, 128), jnp.int32),
            vmem((blocks, 8, 128), f32),
            vmem((blocks, 128), f32),
            vmem((blocks, 128), f32),
            vmem((2, 1, 128), f32),
            vmem((2, tiles, 1, 128), f32),
            vmem((rows, columns), f32),
            dma((5,)),
            dma,
            dma,
            dma,
            dma((levels,)),
            dma((4,)),
            dma((4,)),
            dma((4,)),
            dma((4,)),
            dma((2,)),
            dma((2,)),
            dma,
            dma,
            dma,
        ],
        compiler_params=pltpu.CompilerParams(
            collective_id=0, has_side_effects=True, vmem_limit_bytes=40 * 2**20
        ),
    )(
        in_hbm(background.reshape(rows, columns)),
        in_hbm(norm_factor.reshape(rows, columns)),
        in_hbm(v_diffusivity.reshape(levels, rows, part)),
        h_diffusivity,
        in_hbm(sea_mask.reshape(rows, columns)),
        in_hbm(fold_order.reshape(1, columns)),
    )
    return (solved + coupling[0, 0] * other)[None, None]


def solution(mesh):
    placed = (
        P("var", "lev", "tile", None),
        P("var", "lev", "tile", None),
        P("var", None, "tile", "lev"),
        P("var", "lev"),
        P("lev", "tile", None),
        P(),
        P("var", "lev", "tile", None),
    )
    return jax.shard_map(
        per_device,
        mesh=mesh,
        in_specs=placed,
        out_specs=P("var", "lev", "tile", None),
        check_vma=False,
    )
```

```python
import functools

import jax
import jax.numpy as jnp
from jax import lax
from jax.experimental import pallas as pl
from jax.experimental.pallas import tpu as pltpu
from jax.sharding import PartitionSpec as P

MESH = pl.DeviceIdType.MESH
ROUNDS = (5, 5)
SHIFTS = (0.0, 5.0, 2.0, 7.0, 0.5)
ROWS = 8
PAD = 128
OWN = slice(8, 16)


def tree_sum(terms):
    terms = list(terms)
    while len(terms) > 1:
        terms = [sum(terms[i : i + 2]) for i in range(0, len(terms), 2)]
    return terms[0]


def pairs_of(count):
    return [(i, j) for i in range(count) for j in range(i, count)]


def gram_message(vectors, columns):
    pairs = pairs_of(len(vectors))
    lane = lax.broadcasted_iota(jnp.int32, (8, 128), 1)
    message = jnp.zeros((8, 128), jnp.float32)
    for at in range(0, len(pairs), 28):
        group = pairs[at : at + 28]
        used = sorted({i for pair in group for i in pair})

        def body(block, sums, group=group, used=used):
            held = {i: vectors[i](block) for i in used}
            return tuple(total + held[i] * held[j] for total, (i, j) in zip(sums, group))

        zeros = tuple(jnp.zeros((8, 128), jnp.float32) for _ in group)
        sums = lax.fori_loop(0, columns // 128, body, zeros, unroll=True)
        for place, total in enumerate(sums):
            message = jnp.where(lane == at + place, jnp.sum(total, axis=1, keepdims=True), message)
    return jnp.sum(message, axis=0, keepdims=True)


def coefficient_cg(totals, chains, diffusivity, steps, last):
    count = sum(chains)
    first = count - chains[-1]
    totals = jnp.broadcast_to(totals, (8, 128))
    gram = {}
    for place, (i, j) in enumerate(pairs_of(count)):
        gram[i, j] = gram[j, i] = jnp.broadcast_to(totals[:, place : place + 1], (8, 128))
    same, start = {}, 0
    for length in chains:
        for j in range(length - 1):
            same[start + j] = 1.0 + diffusivity * SHIFTS[j]
        start += length
    up = 4.0 * diffusivity

    def image_of(d):
        parts = {}
        for j, value in d.items():
            parts.setdefault(j, []).append(same[j] * value)
            parts.setdefault(j + 1, []).append(up * value)
        return {j: sum(terms) for j, terms in sorted(parts.items())}

    def product(u, v):
        return tree_sum(u[i] * tree_sum(gram[i, j] * v[j] for j in v) for i in u)

    def add(u, factor, v):
        return {j: (u[j] if j in u else 0.0) + (factor * v[j] if j in v else 0.0) for j in sorted({*u, *v})}

    d, r, x = {0: 1.0}, {first: 1.0}, {}
    norm_now = gram[first, first]
    for step in range(steps):
        image = image_of(d)
        energy = product(d, image)
        size = jnp.where(energy > 0, jnp.minimum(norm_now / energy, 1.0), 0.0)
        x = add(x, size, d)
        if last and step == steps - 1:
            break
        r = add(r, -size, image)
        norm_next = jnp.maximum(product(r, r), 0.0)
        d = add(r, jnp.where(norm_now > 0, norm_next / norm_now, 0.0), d)
        norm_now = norm_next
    return x, r, d


def packed(tall):
    upper_half = lax.broadcasted_iota(jnp.int32, (8, 128), 0) < 4
    return jnp.concatenate([tall[8:16], jnp.where(upper_half, tall[16:24], tall[0:8])], axis=0)


def operator(source, target, quarter_mask, columns, shift, rows, loaded, pack=False, folded=None, group=8):
    lane = lax.broadcasted_iota(jnp.int32, (rows, 128), 1)
    if folded is not None:
        line, last_row = folded
        is_last = lax.broadcasted_iota(jnp.int32, (rows, 128), 0) == last_row
    cut = packed if pack else lambda value: value[0:rows]

    def body(chunk, carry):
        at = pl.multiple_of(chunk * (group * 128), 128)
        held, ahead, behind = {}, {}, {}
        for k in range(group + 2):
            held[k] = source[0:loaded, pl.ds(at + 128 * k, 128)]
            ahead[k] = pltpu.roll(cut(held[k]), 127, 1)
            behind[k] = pltpu.roll(cut(held[k]), 1, 1)
            if k < 2:
                continue
            here = held[k - 1]
            east = jnp.where(lane == 127, ahead[k], ahead[k - 1])
            west = jnp.where(lane == 0, behind[k - 2], behind[k - 1])
            north = cut(pltpu.roll(here, loaded - 1, 0))
            south = cut(pltpu.roll(here, 1, 0))
            if folded is not None:
                north = jnp.where(is_last, line[pl.ds(chunk * group + k - 2, 1), :], north)
            here = cut(here)
            value = 4.0 * here - ((north + south) + (east + west))
            value = quarter_mask[0:rows, pl.ds(at + 128 * (k - 2), 128)] * value
            if shift:
                value = value - (0.25 * shift) * here
            target[0:rows, pl.ds(at + 128 * (k - 1), 128)] = value
        return carry

    lax.fori_loop(0, columns // (group * 128), body, 0, unroll=True)
    wrap(target, rows, columns)


def wrap(target, rows, columns):
    target[0:rows, 0:PAD] = target[0:rows, columns : columns + PAD]
    target[0:rows, columns + PAD : columns + 2 * PAD] = target[0:rows, PAD : 2 * PAD]


def kernel(
    background, norm_factor, v_diffusivity, h_diffusivity, sea_mask, fold_order,
    solved_out, other_out,
    bg, nf, vd, mask_in, fold_in, scaled, rhs, solved, inverse, below, upper,
    field, quarter_mask, packed_mask, masked, v_chain, p_chain, r_chain, masked_p, masked_r, p_own, r_own,
    partner_row, partner_lane, lines, folded_p, folded_r, message, received, result,
    load_sem, there_send, there_recv, back_send, back_recv,
    halo_send, halo_recv, mask_send, mask_recv, sum_send, sum_recv, last_send, last_recv, last_local,
):
    tile, lev, var = (lax.axis_index(a) for a in ("tile", "lev", "var"))
    tiles, levels = lax.axis_size("tile"), lax.axis_size("lev")
    columns = bg.shape[1]
    part = columns // levels
    top = tiles - 1
    blocks = columns // 128
    f32 = jnp.float32

    loads = [
        pltpu.make_async_copy(source, target, load_sem.at[i])
        for i, (source, target) in enumerate(
            ((background, bg), (norm_factor, nf), (sea_mask, mask_in), (v_diffusivity, vd), (fold_order, fold_in))
        )
    ]
    for load in loads:
        load.start()
    barrier = pltpu.get_barrier_semaphore()
    bits = (lax.rem(lev, 2), lax.rem(lev // 2, 2), lev // 4)

    def peer_level(d):
        return sum(
            (1 - bit if d >> place & 1 else bit) * (1 << place) for place, bit in enumerate(bits)
        )

    peers = [peer_level(d) for d in range(levels)]

    def greet_tile(d, carry):
        pl.semaphore_signal(barrier, inc=1, device_id={"tile": lax.rem(tile + d, tiles)}, device_id_type=MESH)
        return carry

    for d in range(1, levels):
        pl.semaphore_signal(barrier, inc=1, device_id={"lev": peers[d]}, device_id_type=MESH)
    pl.semaphore_signal(barrier, inc=1, device_id={"var": 1 - var}, device_id_type=MESH)
    lax.fori_loop(1, tiles, greet_tile, 0, unroll=True)
    loads[0].wait()
    loads[1].wait()
    scaled[...] = nf[...] * bg[...]
    loads[2].wait()
    quarter_mask[OWN, :] = 0.25 * mask_in[...].astype(f32)
    pl.semaphore_wait(barrier, (levels - 1) + (tiles - 1) + 1)

    for d in reversed(range(1, levels)):
        pltpu.make_async_remote_copy(
            src_ref=scaled.at[:, pl.ds(pl.multiple_of(peers[d] * part, part), part)],
            dst_ref=rhs.at[lev],
            send_sem=there_send,
            recv_sem=there_recv,
            device_id={"lev": peers[d]},
            device_id_type=MESH,
        ).start()
    rhs[lev] = scaled[:, pl.ds(pl.multiple_of(lev * part, part), part)]

    sides = ((8, 16, 0, 1), (8, 16, 16, -1), (14, 16, 30, 2), (8, 10, 24, -2))

    def reached(distance):
        return tile + distance <= top if distance > 0 else tile + distance >= 0

    def halo_copies(buffer, send, recv, at, width):
        for side, (low, high, land, distance) in enumerate(sides):

            @pl.when(reached(distance))
            def _(side=side, low=low, high=high, land=land, distance=distance):
                pltpu.make_async_remote_copy(
                    src_ref=buffer.at[low:high, pl.ds(at, width)],
                    dst_ref=buffer.at[land : land + high - low, pl.ds(at, width)],
                    send_sem=send.at[side],
                    recv_sem=recv.at[side],
                    device_id={"tile": tile + distance},
                    device_id_type=MESH,
                ).start()

    def halo_wait(buffer, sem, receive):
        for side, (low, high, land, distance) in enumerate(sides):

            @pl.when(reached(-distance if receive else distance))
            def _(side=side, low=low, high=high, land=land):
                at = slice(land, land + high - low) if receive else slice(low, high)
                pltpu.make_async_copy(buffer.at[at, :], buffer.at[at, :], sem.at[side]).wait()

    halo_copies(quarter_mask, mask_send, mask_recv, 0, columns)
    for low, high, land, distance in sides:

        @pl.when(jnp.logical_not(reached(-distance)))
        def _(land=land, rows=high - low):
            for buffer in (field, quarter_mask):
                buffer[land : land + rows, :] = jnp.zeros((rows, columns), f32)

    @pl.when(tile == top)
    def _():
        for chain in v_chain[1:]:
            chain[16:24, :] = jnp.zeros((8, chain.shape[1]), f32)

    loads[3].wait()
    above = jnp.zeros((ROWS, part), f32)
    upper_now = above
    for level in range(levels):
        coefficient = vd[level]
        inv = 1.0 / (1.0 + above + coefficient + above * upper_now)
        inverse[level] = inv
        below[level] = above * inv
        upper_now = -coefficient * inv
        upper[level] = upper_now
        above = coefficient

    loads[4].wait()

    @pl.when(tile >= top - 1)
    def _():
        order = fold_in[...]
        lane = lax.broadcasted_iota(jnp.int32, (1, columns), 1)
        mate = jnp.where(lane % 2 == 0, pltpu.roll(order, columns - 1, 1), pltpu.roll(order, 1, 1))
        row_hot = lax.broadcasted_iota(jnp.int32, (blocks, columns), 0) == order // 128
        lane_hot = lax.broadcasted_iota(jnp.int32, (128, columns), 0) == order % 128
        high = jnp.where(row_hot, (mate // 64).astype(f32), 0.0)
        low = jnp.where(row_hot, (mate % 64).astype(f32), 0.0)
        left = jnp.concatenate([high, low], axis=0).astype(jnp.bfloat16)
        right = jnp.where(lane_hot, 1.0, 0.0).astype(jnp.bfloat16)
        found = lax.dot_general(left, right, (((1,), (1,)), ((), ())), preferred_element_type=f32)
        partner = 64 * found[:blocks].astype(jnp.int32) + found[blocks:].astype(jnp.int32)
        partner_row[...] = partner // 128
        partner_lane[...] = partner % 128

    pltpu.make_async_copy(rhs.at[0 : levels - 1], rhs.at[0 : levels - 1], there_recv).wait()
    reduced = jnp.zeros((ROWS, part), f32)
    for level in range(levels):
        reduced = rhs[level] * inverse[level] + below[level] * reduced
        solved[level] = reduced
    value = jnp.zeros((ROWS, part), f32)
    for level in reversed(range(levels)):
        value = solved[level] - upper[level] * value
        solved[level] = value

    my_columns = pl.multiple_of(lev * part, part)

    for d in reversed(range(1, levels)):
        pltpu.make_async_remote_copy(
            src_ref=solved.at[peers[d]],
            dst_ref=field.at[OWN, pl.ds(my_columns, part)],
            send_sem=back_send,
            recv_sem=back_recv.at[d],
            device_id={"lev": peers[d]},
            device_id_type=MESH,
        ).start()
    field[OWN, pl.ds(my_columns, part)] = solved[lev]
    for d in range(1, levels):
        at = pl.multiple_of(peers[d] * part, part)
        here = field.at[OWN, pl.ds(at, part)]
        pltpu.make_async_copy(here, here, back_recv.at[d]).wait()
        if d % 2 == 1:
            at = pl.multiple_of(peers[d] // 2 * (2 * part), 2 * part)
            halo_copies(field, halo_send, halo_recv, at, 2 * part)

    def fold(buffer, last_row, folded):
        def repeat(block, carry):
            at = pl.multiple_of(PAD + block * 128, 128)
            lines[block] = jnp.broadcast_to(buffer[last_row : last_row + 1, pl.ds(at, 128)], (8, 128))
            return carry

        lax.fori_loop(0, blocks, repeat, 0, unroll=True)
        for q in range(blocks // 8):
            rows = slice(8 * q, 8 * q + 8)
            at_lane, at_row = partner_lane[rows, :], partner_row[rows, :]

            def pick(block, now, at_lane=at_lane, at_row=at_row):
                moved = jnp.take_along_axis(lines[block], at_lane, axis=1, mode="promise_in_bounds")
                return jnp.where(at_row == block, moved, now)

            folded[rows, :] = lax.fori_loop(0, blocks, pick, jnp.zeros((8, 128), f32), unroll=True)

    is_top = tile == top

    first, second = ROUNDS
    halo_wait(quarter_mask, mask_recv, True)

    def pack_mask(block, carry):
        at = pl.multiple_of(block * 128, 128)
        packed_mask[:, pl.ds(at, 128)] = packed(quarter_mask[0:24, pl.ds(at, 128)])
        return carry

    lax.fori_loop(0, blocks, pack_mask, 0, unroll=True)
    halo_wait(field, halo_recv, True)

    def apply_mask(block, carry):
        at = pl.multiple_of(block * 128, 128)
        masked[:, pl.ds(at + PAD, 128)] = (4.0 * quarter_mask[:, pl.ds(at, 128)]) * field[:, pl.ds(at, 128)]
        return carry

    lax.fori_loop(0, blocks, apply_mask, 0, unroll=True)
    wrap(masked, 32, columns)
    def first_chain(strip):
        source = masked
        for j in range(first):
            folded, rows = None, 24
            if strip == "top":
                fold(source, 15, folded_p)
                folded, rows = (folded_p, 15), 16
            elif strip == "next" and j < 2:
                fold(source, 23, folded_p)
                for block in range(blocks):
                    at = PAD + block * 128
                    source[24:25, at : at + 128] = folded_p[block : block + 1, :]
            if j == 0:
                rows = 32
            operator(
                source, v_chain[j], quarter_mask, columns, SHIFTS[j], rows, 32 if j < 2 else rows, folded=folded
            )
            source = v_chain[j]
        message[0] = gram_message([of(field, OWN, 0)] + [of(v, OWN, PAD) for v in v_chain], columns)

    def of(buffer, rows, pad):
        return lambda block: buffer[rows, pl.ds(pl.multiple_of(block * 128 + pad, 128), 128)]

    def reduce_over_tiles(index):
        def send(d, carry):
            pltpu.make_async_remote_copy(
                src_ref=message.at[index],
                dst_ref=received.at[index, tile],
                send_sem=sum_send.at[index],
                recv_sem=sum_recv.at[index],
                device_id={"tile": lax.rem(tile + d, tiles)},
                device_id_type=MESH,
            ).start()
            return carry

        lax.fori_loop(1, tiles, send, 0, unroll=True)

    def sum_over_tiles(index):
        others = received.at[index, 0 : tiles - 1]
        pltpu.make_async_copy(others, others, sum_recv.at[index]).wait()
        return jnp.sum(received[index], axis=0)

    pl.when(is_top)(functools.partial(first_chain, "top"))
    pl.when(tile == top - 1)(functools.partial(first_chain, "next"))
    pl.when(tile < top - 1)(functools.partial(first_chain, "other"))
    received[0, tile] = message[0]
    reduce_over_tiles(0)
    diffusivity = h_diffusivity[0, 0]
    x_first, r_next, d_next = coefficient_cg(sum_over_tiles(0), (first + 1,), diffusivity, first, False)

    def next_round(block, carry):
        at = pl.multiple_of(block * 128, 128)
        rows = slice(0, 24)
        held = [field[rows, pl.ds(at, 128)]] + [v[rows, pl.ds(at + PAD, 128)] for v in v_chain]
        mask = 4.0 * quarter_mask[rows, pl.ds(at, 128)]
        for masked_one, own, numbers in ((masked_r, r_own, r_next), (masked_p, p_own, d_next)):
            tall = [jnp.concatenate([numbers[j]] * 3, axis=0) for j in numbers]
            value = tree_sum(number * held[j] for number, j in zip(tall, numbers))
            masked_one[:, pl.ds(at + PAD, 128)] = mask * value
            own[:, pl.ds(at, 128)] = value[8:16]
        return carry

    lax.fori_loop(0, blocks, next_round, 0, unroll=True)
    wrap(masked_r, 24, columns)
    wrap(masked_p, 24, columns)

    strip_rows = slice(0, 8)
    p_basis = [of(p_own, strip_rows, 0)] + [of(p, strip_rows, PAD) for p in p_chain]
    r_basis = [of(r_own, strip_rows, 0)] + [of(r, strip_rows, PAD) for r in r_chain]

    def second_chains(at_top):
        sources = [masked_p, masked_r]
        for j in range(second):
            work = [(sources[0], p_chain[j], folded_p, 8 if j == second - 1 else 16)]
            if j < second - 1:
                work.append((sources[1], r_chain[j], folded_r, 8 if j == second - 2 else 16))
            if at_top:
                for source, _, folded, _ in work:
                    fold(source, 15 if j == 0 else 7, folded)
            for source, target, folded, rows in work:
                operator(
                    source, target, packed_mask, columns, SHIFTS[j], rows, 24 if j == 0 else 16,
                    pack=j == 0, folded=(folded, 7) if at_top else None,
                )
            sources = [target for _, target, _, _ in work]
        message[1] = gram_message(p_basis + r_basis, columns)

    pl.when(is_top)(functools.partial(second_chains, True))
    pl.when(jnp.logical_not(is_top))(functools.partial(second_chains, False))
    received[1, tile] = message[1]
    reduce_over_tiles(1)
    v_basis = [of(field, OWN, 0)] + [of(v, OWN, PAD) for v in v_chain]

    def part_one(block, carry):
        at = pl.multiple_of(block * 128, 128)
        result[:, pl.ds(at, 128)] = tree_sum(x_first[j] * v_basis[j](block) for j in x_first)
        return carry

    lax.fori_loop(0, blocks, part_one, 0, unroll=True)
    x_second, _, _ = coefficient_cg(sum_over_tiles(1), (second + 1, second), diffusivity, second, True)

    basis = p_basis + r_basis
    pieces = 4
    width = columns // pieces
    for piece in range(pieces):

        def part_two(block, carry, piece=piece):
            block = block + piece * (width // 128)
            at = pl.multiple_of(block * 128, 128)
            result[:, pl.ds(at, 128)] += tree_sum(x_second[j] * basis[j](block) for j in x_second)
            return carry

        lax.fori_loop(0, width // 128, part_two, 0, unroll=True)
        here = slice(piece * width, piece * width + width)
        pltpu.make_async_remote_copy(
            src_ref=result.at[:, here],
            dst_ref=other_out.at[:, here],
            send_sem=last_send,
            recv_sem=last_recv,
            device_id={"var": 1 - var},
            device_id_type=MESH,
        ).start()
    keep = pltpu.make_async_copy(result, solved_out, last_local)
    keep.start()

    def sent(buffer, sem):
        pltpu.make_async_copy(buffer, buffer, sem).wait()

    sent(rhs.at[0 : levels - 1], there_send)
    sent(rhs.at[0 : levels - 1], back_send)
    halo_wait(quarter_mask, mask_send, False)
    halo_wait(field, halo_send, False)
    for index in range(2):
        sent(received.at[index, 0 : tiles - 1], sum_send.at[index])
    keep.wait()
    sent(result, last_send)
    pltpu.make_async_copy(other_out, other_out, last_recv).wait()


def per_device(
    background, norm_factor, v_diffusivity, h_diffusivity, sea_mask, fold_order, coupling
):
    rows, columns = background.shape[2:]
    levels, tiles = lax.axis_size("lev"), lax.axis_size("tile")
    part = columns // levels
    f32 = jnp.float32
    strip = jax.ShapeDtypeStruct((rows, columns), f32)
    vmem = pltpu.VMEM
    tall = vmem((32, columns), f32)

    def padded(height):
        return vmem((height, columns + 2 * PAD), f32)

    first, second = ROUNDS
    blocks = columns // 128
    dma = pltpu.SemaphoreType.DMA
    in_hbm = functools.partial(pltpu.with_memory_space_constraint, memory_space=pltpu.HBM)
    solved, other = pl.pallas_call(
        kernel,
        out_shape=(strip, strip),
        in_specs=[pl.BlockSpec(memory_space=pl.ANY)] * 3
        + [pl.BlockSpec(memory_space=pltpu.SMEM)]
        + [pl.BlockSpec(memory_space=pl.ANY)] * 2,
        out_specs=(pl.BlockSpec(memory_space=pl.ANY),) * 2,
        scratch_shapes=[
            vmem((rows, columns), f32),
            vmem((rows, columns), f32),
            vmem((levels, rows, part), f32),
            vmem((rows, columns), jnp.int32),
            vmem((1, columns), jnp.int32),
            vmem((rows, columns), f32),
            vmem((levels, rows, part), f32),
            vmem((levels, rows, part), f32),
            vmem((levels, rows, part), f32),
            vmem((levels, rows, part), f32),
            vmem((levels, rows, part), f32),
            tall,
            tall,
            vmem((16, columns), f32),
            padded(32),
            [padded(32 if j == 0 else 24) for j in range(first)],
            [padded(16)] * second,
            [padded(16)] * (second - 1),
            padded(24),
            padded(24),
            vmem((rows, columns), f32),
            vmem((rows, columns), f32),
            vmem((blocks, 128), jnp.int32),
            vmem((blocks, 128), jnp.int32),
            vmem((blocks, 8, 128), f32),
            vmem((blocks, 128), f32),
            vmem((blocks, 128), f32),
            vmem((2, 1, 128), f32),
            vmem((2, tiles, 1, 128), f32),
            vmem((rows, columns), f32),
            dma((5,)),
            dma,
            dma,
            dma,
            dma((levels,)),
            dma((4,)),
            dma((4,)),
            dma((4,)),
            dma((4,)),
            dma((2,)),
            dma((2,)),
            dma,
            dma,
            dma,
        ],
        compiler_params=pltpu.CompilerParams(
            collective_id=0, has_side_effects=True, vmem_limit_bytes=40 * 2**20
        ),
    )(
        in_hbm(background.reshape(rows, columns)),
        in_hbm(norm_factor.reshape(rows, columns)),
        in_hbm(v_diffusivity.reshape(levels, rows, part)),
        h_diffusivity,
        in_hbm(sea_mask.reshape(rows, columns)),
        in_hbm(fold_order.reshape(1, columns)),
    )
    return (solved + coupling[0, 0] * other)[None, None]


def solution(mesh):
    placed = (
        P("var", "lev", "tile", None),
        P("var", "lev", "tile", None),
        P("var", None, "tile", "lev"),
        P("var", "lev"),
        P("lev", "tile", None),
        P(),
        P("var", "lev", "tile", None),
    )
    return jax.shard_map(
        per_device,
        mesh=mesh,
        in_specs=placed,
        out_specs=P("var", "lev", "tile", None),
        check_vma=False,
    )
```

```python
import functools

import jax
import jax.numpy as jnp
from jax import lax
from jax.experimental import pallas as pl
from jax.experimental.pallas import tpu as pltpu
from jax.sharding import PartitionSpec as P

MESH = pl.DeviceIdType.MESH
ROUNDS = (5, 5)
SHIFTS = (0.0, 5.0, 2.0, 7.0, 0.5)
ROWS = 8
PAD = 128
OWN = slice(8, 16)


def tree_sum(terms):
    terms = list(terms)
    while len(terms) > 1:
        terms = [sum(terms[i : i + 2]) for i in range(0, len(terms), 2)]
    return terms[0]


def pairs_of(chains, last):
    count = sum(chains)
    ends = {sum(chains[: i + 1]) - 1 for i in range(len(chains))} if last else set()
    return [(i, j) for i in range(count) for j in range(i, count) if not (i in ends and j in ends)]


def gram_message(vectors, pairs, columns):
    lane = lax.broadcasted_iota(jnp.int32, (8, 128), 1)
    message = jnp.zeros((8, 128), jnp.float32)
    for at in range(0, len(pairs), 28):
        group = pairs[at : at + 28]
        used = sorted({i for pair in group for i in pair})

        def body(block, sums, group=group, used=used):
            held = {i: vectors[i](block) for i in used}
            return tuple(total + held[i] * held[j] for total, (i, j) in zip(sums, group))

        zeros = tuple(jnp.zeros((8, 128), jnp.float32) for _ in group)
        sums = lax.fori_loop(0, columns // 128, body, zeros, unroll=True)
        for place, total in enumerate(sums):
            message = jnp.where(lane == at + place, jnp.sum(total, axis=1, keepdims=True), message)
    return jnp.sum(message, axis=0, keepdims=True)


def coefficient_cg(totals, chains, diffusivity, steps, last):
    count = sum(chains)
    first = count - chains[-1]
    totals = jnp.broadcast_to(totals, (8, 128))
    gram = {}
    for place, (i, j) in enumerate(pairs_of(chains, last)):
        gram[i, j] = gram[j, i] = jnp.broadcast_to(totals[:, place : place + 1], (8, 128))
    same, start = {}, 0
    for length in chains:
        for j in range(length - 1):
            same[start + j] = 1.0 + diffusivity * SHIFTS[j]
        start += length
    up = 4.0 * diffusivity

    def image_of(d):
        parts = {}
        for j, value in d.items():
            parts.setdefault(j, []).append(same[j] * value)
            parts.setdefault(j + 1, []).append(up * value)
        return {j: sum(terms) for j, terms in sorted(parts.items())}

    def product(u, v):
        return tree_sum(u[i] * tree_sum(gram[i, j] * v[j] for j in v) for i in u)

    def add(u, factor, v):
        return {j: (u[j] if j in u else 0.0) + (factor * v[j] if j in v else 0.0) for j in sorted({*u, *v})}

    d, r, x = {0: 1.0}, {first: 1.0}, {}
    norm_now = gram[first, first]
    for step in range(steps):
        inverse_now = jnp.where(norm_now > 1e-37, 1.0 / norm_now, 0.0)
        image = image_of(d)
        energy = product(d, image)
        size = jnp.where(energy > 0, jnp.minimum(norm_now / energy, 1.0), 0.0)
        x = add(x, size, d)
        if last and step == steps - 1:
            break
        r = add(r, -size, image)
        norm_next = jnp.maximum(product(r, r), 0.0)
        d = add(r, norm_next * inverse_now, d)
        norm_now = norm_next
    return x, r, d


def packed(tall):
    upper_half = lax.broadcasted_iota(jnp.int32, (8, 128), 0) < 4
    return jnp.concatenate([tall[8:16], jnp.where(upper_half, tall[16:24], tall[0:8])], axis=0)


def operator(source, target, quarter_mask, columns, shift, rows, loaded, pack=False, folded=None, group=8):
    lane = lax.broadcasted_iota(jnp.int32, (rows, 128), 1)
    if folded is not None:
        line, last_row = folded
        is_last = lax.broadcasted_iota(jnp.int32, (rows, 128), 0) == last_row
    cut = packed if pack else lambda value: value[0:rows]

    def body(chunk, carry):
        at = pl.multiple_of(chunk * (group * 128), 128)
        held, ahead, behind = {}, {}, {}
        for k in range(group + 2):
            held[k] = source[0:loaded, pl.ds(at + 128 * k, 128)]
            ahead[k] = pltpu.roll(cut(held[k]), 127, 1)
            behind[k] = pltpu.roll(cut(held[k]), 1, 1)
            if k < 2:
                continue
            here = held[k - 1]
            east = jnp.where(lane == 127, ahead[k], ahead[k - 1])
            west = jnp.where(lane == 0, behind[k - 2], behind[k - 1])
            north = cut(pltpu.roll(here, loaded - 1, 0))
            south = cut(pltpu.roll(here, 1, 0))
            if folded is not None:
                north = jnp.where(is_last, line[pl.ds(chunk * group + k - 2, 1), :], north)
            here = cut(here)
            beside = (north + south) + (east + west)
            value = (1.0 - 0.25 * shift) * here if shift else here
            value = value - quarter_mask[0:rows, pl.ds(at + 128 * (k - 2), 128)] * beside
            target[0:rows, pl.ds(at + 128 * (k - 1), 128)] = value
        return carry

    lax.fori_loop(0, columns // (group * 128), body, 0, unroll=True)
    wrap(target, rows, columns)


def wrap(target, rows, columns):
    target[0:rows, 0:PAD] = target[0:rows, columns : columns + PAD]
    target[0:rows, columns + PAD : columns + 2 * PAD] = target[0:rows, PAD : 2 * PAD]


def kernel(
    background, norm_factor, v_diffusivity, h_diffusivity, sea_mask, fold_order,
    solved_out, other_out,
    bg, nf, vd, mask_in, fold_in, scaled, rhs, solved, inverse, below, upper,
    field, quarter_mask, packed_mask, masked, v_chain, p_chain, r_chain, masked_p, masked_r, p_own, r_own,
    partner_row, partner_lane, lines, folded_p, folded_r, message, received, result,
    load_sem, there_send, there_recv, back_send, back_recv,
    halo_send, halo_recv, mask_send, mask_recv, sum_send, sum_recv, last_send, last_recv, last_local,
):
    tile, lev, var = (lax.axis_index(a) for a in ("tile", "lev", "var"))
    tiles, levels = lax.axis_size("tile"), lax.axis_size("lev")
    columns = bg.shape[1]
    part = columns // levels
    top = tiles - 1
    blocks = columns // 128
    f32 = jnp.float32

    loads = [
        pltpu.make_async_copy(source, target, load_sem.at[i])
        for i, (source, target) in enumerate(
            ((background, bg), (norm_factor, nf), (sea_mask, mask_in), (v_diffusivity, vd), (fold_order, fold_in))
        )
    ]
    for load in loads:
        load.start()
    barrier = pltpu.get_barrier_semaphore()
    bits = (lax.rem(lev, 2), lax.rem(lev // 2, 2), lev // 4)

    def peer_level(d):
        return sum(
            (1 - bit if d >> place & 1 else bit) * (1 << place) for place, bit in enumerate(bits)
        )

    peers = [peer_level(d) for d in range(levels)]

    def greet_tile(d, carry):
        pl.semaphore_signal(barrier, inc=1, device_id={"tile": lax.rem(tile + d, tiles)}, device_id_type=MESH)
        return carry

    for d in range(1, levels):
        pl.semaphore_signal(barrier, inc=1, device_id={"lev": peers[d]}, device_id_type=MESH)
    pl.semaphore_signal(barrier, inc=1, device_id={"var": 1 - var}, device_id_type=MESH)
    lax.fori_loop(1, tiles, greet_tile, 0, unroll=True)
    loads[0].wait()
    loads[1].wait()
    scaled[...] = nf[...] * bg[...]
    loads[2].wait()
    quarter_mask[OWN, :] = 0.25 * mask_in[...].astype(f32)
    pl.semaphore_wait(barrier, (levels - 1) + (tiles - 1) + 1)

    for d in reversed(range(1, levels)):
        pltpu.make_async_remote_copy(
            src_ref=scaled.at[:, pl.ds(pl.multiple_of(peers[d] * part, part), part)],
            dst_ref=rhs.at[lev],
            send_sem=there_send,
            recv_sem=there_recv,
            device_id={"lev": peers[d]},
            device_id_type=MESH,
        ).start()
    rhs[lev] = scaled[:, pl.ds(pl.multiple_of(lev * part, part), part)]

    sides = ((8, 16, 0, 1), (8, 16, 16, -1), (14, 16, 30, 2), (8, 10, 24, -2))

    def reached(distance):
        return tile + distance <= top if distance > 0 else tile + distance >= 0

    def halo_copies(buffer, send, recv, at, width):
        for side, (low, high, land, distance) in enumerate(sides):

            @pl.when(reached(distance))
            def _(side=side, low=low, high=high, land=land, distance=distance):
                pltpu.make_async_remote_copy(
                    src_ref=buffer.at[low:high, pl.ds(at, width)],
                    dst_ref=buffer.at[land : land + high - low, pl.ds(at, width)],
                    send_sem=send.at[side],
                    recv_sem=recv.at[side],
                    device_id={"tile": tile + distance},
                    device_id_type=MESH,
                ).start()

    def halo_wait(buffer, sem, receive):
        for side, (low, high, land, distance) in enumerate(sides):

            @pl.when(reached(-distance if receive else distance))
            def _(side=side, low=low, high=high, land=land):
                at = slice(land, land + high - low) if receive else slice(low, high)
                pltpu.make_async_copy(buffer.at[at, :], buffer.at[at, :], sem.at[side]).wait()

    halo_copies(quarter_mask, mask_send, mask_recv, 0, columns)
    for low, high, land, distance in sides:

        @pl.when(jnp.logical_not(reached(-distance)))
        def _(land=land, rows=high - low):
            for buffer in (field, quarter_mask):
                buffer[land : land + rows, :] = jnp.zeros((rows, columns), f32)

    @pl.when(tile == top)
    def _():
        for chain in v_chain[1:]:
            chain[16:24, :] = jnp.zeros((8, chain.shape[1]), f32)

    loads[3].wait()
    above = jnp.zeros((ROWS, part), f32)
    upper_now = above
    for level in range(levels):
        coefficient = vd[level]
        inv = 1.0 / (1.0 + above + coefficient + above * upper_now)
        inverse[level] = inv
        below[level] = above * inv
        upper_now = -coefficient * inv
        upper[level] = upper_now
        above = coefficient

    loads[4].wait()

    @pl.when(tile >= top - 1)
    def _():
        order = fold_in[...]
        lane = lax.broadcasted_iota(jnp.int32, (1, columns), 1)
        mate = jnp.where(lane % 2 == 0, pltpu.roll(order, columns - 1, 1), pltpu.roll(order, 1, 1))
        row_hot = lax.broadcasted_iota(jnp.int32, (blocks, columns), 0) == order // 128
        lane_hot = lax.broadcasted_iota(jnp.int32, (128, columns), 0) == order % 128
        high = jnp.where(row_hot, (mate // 64).astype(f32), 0.0)
        low = jnp.where(row_hot, (mate % 64).astype(f32), 0.0)
        left = jnp.concatenate([high, low], axis=0).astype(jnp.bfloat16)
        right = jnp.where(lane_hot, 1.0, 0.0).astype(jnp.bfloat16)
        found = lax.dot_general(left, right, (((1,), (1,)), ((), ())), preferred_element_type=f32)
        partner = 64 * found[:blocks].astype(jnp.int32) + found[blocks:].astype(jnp.int32)
        partner_row[...] = partner // 128
        partner_lane[...] = partner % 128

    pltpu.make_async_copy(rhs.at[0 : levels - 1], rhs.at[0 : levels - 1], there_recv).wait()
    reduced = jnp.zeros((ROWS, part), f32)
    for level in range(levels):
        reduced = rhs[level] * inverse[level] + below[level] * reduced
        solved[level] = reduced
    value = jnp.zeros((ROWS, part), f32)
    for level in reversed(range(levels)):
        value = solved[level] - upper[level] * value
        solved[level] = value

    my_columns = pl.multiple_of(lev * part, part)

    for d in reversed(range(1, levels)):
        pltpu.make_async_remote_copy(
            src_ref=solved.at[peers[d]],
            dst_ref=field.at[OWN, pl.ds(my_columns, part)],
            send_sem=back_send,
            recv_sem=back_recv.at[d],
            device_id={"lev": peers[d]},
            device_id_type=MESH,
        ).start()
    field[OWN, pl.ds(my_columns, part)] = solved[lev]
    for d in range(1, levels):
        at = pl.multiple_of(peers[d] * part, part)
        here = field.at[OWN, pl.ds(at, part)]
        pltpu.make_async_copy(here, here, back_recv.at[d]).wait()
        if d % 2 == 1:
            at = pl.multiple_of(peers[d] // 2 * (2 * part), 2 * part)
            halo_copies(field, halo_send, halo_recv, at, 2 * part)

    def fold(buffer, last_row, folded):
        def repeat(block, carry):
            at = pl.multiple_of(PAD + block * 128, 128)
            lines[block] = jnp.broadcast_to(buffer[last_row : last_row + 1, pl.ds(at, 128)], (8, 128))
            return carry

        lax.fori_loop(0, blocks, repeat, 0, unroll=True)
        for q in range(blocks // 8):
            rows = slice(8 * q, 8 * q + 8)
            at_lane, at_row = partner_lane[rows, :], partner_row[rows, :]

            def pick(block, now, at_lane=at_lane, at_row=at_row):
                moved = jnp.take_along_axis(lines[block], at_lane, axis=1, mode="promise_in_bounds")
                return jnp.where(at_row == block, moved, now)

            folded[rows, :] = lax.fori_loop(0, blocks, pick, jnp.zeros((8, 128), f32), unroll=True)

    is_top = tile == top

    first, second = ROUNDS
    halo_wait(quarter_mask, mask_recv, True)

    def pack_mask(block, carry):
        at = pl.multiple_of(block * 128, 128)
        packed_mask[:, pl.ds(at, 128)] = packed(quarter_mask[0:24, pl.ds(at, 128)])
        return carry

    lax.fori_loop(0, blocks, pack_mask, 0, unroll=True)
    halo_wait(field, halo_recv, True)

    def apply_mask(block, carry):
        at = pl.multiple_of(block * 128, 128)
        masked[:, pl.ds(at + PAD, 128)] = (4.0 * quarter_mask[:, pl.ds(at, 128)]) * field[:, pl.ds(at, 128)]
        return carry

    lax.fori_loop(0, blocks, apply_mask, 0, unroll=True)
    wrap(masked, 32, columns)
    def first_chain(strip):
        source = masked
        for j in range(first):
            folded, rows = None, 24
            if strip == "top":
                fold(source, 15, folded_p)
                folded, rows = (folded_p, 15), 16
            elif strip == "next" and j < 2:
                fold(source, 23, folded_p)
                for block in range(blocks):
                    at = PAD + block * 128
                    source[24:25, at : at + 128] = folded_p[block : block + 1, :]
            if j == 0:
                rows = 32
            operator(
                source, v_chain[j], quarter_mask, columns, SHIFTS[j], rows, 32 if j < 2 else rows, folded=folded
            )
            source = v_chain[j]
        message[0] = gram_message([of(field, OWN, 0)] + [of(v, OWN, PAD) for v in v_chain], pairs_of((first + 1,), False), columns)

    def of(buffer, rows, pad):
        return lambda block: buffer[rows, pl.ds(pl.multiple_of(block * 128 + pad, 128), 128)]

    across = 8
    run, place = tile // across, lax.rem(tile, across)
    away = sorted(
        ((i, j) for i in range(tiles // across) for j in range(across) if i or j),
        key=lambda at: -min(at[0], tiles // across - at[0]) - min(at[1], across - at[1]),
    )
    others = [
        across * lax.rem(run + i, tiles // across) + lax.rem(place + j, across) for i, j in away
    ]

    def reduce_over_tiles(index):
        for to in others:
            pltpu.make_async_remote_copy(
                src_ref=message.at[index],
                dst_ref=received.at[index, tile],
                send_sem=sum_send.at[index],
                recv_sem=sum_recv.at[index],
                device_id={"tile": to},
                device_id_type=MESH,
            ).start()

    def sum_over_tiles(index):
        all_others = received.at[index, 0 : tiles - 1]
        pltpu.make_async_copy(all_others, all_others, sum_recv.at[index]).wait()
        return jnp.sum(received[index], axis=0)

    pl.when(is_top)(functools.partial(first_chain, "top"))
    pl.when(tile == top - 1)(functools.partial(first_chain, "next"))
    pl.when(tile < top - 1)(functools.partial(first_chain, "other"))
    received[0, tile] = message[0]
    reduce_over_tiles(0)
    diffusivity = h_diffusivity[0, 0]
    x_first, r_next, d_next = coefficient_cg(sum_over_tiles(0), (first + 1,), diffusivity, first, False)

    def next_round(block, carry):
        at = pl.multiple_of(block * 128, 128)
        rows = slice(0, 24)
        held = [field[rows, pl.ds(at, 128)]] + [v[rows, pl.ds(at + PAD, 128)] for v in v_chain]
        mask = 4.0 * quarter_mask[rows, pl.ds(at, 128)]
        for masked_one, own, numbers in ((masked_r, r_own, r_next), (masked_p, p_own, d_next)):
            tall = [jnp.concatenate([numbers[j]] * 3, axis=0) for j in numbers]
            value = tree_sum(number * held[j] for number, j in zip(tall, numbers))
            masked_one[:, pl.ds(at + PAD, 128)] = mask * value
            own[:, pl.ds(at, 128)] = value[8:16]
        return carry

    lax.fori_loop(0, blocks, next_round, 0, unroll=True)
    wrap(masked_r, 24, columns)
    wrap(masked_p, 24, columns)

    strip_rows = slice(0, 8)
    p_basis = [of(p_own, strip_rows, 0)] + [of(p, strip_rows, PAD) for p in p_chain]
    r_basis = [of(r_own, strip_rows, 0)] + [of(r, strip_rows, PAD) for r in r_chain]

    def second_chains(at_top):
        sources = [masked_p, masked_r]
        for j in range(second):
            work = [(sources[0], p_chain[j], folded_p, 8 if j == second - 1 else 16)]
            if j < second - 1:
                work.append((sources[1], r_chain[j], folded_r, 8 if j == second - 2 else 16))
            if at_top:
                for source, _, folded, _ in work:
                    fold(source, 15 if j == 0 else 7, folded)
            for source, target, folded, rows in work:
                operator(
                    source, target, packed_mask, columns, SHIFTS[j], rows, 24 if j == 0 else 16,
                    pack=j == 0, folded=(folded, 7) if at_top else None,
                )
            sources = [target for _, target, _, _ in work]
        message[1] = gram_message(p_basis + r_basis, pairs_of((second + 1, second), True), columns)

    pl.when(is_top)(functools.partial(second_chains, True))
    pl.when(jnp.logical_not(is_top))(functools.partial(second_chains, False))
    received[1, tile] = message[1]
    reduce_over_tiles(1)
    v_basis = [of(field, OWN, 0)] + [of(v, OWN, PAD) for v in v_chain]

    def part_one(block, carry):
        at = pl.multiple_of(block * 128, 128)
        result[:, pl.ds(at, 128)] = tree_sum(x_first[j] * v_basis[j](block) for j in x_first)
        return carry

    lax.fori_loop(0, blocks, part_one, 0, unroll=True)
    x_second, _, _ = coefficient_cg(sum_over_tiles(1), (second + 1, second), diffusivity, second, True)

    basis = p_basis + r_basis
    pieces = 4
    width = columns // pieces
    for piece in range(pieces):

        def part_two(block, carry, piece=piece):
            block = block + piece * (width // 128)
            at = pl.multiple_of(block * 128, 128)
            result[:, pl.ds(at, 128)] += tree_sum(x_second[j] * basis[j](block) for j in x_second)
            return carry

        lax.fori_loop(0, width // 128, part_two, 0, unroll=True)
        here = slice(piece * width, piece * width + width)
        pltpu.make_async_remote_copy(
            src_ref=result.at[:, here],
            dst_ref=other_out.at[:, here],
            send_sem=last_send,
            recv_sem=last_recv,
            device_id={"var": 1 - var},
            device_id_type=MESH,
        ).start()
    keep = pltpu.make_async_copy(result, solved_out, last_local)
    keep.start()

    def sent(buffer, sem):
        pltpu.make_async_copy(buffer, buffer, sem).wait()

    sent(rhs.at[0 : levels - 1], there_send)
    sent(rhs.at[0 : levels - 1], back_send)
    halo_wait(quarter_mask, mask_send, False)
    halo_wait(field, halo_send, False)
    for index in range(2):
        sent(received.at[index, 0 : tiles - 1], sum_send.at[index])
    keep.wait()
    sent(result, last_send)
    pltpu.make_async_copy(other_out, other_out, last_recv).wait()


def per_device(
    background, norm_factor, v_diffusivity, h_diffusivity, sea_mask, fold_order, coupling
):
    rows, columns = background.shape[2:]
    levels, tiles = lax.axis_size("lev"), lax.axis_size("tile")
    part = columns // levels
    f32 = jnp.float32
    strip = jax.ShapeDtypeStruct((rows, columns), f32)
    vmem = pltpu.VMEM
    tall = vmem((32, columns), f32)

    def padded(height):
        return vmem((height, columns + 2 * PAD), f32)

    first, second = ROUNDS
    blocks = columns // 128
    dma = pltpu.SemaphoreType.DMA
    in_hbm = functools.partial(pltpu.with_memory_space_constraint, memory_space=pltpu.HBM)
    solved, other = pl.pallas_call(
        kernel,
        out_shape=(strip, strip),
        in_specs=[pl.BlockSpec(memory_space=pl.ANY)] * 3
        + [pl.BlockSpec(memory_space=pltpu.SMEM)]
        + [pl.BlockSpec(memory_space=pl.ANY)] * 2,
        out_specs=(pl.BlockSpec(memory_space=pl.ANY),) * 2,
        scratch_shapes=[
            vmem((rows, columns), f32),
            vmem((rows, columns), f32),
            vmem((levels, rows, part), f32),
            vmem((rows, columns), jnp.int32),
            vmem((1, columns), jnp.int32),
            vmem((rows, columns), f32),
            vmem((levels, rows, part), f32),
            vmem((levels, rows, part), f32),
            vmem((levels, rows, part), f32),
            vmem((levels, rows, part), f32),
            vmem((levels, rows, part), f32),
            tall,
            tall,
            vmem((16, columns), f32),
            padded(32),
            [padded(32 if j == 0 else 24) for j in range(first)],
            [padded(16)] * second,
            [padded(16)] * (second - 1),
            padded(24),
            padded(24),
            vmem((rows, columns), f32),
            vmem((rows, columns), f32),
            vmem((blocks, 128), jnp.int32),
            vmem((blocks, 128), jnp.int32),
            vmem((blocks, 8, 128), f32),
            vmem((blocks, 128), f32),
            vmem((blocks, 128), f32),
            vmem((2, 1, 128), f32),
            vmem((2, tiles, 1, 128), f32),
            vmem((rows, columns), f32),
            dma((5,)),
            dma,
            dma,
            dma,
            dma((levels,)),
            dma((4,)),
            dma((4,)),
            dma((4,)),
            dma((4,)),
            dma((2,)),
            dma((2,)),
            dma,
            dma,
            dma,
        ],
        compiler_params=pltpu.CompilerParams(
            collective_id=0, has_side_effects=True, vmem_limit_bytes=40 * 2**20
        ),
    )(
        in_hbm(background.reshape(rows, columns)),
        in_hbm(norm_factor.reshape(rows, columns)),
        in_hbm(v_diffusivity.reshape(levels, rows, part)),
        h_diffusivity,
        in_hbm(sea_mask.reshape(rows, columns)),
        in_hbm(fold_order.reshape(1, columns)),
    )
    return (solved + coupling[0, 0] * other)[None, None]


def solution(mesh):
    placed = (
        P("var", "lev", "tile", None),
        P("var", "lev", "tile", None),
        P("var", None, "tile", "lev"),
        P("var", "lev"),
        P("lev", "tile", None),
        P(),
        P("var", "lev", "tile", None),
    )
    return jax.shard_map(
        per_device,
        mesh=mesh,
        in_specs=placed,
        out_specs=P("var", "lev", "tile", None),
        check_vma=False,
    )
```

```python
import functools

import jax
import jax.numpy as jnp
from jax import lax
from jax.experimental import pallas as pl
from jax.experimental.pallas import tpu as pltpu
from jax.sharding import PartitionSpec as P

MESH = pl.DeviceIdType.MESH
ROUNDS = (5, 5)
SHIFTS = (0.0, 5.0, 2.0, 7.0, 0.5)
ROWS = 8
PAD = 128
OWN = slice(8, 16)


def tree_sum(terms):
    terms = list(terms)
    while len(terms) > 1:
        terms = [sum(terms[i : i + 2]) for i in range(0, len(terms), 2)]
    return terms[0]


def pairs_of(chains, last):
    count = sum(chains)
    ends = {sum(chains[: i + 1]) - 1 for i in range(len(chains))} if last else set()
    return [(i, j) for i in range(count) for j in range(i, count) if not (i in ends and j in ends)]


def gram_message(vectors, pairs, columns):
    lane = lax.broadcasted_iota(jnp.int32, (8, 128), 1)
    message = jnp.zeros((8, 128), jnp.float32)
    for at in range(0, len(pairs), 28):
        group = pairs[at : at + 28]
        used = sorted({i for pair in group for i in pair})

        def body(block, sums, group=group, used=used):
            held = {i: vectors[i](block) for i in used}
            return tuple(total + held[i] * held[j] for total, (i, j) in zip(sums, group))

        zeros = tuple(jnp.zeros((8, 128), jnp.float32) for _ in group)
        sums = lax.fori_loop(0, columns // 128, body, zeros, unroll=True)
        for place, total in enumerate(sums):
            message = jnp.where(lane == at + place, jnp.sum(total, axis=1, keepdims=True), message)
    return jnp.sum(message, axis=0, keepdims=True)


def coefficient_cg(totals, chains, diffusivity, steps, last):
    count = sum(chains)
    first = count - chains[-1]
    totals = jnp.broadcast_to(totals, (8, 128))
    gram = {}
    for place, (i, j) in enumerate(pairs_of(chains, last)):
        gram[i, j] = gram[j, i] = jnp.broadcast_to(totals[:, place : place + 1], (8, 128))
    same, start = {}, 0
    for length in chains:
        for j in range(length - 1):
            same[start + j] = 1.0 + diffusivity * SHIFTS[j]
        start += length
    up = 4.0 * diffusivity

    def image_of(d):
        parts = {}
        for j, value in d.items():
            parts.setdefault(j, []).append(same[j] * value)
            parts.setdefault(j + 1, []).append(up * value)
        return {j: sum(terms) for j, terms in sorted(parts.items())}

    def product(u, v):
        return tree_sum(u[i] * tree_sum(gram[i, j] * v[j] for j in v) for i in u)

    def add(u, factor, v):
        return {j: (u[j] if j in u else 0.0) + (factor * v[j] if j in v else 0.0) for j in sorted({*u, *v})}

    d, r, x = {0: 1.0}, {first: 1.0}, {}
    norm_now = gram[first, first]
    for step in range(steps):
        inverse_now = jnp.where(norm_now > 1e-37, 1.0 / norm_now, 0.0)
        image = image_of(d)
        energy = product(d, image)
        size = jnp.where(energy > 0, jnp.minimum(norm_now / energy, 1.0), 0.0)
        x = add(x, size, d)
        if last and step == steps - 1:
            break
        r = add(r, -size, image)
        norm_next = jnp.maximum(product(r, r), 0.0)
        d = add(r, norm_next * inverse_now, d)
        norm_now = norm_next
    return x, r, d


def packed(tall):
    upper_half = lax.broadcasted_iota(jnp.int32, (8, 128), 0) < 4
    return jnp.concatenate([tall[8:16], jnp.where(upper_half, tall[16:24], tall[0:8])], axis=0)


def operator(source, target, quarter_mask, columns, shift, rows, loaded, pack=False, folded=None, group=8):
    lane = lax.broadcasted_iota(jnp.int32, (rows, 128), 1)
    if folded is not None:
        line, last_row = folded
        is_last = lax.broadcasted_iota(jnp.int32, (rows, 128), 0) == last_row
    cut = packed if pack else lambda value: value[0:rows]

    def body(chunk, carry):
        at = pl.multiple_of(chunk * (group * 128), 128)
        held, ahead, behind = {}, {}, {}
        for k in range(group + 2):
            held[k] = source[0:loaded, pl.ds(at + 128 * k, 128)]
            ahead[k] = pltpu.roll(cut(held[k]), 127, 1)
            behind[k] = pltpu.roll(cut(held[k]), 1, 1)
            if k < 2:
                continue
            here = held[k - 1]
            east = jnp.where(lane == 127, ahead[k], ahead[k - 1])
            west = jnp.where(lane == 0, behind[k - 2], behind[k - 1])
            north = cut(pltpu.roll(here, loaded - 1, 0))
            south = cut(pltpu.roll(here, 1, 0))
            if folded is not None:
                north = jnp.where(is_last, line[pl.ds(chunk * group + k - 2, 1), :], north)
            here = cut(here)
            beside = (north + south) + (east + west)
            value = (1.0 - 0.25 * shift) * here if shift else here
            value = value - quarter_mask[0:rows, pl.ds(at + 128 * (k - 2), 128)] * beside
            target[0:rows, pl.ds(at + 128 * (k - 1), 128)] = value
        return carry

    lax.fori_loop(0, columns // (group * 128), body, 0, unroll=True)
    wrap(target, rows, columns)


def wrap(target, rows, columns):
    target[0:rows, 0:PAD] = target[0:rows, columns : columns + PAD]
    target[0:rows, columns + PAD : columns + 2 * PAD] = target[0:rows, PAD : 2 * PAD]


def kernel(
    background, norm_factor, v_diffusivity, h_diffusivity, sea_mask, fold_order,
    solved_out, other_out,
    bg, nf, vd, mask_in, fold_in, scaled, rhs, solved, inverse, below, upper,
    field, quarter_mask, packed_mask, masked, v_chain, v_more, second_basis,
    partner_row, partner_lane, lines, folded_p, message, received, result,
    load_sem, there_send, there_recv, back_send, back_recv,
    halo_send, halo_recv, mask_send, mask_recv, sum_send, sum_recv, last_send, last_recv, last_local,
):
    tile, lev, var = (lax.axis_index(a) for a in ("tile", "lev", "var"))
    tiles, levels = lax.axis_size("tile"), lax.axis_size("lev")
    columns = bg.shape[1]
    part = columns // levels
    top = tiles - 1
    blocks = columns // 128
    f32 = jnp.float32

    loads = [
        pltpu.make_async_copy(source, target, load_sem.at[i])
        for i, (source, target) in enumerate(
            ((background, bg), (norm_factor, nf), (sea_mask, mask_in), (v_diffusivity, vd), (fold_order, fold_in))
        )
    ]
    for load in loads:
        load.start()
    barrier = pltpu.get_barrier_semaphore()
    bits = (lax.rem(lev, 2), lax.rem(lev // 2, 2), lev // 4)

    def peer_level(d):
        return sum(
            (1 - bit if d >> place & 1 else bit) * (1 << place) for place, bit in enumerate(bits)
        )

    peers = [peer_level(d) for d in range(levels)]

    def greet_tile(d, carry):
        pl.semaphore_signal(barrier, inc=1, device_id={"tile": lax.rem(tile + d, tiles)}, device_id_type=MESH)
        return carry

    for d in range(1, levels):
        pl.semaphore_signal(barrier, inc=1, device_id={"lev": peers[d]}, device_id_type=MESH)
    pl.semaphore_signal(barrier, inc=1, device_id={"var": 1 - var}, device_id_type=MESH)
    lax.fori_loop(1, tiles, greet_tile, 0, unroll=True)
    loads[0].wait()
    loads[1].wait()
    scaled[...] = nf[...] * bg[...]
    loads[2].wait()
    quarter_mask[OWN, :] = 0.25 * mask_in[...].astype(f32)
    pl.semaphore_wait(barrier, (levels - 1) + (tiles - 1) + 1)

    for d in reversed(range(1, levels)):
        pltpu.make_async_remote_copy(
            src_ref=scaled.at[:, pl.ds(pl.multiple_of(peers[d] * part, part), part)],
            dst_ref=rhs.at[lev],
            send_sem=there_send,
            recv_sem=there_recv,
            device_id={"lev": peers[d]},
            device_id_type=MESH,
        ).start()
    rhs[lev] = scaled[:, pl.ds(pl.multiple_of(lev * part, part), part)]

    sides = ((8, 16, 0, 1), (8, 16, 16, -1), (14, 16, 30, 2), (8, 10, 24, -2))

    def reached(distance):
        return tile + distance <= top if distance > 0 else tile + distance >= 0

    def halo_copies(buffer, send, recv, at, width):
        for side, (low, high, land, distance) in enumerate(sides):

            @pl.when(reached(distance))
            def _(side=side, low=low, high=high, land=land, distance=distance):
                pltpu.make_async_remote_copy(
                    src_ref=buffer.at[low:high, pl.ds(at, width)],
                    dst_ref=buffer.at[land : land + high - low, pl.ds(at, width)],
                    send_sem=send.at[side],
                    recv_sem=recv.at[side],
                    device_id={"tile": tile + distance},
                    device_id_type=MESH,
                ).start()

    def halo_wait(buffer, sem, receive):
        for side, (low, high, land, distance) in enumerate(sides):

            @pl.when(reached(-distance if receive else distance))
            def _(side=side, low=low, high=high, land=land):
                at = slice(land, land + high - low) if receive else slice(low, high)
                pltpu.make_async_copy(buffer.at[at, :], buffer.at[at, :], sem.at[side]).wait()

    halo_copies(quarter_mask, mask_send, mask_recv, 0, columns)
    for low, high, land, distance in sides:

        @pl.when(jnp.logical_not(reached(-distance)))
        def _(land=land, rows=high - low):
            for buffer in (field, quarter_mask):
                buffer[land : land + rows, :] = jnp.zeros((rows, columns), f32)

    @pl.when(tile == top)
    def _():
        for chain in v_chain[1:]:
            chain[16:24, :] = jnp.zeros((8, chain.shape[1]), f32)

    loads[3].wait()
    above = jnp.zeros((ROWS, part), f32)
    upper_now = above
    for level in range(levels):
        coefficient = vd[level]
        inv = 1.0 / (1.0 + above + coefficient + above * upper_now)
        inverse[level] = inv
        below[level] = above * inv
        upper_now = -coefficient * inv
        upper[level] = upper_now
        above = coefficient

    loads[4].wait()

    @pl.when(tile >= top - 1)
    def _():
        order = fold_in[...]
        lane = lax.broadcasted_iota(jnp.int32, (1, columns), 1)
        mate = jnp.where(lane % 2 == 0, pltpu.roll(order, columns - 1, 1), pltpu.roll(order, 1, 1))
        row_hot = lax.broadcasted_iota(jnp.int32, (blocks, columns), 0) == order // 128
        lane_hot = lax.broadcasted_iota(jnp.int32, (128, columns), 0) == order % 128
        high = jnp.where(row_hot, (mate // 64).astype(f32), 0.0)
        low = jnp.where(row_hot, (mate % 64).astype(f32), 0.0)
        left = jnp.concatenate([high, low], axis=0).astype(jnp.bfloat16)
        right = jnp.where(lane_hot, 1.0, 0.0).astype(jnp.bfloat16)
        found = lax.dot_general(left, right, (((1,), (1,)), ((), ())), preferred_element_type=f32)
        partner = 64 * found[:blocks].astype(jnp.int32) + found[blocks:].astype(jnp.int32)
        partner_row[...] = partner // 128
        partner_lane[...] = partner % 128

    pltpu.make_async_copy(rhs.at[0 : levels - 1], rhs.at[0 : levels - 1], there_recv).wait()
    reduced = jnp.zeros((ROWS, part), f32)
    for level in range(levels):
        reduced = rhs[level] * inverse[level] + below[level] * reduced
        solved[level] = reduced
    value = jnp.zeros((ROWS, part), f32)
    for level in reversed(range(levels)):
        value = solved[level] - upper[level] * value
        solved[level] = value

    my_columns = pl.multiple_of(lev * part, part)

    for d in reversed(range(1, levels)):
        pltpu.make_async_remote_copy(
            src_ref=solved.at[peers[d]],
            dst_ref=field.at[OWN, pl.ds(my_columns, part)],
            send_sem=back_send,
            recv_sem=back_recv.at[d],
            device_id={"lev": peers[d]},
            device_id_type=MESH,
        ).start()
    field[OWN, pl.ds(my_columns, part)] = solved[lev]
    for d in range(1, levels):
        at = pl.multiple_of(peers[d] * part, part)
        here = field.at[OWN, pl.ds(at, part)]
        pltpu.make_async_copy(here, here, back_recv.at[d]).wait()
        if d % 2 == 1:
            at = pl.multiple_of(peers[d] // 2 * (2 * part), 2 * part)
            halo_copies(field, halo_send, halo_recv, at, 2 * part)

    def fold(buffer, last_row, folded):
        def repeat(block, carry):
            at = pl.multiple_of(PAD + block * 128, 128)
            lines[block] = jnp.broadcast_to(buffer[last_row : last_row + 1, pl.ds(at, 128)], (8, 128))
            return carry

        lax.fori_loop(0, blocks, repeat, 0, unroll=True)
        for q in range(blocks // 8):
            rows = slice(8 * q, 8 * q + 8)
            at_lane, at_row = partner_lane[rows, :], partner_row[rows, :]

            def pick(block, now, at_lane=at_lane, at_row=at_row):
                moved = jnp.take_along_axis(lines[block], at_lane, axis=1, mode="promise_in_bounds")
                return jnp.where(at_row == block, moved, now)

            folded[rows, :] = lax.fori_loop(0, blocks, pick, jnp.zeros((8, 128), f32), unroll=True)

    is_top = tile == top

    first, second = ROUNDS
    halo_wait(quarter_mask, mask_recv, True)

    def pack_mask(block, carry):
        at = pl.multiple_of(block * 128, 128)
        packed_mask[:, pl.ds(at, 128)] = packed(quarter_mask[0:24, pl.ds(at, 128)])
        return carry

    lax.fori_loop(0, blocks, pack_mask, 0, unroll=True)
    halo_wait(field, halo_recv, True)

    def apply_mask(block, carry):
        at = pl.multiple_of(block * 128, 128)
        masked[:, pl.ds(at + PAD, 128)] = (4.0 * quarter_mask[:, pl.ds(at, 128)]) * field[:, pl.ds(at, 128)]
        return carry

    lax.fori_loop(0, blocks, apply_mask, 0, unroll=True)
    wrap(masked, 32, columns)
    def first_chain(strip):
        source = masked
        for j in range(first):
            folded, rows = None, 24
            if strip == "top":
                fold(source, 15, folded_p)
                folded, rows = (folded_p, 15), 16
            elif strip == "next" and j < 2:
                fold(source, 23, folded_p)
                for block in range(blocks):
                    at = PAD + block * 128
                    source[24:25, at : at + 128] = folded_p[block : block + 1, :]
            if j == 0:
                rows = 32
            operator(
                source, v_chain[j], quarter_mask, columns, SHIFTS[j], rows, 32 if j < 2 else rows, folded=folded
            )
            source = v_chain[j]
        message[0] = gram_message([of(field, OWN, 0)] + [of(v, OWN, PAD) for v in v_chain], pairs_of((first + 1,), False), columns)

    def of(buffer, rows, pad):
        return lambda block: buffer[rows, pl.ds(pl.multiple_of(block * 128 + pad, 128), 128)]

    across = 8
    run, place = tile // across, lax.rem(tile, across)
    away = sorted(
        ((i, j) for i in range(tiles // across) for j in range(across) if i or j),
        key=lambda at: -min(at[0], tiles // across - at[0]) - min(at[1], across - at[1]),
    )
    others = [
        across * lax.rem(run + i, tiles // across) + lax.rem(place + j, across) for i, j in away
    ]

    def reduce_over_tiles(index):
        for to in others:
            pltpu.make_async_remote_copy(
                src_ref=message.at[index],
                dst_ref=received.at[index, tile],
                send_sem=sum_send.at[index],
                recv_sem=sum_recv.at[index],
                device_id={"tile": to},
                device_id_type=MESH,
            ).start()

    def sum_over_tiles(index):
        all_others = received.at[index, 0 : tiles - 1]
        pltpu.make_async_copy(all_others, all_others, sum_recv.at[index]).wait()
        return jnp.sum(received[index], axis=0)

    pl.when(is_top)(functools.partial(first_chain, "top"))
    pl.when(tile == top - 1)(functools.partial(first_chain, "next"))
    pl.when(tile < top - 1)(functools.partial(first_chain, "other"))
    received[0, tile] = message[0]
    reduce_over_tiles(0)

    def more_chain(at_top):
        source = v_chain[-1]
        for j in range(second):
            if at_top:
                fold(source, 15 if j == 0 else 7, folded_p)
            operator(
                source, v_more[j], packed_mask, columns, SHIFTS[j], 8 if j == second - 1 else 16,
                24 if j == 0 else 16, pack=j == 0, folded=(folded_p, 7) if at_top else None,
            )
            source = v_more[j]

    pl.when(is_top)(functools.partial(more_chain, True))
    pl.when(jnp.logical_not(is_top))(functools.partial(more_chain, False))
    strip_rows = slice(0, 8)
    v_basis = [of(field, OWN, 0)] + [of(v, OWN, PAD) for v in v_chain] + [of(v, strip_rows, PAD) for v in v_more]

    diffusivity = h_diffusivity[0, 0]
    x_first, r_next, d_next = coefficient_cg(sum_over_tiles(0), (first + 1,), diffusivity, first, False)

    all_shifts = SHIFTS[:first] + SHIFTS[:second]

    def chain_numbers(numbers, length):
        chain = [numbers]
        for j in range(length):
            parts = {}
            for i, value in chain[-1].items():
                parts.setdefault(i + 1, []).append(value)
                if all_shifts[i] != SHIFTS[j]:
                    parts.setdefault(i, []).append((0.25 * (all_shifts[i] - SHIFTS[j])) * value)
            chain.append({i: sum(terms) for i, terms in sorted(parts.items())})
        return chain

    numbers = chain_numbers(d_next, second) + chain_numbers(r_next, second - 1)
    basis = [of(one, strip_rows, 0) for one in second_basis]

    def combine(block, carry):
        at = pl.multiple_of(block * 128, 128)
        held = [v(block) for v in v_basis]
        for one, terms in zip(second_basis, numbers):
            one[:, pl.ds(at, 128)] = tree_sum(terms[i] * held[i] for i in terms)
        return carry

    lax.fori_loop(0, blocks, combine, 0, unroll=True)
    message[1] = gram_message(basis, pairs_of((second + 1, second), True), columns)
    received[1, tile] = message[1]
    reduce_over_tiles(1)
    def part_one(block, carry):
        at = pl.multiple_of(block * 128, 128)
        result[:, pl.ds(at, 128)] = tree_sum(x_first[j] * v_basis[j](block) for j in x_first)
        return carry

    lax.fori_loop(0, blocks, part_one, 0, unroll=True)
    x_second, _, _ = coefficient_cg(sum_over_tiles(1), (second + 1, second), diffusivity, second, True)

    pieces = 4
    width = columns // pieces
    for piece in range(pieces):

        def part_two(block, carry, piece=piece):
            block = block + piece * (width // 128)
            at = pl.multiple_of(block * 128, 128)
            result[:, pl.ds(at, 128)] += tree_sum(x_second[j] * basis[j](block) for j in x_second)
            return carry

        lax.fori_loop(0, width // 128, part_two, 0, unroll=True)
        here = slice(piece * width, piece * width + width)
        pltpu.make_async_remote_copy(
            src_ref=result.at[:, here],
            dst_ref=other_out.at[:, here],
            send_sem=last_send,
            recv_sem=last_recv,
            device_id={"var": 1 - var},
            device_id_type=MESH,
        ).start()
    keep = pltpu.make_async_copy(result, solved_out, last_local)
    keep.start()

    def sent(buffer, sem):
        pltpu.make_async_copy(buffer, buffer, sem).wait()

    sent(rhs.at[0 : levels - 1], there_send)
    sent(rhs.at[0 : levels - 1], back_send)
    halo_wait(quarter_mask, mask_send, False)
    halo_wait(field, halo_send, False)
    for index in range(2):
        sent(received.at[index, 0 : tiles - 1], sum_send.at[index])
    keep.wait()
    sent(result, last_send)
    pltpu.make_async_copy(other_out, other_out, last_recv).wait()


def per_device(
    background, norm_factor, v_diffusivity, h_diffusivity, sea_mask, fold_order, coupling
):
    rows, columns = background.shape[2:]
    levels, tiles = lax.axis_size("lev"), lax.axis_size("tile")
    part = columns // levels
    f32 = jnp.float32
    strip = jax.ShapeDtypeStruct((rows, columns), f32)
    vmem = pltpu.VMEM
    tall = vmem((32, columns), f32)

    def padded(height):
        return vmem((height, columns + 2 * PAD), f32)

    first, second = ROUNDS
    blocks = columns // 128
    dma = pltpu.SemaphoreType.DMA
    in_hbm = functools.partial(pltpu.with_memory_space_constraint, memory_space=pltpu.HBM)
    solved, other = pl.pallas_call(
        kernel,
        out_shape=(strip, strip),
        in_specs=[pl.BlockSpec(memory_space=pl.ANY)] * 3
        + [pl.BlockSpec(memory_space=pltpu.SMEM)]
        + [pl.BlockSpec(memory_space=pl.ANY)] * 2,
        out_specs=(pl.BlockSpec(memory_space=pl.ANY),) * 2,
        scratch_shapes=[
            vmem((rows, columns), f32),
            vmem((rows, columns), f32),
            vmem((levels, rows, part), f32),
            vmem((rows, columns), jnp.int32),
            vmem((1, columns), jnp.int32),
            vmem((rows, columns), f32),
            vmem((levels, rows, part), f32),
            vmem((levels, rows, part), f32),
            vmem((levels, rows, part), f32),
            vmem((levels, rows, part), f32),
            vmem((levels, rows, part), f32),
            tall,
            tall,
            vmem((16, columns), f32),
            padded(32),
            [padded(32 if j == 0 else 24) for j in range(first)],
            [padded(16)] * second,
            [vmem((rows, columns), f32)] * (2 * second + 1),
            vmem((blocks, 128), jnp.int32),
            vmem((blocks, 128), jnp.int32),
            vmem((blocks, 8, 128), f32),
            vmem((blocks, 128), f32),
            vmem((2, 1, 128), f32),
            vmem((2, tiles, 1, 128), f32),
            vmem((rows, columns), f32),
            dma((5,)),
            dma,
            dma,
            dma,
            dma((levels,)),
            dma((4,)),
            dma((4,)),
            dma((4,)),
            dma((4,)),
            dma((2,)),
            dma((2,)),
            dma,
            dma,
            dma,
        ],
        compiler_params=pltpu.CompilerParams(
            collective_id=0, has_side_effects=True, vmem_limit_bytes=40 * 2**20
        ),
    )(
        in_hbm(background.reshape(rows, columns)),
        in_hbm(norm_factor.reshape(rows, columns)),
        in_hbm(v_diffusivity.reshape(levels, rows, part)),
        h_diffusivity,
        in_hbm(sea_mask.reshape(rows, columns)),
        in_hbm(fold_order.reshape(1, columns)),
    )
    return (solved + coupling[0, 0] * other)[None, None]


def solution(mesh):
    placed = (
        P("var", "lev", "tile", None),
        P("var", "lev", "tile", None),
        P("var", None, "tile", "lev"),
        P("var", "lev"),
        P("lev", "tile", None),
        P(),
        P("var", "lev", "tile", None),
    )
    return jax.shard_map(
        per_device,
        mesh=mesh,
        in_specs=placed,
        out_specs=P("var", "lev", "tile", None),
        check_vma=False,
    )
```

```python
import functools

import jax
import jax.numpy as jnp
from jax import lax
from jax.experimental import pallas as pl
from jax.experimental.pallas import tpu as pltpu
from jax.sharding import PartitionSpec as P

MESH = pl.DeviceIdType.MESH
ROUNDS = (5, 5)
SHIFTS = (0.0, 5.0, 2.0, 7.0, 0.5)
ROWS = 8
PAD = 128
OWN = slice(8, 16)


def tree_sum(terms):
    terms = list(terms)
    while len(terms) > 1:
        terms = [sum(terms[i : i + 2]) for i in range(0, len(terms), 2)]
    return terms[0]


def pairs_of(chains, last):
    count = sum(chains)
    ends = {sum(chains[: i + 1]) - 1 for i in range(len(chains))} if last else set()
    return [(i, j) for i in range(count) for j in range(i, count) if not (i in ends and j in ends)]


def gram_message(vectors, pairs, columns):
    lane = lax.broadcasted_iota(jnp.int32, (8, 128), 1)
    message = jnp.zeros((8, 128), jnp.float32)
    for at in range(0, len(pairs), 28):
        group = pairs[at : at + 28]
        used = sorted({i for pair in group for i in pair})

        def body(block, sums, group=group, used=used):
            held = {i: vectors[i](block) for i in used}
            return tuple(total + held[i] * held[j] for total, (i, j) in zip(sums, group))

        zeros = tuple(jnp.zeros((8, 128), jnp.float32) for _ in group)
        sums = lax.fori_loop(0, columns // 128, body, zeros, unroll=True)
        for place, total in enumerate(sums):
            message = jnp.where(lane == at + place, jnp.sum(total, axis=1, keepdims=True), message)
    return jnp.sum(message, axis=0, keepdims=True)


def coefficient_cg(totals, chains, diffusivity, steps, last):
    count = sum(chains)
    first = count - chains[-1]
    totals = jnp.broadcast_to(totals, (8, 128))
    gram = {}
    for place, (i, j) in enumerate(pairs_of(chains, last)):
        gram[i, j] = gram[j, i] = jnp.broadcast_to(totals[:, place : place + 1], (8, 128))
    same, start = {}, 0
    for length in chains:
        for j in range(length - 1):
            same[start + j] = 1.0 + diffusivity * SHIFTS[j]
        start += length
    up = 4.0 * diffusivity

    def image_of(d):
        parts = {}
        for j, value in d.items():
            parts.setdefault(j, []).append(same[j] * value)
            parts.setdefault(j + 1, []).append(up * value)
        return {j: sum(terms) for j, terms in sorted(parts.items())}

    def product(u, v):
        return tree_sum(u[i] * tree_sum(gram[i, j] * v[j] for j in v) for i in u)

    def add(u, factor, v):
        return {j: (u[j] if j in u else 0.0) + (factor * v[j] if j in v else 0.0) for j in sorted({*u, *v})}

    d, r, x = {0: 1.0}, {first: 1.0}, {}
    norm_now = gram[first, first]
    for step in range(steps):
        inverse_now = jnp.where(norm_now > 1e-37, 1.0 / norm_now, 0.0)
        image = image_of(d)
        energy = product(d, image)
        size = jnp.where(energy > 0, jnp.minimum(norm_now / energy, 1.0), 0.0)
        x = add(x, size, d)
        if last and step == steps - 1:
            break
        r = add(r, -size, image)
        norm_next = jnp.maximum(product(r, r), 0.0)
        d = add(r, norm_next * inverse_now, d)
        norm_now = norm_next
    return x, r, d


def packed(tall):
    upper_half = lax.broadcasted_iota(jnp.int32, (8, 128), 0) < 4
    return jnp.concatenate([tall[8:16], jnp.where(upper_half, tall[16:24], tall[0:8])], axis=0)


def operator(source, target, quarter_mask, columns, shift, rows, loaded, pack=False, folded=None, group=8):
    lane = lax.broadcasted_iota(jnp.int32, (rows, 128), 1)
    if folded is not None:
        line, last_row = folded
        is_last = lax.broadcasted_iota(jnp.int32, (rows, 128), 0) == last_row
    cut = packed if pack else lambda value: value[0:rows]

    def body(chunk, carry):
        at = pl.multiple_of(chunk * (group * 128), 128)
        held, ahead, behind = {}, {}, {}
        for k in range(group + 2):
            held[k] = source[0:loaded, pl.ds(at + 128 * k, 128)]
            ahead[k] = pltpu.roll(cut(held[k]), 127, 1)
            behind[k] = pltpu.roll(cut(held[k]), 1, 1)
            if k < 2:
                continue
            here = held[k - 1]
            east = jnp.where(lane == 127, ahead[k], ahead[k - 1])
            west = jnp.where(lane == 0, behind[k - 2], behind[k - 1])
            north = cut(pltpu.roll(here, loaded - 1, 0))
            south = cut(pltpu.roll(here, 1, 0))
            if folded is not None:
                north = jnp.where(is_last, line[pl.ds(chunk * group + k - 2, 1), :], north)
            here = cut(here)
            beside = (north + south) + (east + west)
            value = (1.0 - 0.25 * shift) * here if shift else here
            value = value - quarter_mask[0:rows, pl.ds(at + 128 * (k - 2), 128)] * beside
            target[0:rows, pl.ds(at + 128 * (k - 1), 128)] = value
        return carry

    lax.fori_loop(0, columns // (group * 128), body, 0, unroll=True)
    wrap(target, rows, columns)


def wrap(target, rows, columns):
    target[0:rows, 0:PAD] = target[0:rows, columns : columns + PAD]
    target[0:rows, columns + PAD : columns + 2 * PAD] = target[0:rows, PAD : 2 * PAD]


def kernel(
    background, norm_factor, v_diffusivity, h_diffusivity, sea_mask, fold_order,
    solved_out, other_out,
    bg, nf, vd, mask_in, fold_in, scaled, rhs, solved, inverse, below, upper,
    field, quarter_mask, packed_mask, masked, v_chain, v_more, second_basis,
    partner_row, partner_lane, lines, folded_p, message, received, result,
    load_sem, there_send, there_recv, back_send, back_recv,
    halo_send, halo_recv, mask_send, mask_recv, sum_send, sum_recv, last_send, last_recv, last_local,
):
    tile, lev, var = (lax.axis_index(a) for a in ("tile", "lev", "var"))
    tiles, levels = lax.axis_size("tile"), lax.axis_size("lev")
    columns = bg.shape[1]
    part = columns // levels
    top = tiles - 1
    blocks = columns // 128
    f32 = jnp.float32

    loads = [
        pltpu.make_async_copy(source, target, load_sem.at[i])
        for i, (source, target) in enumerate(
            ((background, bg), (norm_factor, nf), (sea_mask, mask_in), (v_diffusivity, vd), (fold_order, fold_in))
        )
    ]
    for load in loads[:2]:
        load.start()
    barrier = pltpu.get_barrier_semaphore()
    bits = (lax.rem(lev, 2), lax.rem(lev // 2, 2), lev // 4)

    def peer_level(d):
        return sum(
            (1 - bit if d >> place & 1 else bit) * (1 << place) for place, bit in enumerate(bits)
        )

    peers = [peer_level(d) for d in range(levels)]

    def greet_tile(d, carry):
        pl.semaphore_signal(barrier, inc=1, device_id={"tile": lax.rem(tile + d, tiles)}, device_id_type=MESH)
        return carry

    for d in range(1, levels):
        pl.semaphore_signal(barrier, inc=1, device_id={"lev": peers[d]}, device_id_type=MESH)
    pl.semaphore_signal(barrier, inc=1, device_id={"var": 1 - var}, device_id_type=MESH)
    lax.fori_loop(1, tiles, greet_tile, 0, unroll=True)
    for load in loads[2:]:
        load.start()
    loads[0].wait()
    loads[1].wait()
    scaled[...] = nf[...] * bg[...]
    pl.semaphore_wait(barrier, (levels - 1) + (tiles - 1) + 1)

    for d in reversed(range(1, levels)):
        pltpu.make_async_remote_copy(
            src_ref=scaled.at[:, pl.ds(pl.multiple_of(peers[d] * part, part), part)],
            dst_ref=rhs.at[lev],
            send_sem=there_send,
            recv_sem=there_recv,
            device_id={"lev": peers[d]},
            device_id_type=MESH,
        ).start()
    rhs[lev] = scaled[:, pl.ds(pl.multiple_of(lev * part, part), part)]

    sides = ((8, 16, 0, 1), (8, 16, 16, -1), (14, 16, 30, 2), (8, 10, 24, -2))

    def reached(distance):
        return tile + distance <= top if distance > 0 else tile + distance >= 0

    def halo_copies(buffer, send, recv, at, width):
        for side, (low, high, land, distance) in enumerate(sides):

            @pl.when(reached(distance))
            def _(side=side, low=low, high=high, land=land, distance=distance):
                pltpu.make_async_remote_copy(
                    src_ref=buffer.at[low:high, pl.ds(at, width)],
                    dst_ref=buffer.at[land : land + high - low, pl.ds(at, width)],
                    send_sem=send.at[side],
                    recv_sem=recv.at[side],
                    device_id={"tile": tile + distance},
                    device_id_type=MESH,
                ).start()

    def halo_wait(buffer, sem, receive):
        for side, (low, high, land, distance) in enumerate(sides):

            @pl.when(reached(-distance if receive else distance))
            def _(side=side, low=low, high=high, land=land):
                at = slice(land, land + high - low) if receive else slice(low, high)
                pltpu.make_async_copy(buffer.at[at, :], buffer.at[at, :], sem.at[side]).wait()

    loads[2].wait()
    quarter_mask[OWN, :] = 0.25 * mask_in[...].astype(f32)
    halo_copies(quarter_mask, mask_send, mask_recv, 0, columns)
    for low, high, land, distance in sides:

        @pl.when(jnp.logical_not(reached(-distance)))
        def _(land=land, rows=high - low):
            for buffer in (field, quarter_mask):
                buffer[land : land + rows, :] = jnp.zeros((rows, columns), f32)

    @pl.when(tile == top)
    def _():
        for chain in v_chain[1:]:
            chain[16:24, :] = jnp.zeros((8, chain.shape[1]), f32)

    loads[3].wait()
    above = jnp.zeros((ROWS, part), f32)
    upper_now = above
    for level in range(levels):
        coefficient = vd[level]
        inv = 1.0 / (1.0 + above + coefficient + above * upper_now)
        inverse[level] = inv
        below[level] = above * inv
        upper_now = -coefficient * inv
        upper[level] = upper_now
        above = coefficient

    loads[4].wait()

    @pl.when(tile >= top - 1)
    def _():
        order = fold_in[...]
        lane = lax.broadcasted_iota(jnp.int32, (1, columns), 1)
        mate = jnp.where(lane % 2 == 0, pltpu.roll(order, columns - 1, 1), pltpu.roll(order, 1, 1))
        row_hot = lax.broadcasted_iota(jnp.int32, (blocks, columns), 0) == order // 128
        lane_hot = lax.broadcasted_iota(jnp.int32, (128, columns), 0) == order % 128
        high = jnp.where(row_hot, (mate // 64).astype(f32), 0.0)
        low = jnp.where(row_hot, (mate % 64).astype(f32), 0.0)
        left = jnp.concatenate([high, low], axis=0).astype(jnp.bfloat16)
        right = jnp.where(lane_hot, 1.0, 0.0).astype(jnp.bfloat16)
        found = lax.dot_general(left, right, (((1,), (1,)), ((), ())), preferred_element_type=f32)
        partner = 64 * found[:blocks].astype(jnp.int32) + found[blocks:].astype(jnp.int32)
        partner_row[...] = partner // 128
        partner_lane[...] = partner % 128

    pltpu.make_async_copy(rhs.at[0 : levels - 1], rhs.at[0 : levels - 1], there_recv).wait()
    reduced = jnp.zeros((ROWS, part), f32)
    for level in range(levels):
        reduced = rhs[level] * inverse[level] + below[level] * reduced
        solved[level] = reduced
    value = jnp.zeros((ROWS, part), f32)
    for level in reversed(range(levels)):
        value = solved[level] - upper[level] * value
        solved[level] = value

    my_columns = pl.multiple_of(lev * part, part)

    for d in reversed(range(1, levels)):
        pltpu.make_async_remote_copy(
            src_ref=solved.at[peers[d]],
            dst_ref=field.at[OWN, pl.ds(my_columns, part)],
            send_sem=back_send,
            recv_sem=back_recv.at[d],
            device_id={"lev": peers[d]},
            device_id_type=MESH,
        ).start()
    field[OWN, pl.ds(my_columns, part)] = solved[lev]
    for d in range(1, levels):
        at = pl.multiple_of(peers[d] * part, part)
        here = field.at[OWN, pl.ds(at, part)]
        pltpu.make_async_copy(here, here, back_recv.at[d]).wait()
        if d % 2 == 1:
            at = pl.multiple_of(peers[d] // 2 * (2 * part), 2 * part)
            halo_copies(field, halo_send, halo_recv, at, 2 * part)

    def fold(buffer, last_row, folded):
        def repeat(block, carry):
            at = pl.multiple_of(PAD + block * 128, 128)
            lines[block] = jnp.broadcast_to(buffer[last_row : last_row + 1, pl.ds(at, 128)], (8, 128))
            return carry

        lax.fori_loop(0, blocks, repeat, 0, unroll=True)
        for q in range(blocks // 8):
            rows = slice(8 * q, 8 * q + 8)
            at_lane, at_row = partner_lane[rows, :], partner_row[rows, :]

            def pick(block, now, at_lane=at_lane, at_row=at_row):
                moved = jnp.take_along_axis(lines[block], at_lane, axis=1, mode="promise_in_bounds")
                return jnp.where(at_row == block, moved, now)

            folded[rows, :] = lax.fori_loop(0, blocks, pick, jnp.zeros((8, 128), f32), unroll=True)

    is_top = tile == top

    first, second = ROUNDS
    halo_wait(quarter_mask, mask_recv, True)

    def pack_mask(block, carry):
        at = pl.multiple_of(block * 128, 128)
        packed_mask[:, pl.ds(at, 128)] = packed(quarter_mask[0:24, pl.ds(at, 128)])
        return carry

    lax.fori_loop(0, blocks, pack_mask, 0, unroll=True)
    halo_wait(field, halo_recv, True)

    def apply_mask(block, carry):
        at = pl.multiple_of(block * 128, 128)
        masked[:, pl.ds(at + PAD, 128)] = (4.0 * quarter_mask[:, pl.ds(at, 128)]) * field[:, pl.ds(at, 128)]
        return carry

    lax.fori_loop(0, blocks, apply_mask, 0, unroll=True)
    wrap(masked, 32, columns)
    def first_chain(strip):
        source = masked
        for j in range(first):
            folded, rows = None, 24
            if strip == "top":
                fold(source, 15, folded_p)
                folded, rows = (folded_p, 15), 16
            elif strip == "next" and j < 2:
                fold(source, 23, folded_p)
                folded = (folded_p, 23)
            if j == 0:
                rows = 32
            operator(
                source, v_chain[j], quarter_mask, columns, SHIFTS[j], rows, 32 if j < 2 else rows, folded=folded
            )
            source = v_chain[j]
        message[0] = gram_message([of(field, OWN, 0)] + [of(v, OWN, PAD) for v in v_chain], pairs_of((first + 1,), False), columns)

    def of(buffer, rows, pad):
        return lambda block: buffer[rows, pl.ds(pl.multiple_of(block * 128 + pad, 128), 128)]

    across = 8
    run, place = tile // across, lax.rem(tile, across)
    away = sorted(
        ((i, j) for i in range(tiles // across) for j in range(across) if i or j),
        key=lambda at: -min(at[0], tiles // across - at[0]) - min(at[1], across - at[1]),
    )
    others = [
        across * lax.rem(run + i, tiles // across) + lax.rem(place + j, across) for i, j in away
    ]

    def reduce_over_tiles(index):
        for to in others:
            pltpu.make_async_remote_copy(
                src_ref=message.at[index],
                dst_ref=received.at[index, tile],
                send_sem=sum_send.at[index],
                recv_sem=sum_recv.at[index],
                device_id={"tile": to},
                device_id_type=MESH,
            ).start()

    def sum_over_tiles(index):
        all_others = received.at[index, 0 : tiles - 1]
        pltpu.make_async_copy(all_others, all_others, sum_recv.at[index]).wait()
        return jnp.sum(received[index], axis=0)

    pl.when(is_top)(functools.partial(first_chain, "top"))
    pl.when(tile == top - 1)(functools.partial(first_chain, "next"))
    pl.when(tile < top - 1)(functools.partial(first_chain, "other"))
    received[0, tile] = message[0]
    reduce_over_tiles(0)

    def more_chain(at_top):
        source = v_chain[-1]
        for j in range(second):
            if at_top:
                fold(source, 15 if j == 0 else 7, folded_p)
            operator(
                source, v_more[j], packed_mask, columns, SHIFTS[j], 8 if j == second - 1 else 16,
                24 if j == 0 else 16, pack=j == 0, folded=(folded_p, 7) if at_top else None,
            )
            source = v_more[j]

    pl.when(is_top)(functools.partial(more_chain, True))
    pl.when(jnp.logical_not(is_top))(functools.partial(more_chain, False))
    strip_rows = slice(0, 8)
    v_basis = [of(field, OWN, 0)] + [of(v, OWN, PAD) for v in v_chain] + [of(v, strip_rows, PAD) for v in v_more]

    diffusivity = h_diffusivity[0, 0]
    x_first, r_next, d_next = coefficient_cg(sum_over_tiles(0), (first + 1,), diffusivity, first, False)

    all_shifts = SHIFTS[:first] + SHIFTS[:second]

    def chain_numbers(numbers, length):
        chain = [numbers]
        for j in range(length):
            parts = {}
            for i, value in chain[-1].items():
                parts.setdefault(i + 1, []).append(value)
                if all_shifts[i] != SHIFTS[j]:
                    parts.setdefault(i, []).append((0.25 * (all_shifts[i] - SHIFTS[j])) * value)
            chain.append({i: sum(terms) for i, terms in sorted(parts.items())})
        return chain

    numbers = chain_numbers(d_next, second) + chain_numbers(r_next, second - 1)
    basis = [of(one, strip_rows, 0) for one in second_basis]

    def combine(block, carry):
        at = pl.multiple_of(block * 128, 128)
        held = [v(block) for v in v_basis]
        for one, terms in zip(second_basis, numbers):
            one[:, pl.ds(at, 128)] = tree_sum(terms[i] * held[i] for i in terms)
        return carry

    lax.fori_loop(0, blocks, combine, 0, unroll=True)
    message[1] = gram_message(basis, pairs_of((second + 1, second), True), columns)
    received[1, tile] = message[1]
    reduce_over_tiles(1)
    def part_one(block, carry):
        at = pl.multiple_of(block * 128, 128)
        result[:, pl.ds(at, 128)] = tree_sum(x_first[j] * v_basis[j](block) for j in x_first)
        return carry

    lax.fori_loop(0, blocks, part_one, 0, unroll=True)
    x_second, _, _ = coefficient_cg(sum_over_tiles(1), (second + 1, second), diffusivity, second, True)

    pieces = 4
    width = columns // pieces
    for piece in range(pieces):

        def part_two(block, carry, piece=piece):
            block = block + piece * (width // 128)
            at = pl.multiple_of(block * 128, 128)
            result[:, pl.ds(at, 128)] += tree_sum(x_second[j] * basis[j](block) for j in x_second)
            return carry

        lax.fori_loop(0, width // 128, part_two, 0, unroll=True)
        here = slice(piece * width, piece * width + width)
        pltpu.make_async_remote_copy(
            src_ref=result.at[:, here],
            dst_ref=other_out.at[:, here],
            send_sem=last_send,
            recv_sem=last_recv,
            device_id={"var": 1 - var},
            device_id_type=MESH,
        ).start()
    keep = pltpu.make_async_copy(result, solved_out, last_local)
    keep.start()

    def sent(buffer, sem):
        pltpu.make_async_copy(buffer, buffer, sem).wait()

    sent(rhs.at[0 : levels - 1], there_send)
    sent(rhs.at[0 : levels - 1], back_send)
    halo_wait(quarter_mask, mask_send, False)
    halo_wait(field, halo_send, False)
    for index in range(2):
        sent(received.at[index, 0 : tiles - 1], sum_send.at[index])
    keep.wait()
    sent(result, last_send)
    pltpu.make_async_copy(other_out, other_out, last_recv).wait()


def per_device(
    background, norm_factor, v_diffusivity, h_diffusivity, sea_mask, fold_order, coupling
):
    rows, columns = background.shape[2:]
    levels, tiles = lax.axis_size("lev"), lax.axis_size("tile")
    part = columns // levels
    f32 = jnp.float32
    strip = jax.ShapeDtypeStruct((rows, columns), f32)
    vmem = pltpu.VMEM
    tall = vmem((32, columns), f32)

    def padded(height):
        return vmem((height, columns + 2 * PAD), f32)

    first, second = ROUNDS
    blocks = columns // 128
    dma = pltpu.SemaphoreType.DMA
    in_hbm = functools.partial(pltpu.with_memory_space_constraint, memory_space=pltpu.HBM)
    solved, other = pl.pallas_call(
        kernel,
        out_shape=(strip, strip),
        in_specs=[pl.BlockSpec(memory_space=pl.ANY)] * 3
        + [pl.BlockSpec(memory_space=pltpu.SMEM)]
        + [pl.BlockSpec(memory_space=pl.ANY)] * 2,
        out_specs=(pl.BlockSpec(memory_space=pl.ANY),) * 2,
        scratch_shapes=[
            vmem((rows, columns), f32),
            vmem((rows, columns), f32),
            vmem((levels, rows, part), f32),
            vmem((rows, columns), jnp.int32),
            vmem((1, columns), jnp.int32),
            vmem((rows, columns), f32),
            vmem((levels, rows, part), f32),
            vmem((levels, rows, part), f32),
            vmem((levels, rows, part), f32),
            vmem((levels, rows, part), f32),
            vmem((levels, rows, part), f32),
            tall,
            tall,
            vmem((16, columns), f32),
            padded(32),
            [padded(32 if j == 0 else 24) for j in range(first)],
            [padded(16)] * second,
            [vmem((rows, columns), f32)] * (2 * second + 1),
            vmem((blocks, 128), jnp.int32),
            vmem((blocks, 128), jnp.int32),
            vmem((blocks, 8, 128), f32),
            vmem((blocks, 128), f32),
            vmem((2, 1, 128), f32),
            vmem((2, tiles, 1, 128), f32),
            vmem((rows, columns), f32),
            dma((5,)),
            dma,
            dma,
            dma,
            dma((levels,)),
            dma((4,)),
            dma((4,)),
            dma((4,)),
            dma((4,)),
            dma((2,)),
            dma((2,)),
            dma,
            dma,
            dma,
        ],
        compiler_params=pltpu.CompilerParams(
            collective_id=0, has_side_effects=True, vmem_limit_bytes=40 * 2**20
        ),
    )(
        in_hbm(background.reshape(rows, columns)),
        in_hbm(norm_factor.reshape(rows, columns)),
        in_hbm(v_diffusivity.reshape(levels, rows, part)),
        h_diffusivity,
        in_hbm(sea_mask.reshape(rows, columns)),
        in_hbm(fold_order.reshape(1, columns)),
    )
    return (solved + coupling[0, 0] * other)[None, None]


def solution(mesh):
    placed = (
        P("var", "lev", "tile", None),
        P("var", "lev", "tile", None),
        P("var", None, "tile", "lev"),
        P("var", "lev"),
        P("lev", "tile", None),
        P(),
        P("var", "lev", "tile", None),
    )
    return jax.shard_map(
        per_device,
        mesh=mesh,
        in_specs=placed,
        out_specs=P("var", "lev", "tile", None),
        check_vma=False,
    )
```

```python
import functools

import jax
import jax.numpy as jnp
from jax import lax
from jax.experimental import pallas as pl
from jax.experimental.pallas import tpu as pltpu
from jax.sharding import PartitionSpec as P

MESH = pl.DeviceIdType.MESH
ROUNDS = (5, 5)
SHIFTS = (0.0, 5.0, 2.0, 7.0, 0.5)
ROWS = 8
PAD = 128
OWN = slice(8, 16)


def tree_sum(terms):
    terms = list(terms)
    while len(terms) > 1:
        terms = [sum(terms[i : i + 2]) for i in range(0, len(terms), 2)]
    return terms[0]


def pairs_of(chains, last):
    count = sum(chains)
    ends = {sum(chains[: i + 1]) - 1 for i in range(len(chains))} if last else set()
    return [(i, j) for i in range(count) for j in range(i, count) if not (i in ends and j in ends)]


def gram_message(vectors, pairs, columns):
    lane = lax.broadcasted_iota(jnp.int32, (8, 128), 1)
    message = jnp.zeros((8, 128), jnp.float32)
    for at in range(0, len(pairs), 28):
        group = pairs[at : at + 28]
        used = sorted({i for pair in group for i in pair})

        def body(step, sums, group=group, used=used):
            block = lax.rem(step + 8, columns // 128)
            held = {i: vectors[i](block) for i in used}
            return tuple(total + held[i] * held[j] for total, (i, j) in zip(sums, group))

        zeros = tuple(jnp.zeros((8, 128), jnp.float32) for _ in group)
        sums = lax.fori_loop(0, columns // 128, body, zeros, unroll=True)
        for place, total in enumerate(sums):
            message = jnp.where(lane == at + place, jnp.sum(total, axis=1, keepdims=True), message)
    return jnp.sum(message, axis=0, keepdims=True)


def coefficient_cg(totals, chains, diffusivity, steps, last):
    count = sum(chains)
    first = count - chains[-1]
    totals = jnp.broadcast_to(totals, (8, 128))
    gram = {}
    for place, (i, j) in enumerate(pairs_of(chains, last)):
        gram[i, j] = gram[j, i] = jnp.broadcast_to(totals[:, place : place + 1], (8, 128))
    same, start = {}, 0
    for length in chains:
        for j in range(length - 1):
            same[start + j] = 1.0 + diffusivity * SHIFTS[j]
        start += length
    up = 4.0 * diffusivity

    def image_of(d):
        parts = {}
        for j, value in d.items():
            parts.setdefault(j, []).append(same[j] * value)
            parts.setdefault(j + 1, []).append(up * value)
        return {j: sum(terms) for j, terms in sorted(parts.items())}

    def product(u, v):
        return tree_sum(u[i] * tree_sum(gram[i, j] * v[j] for j in v) for i in u)

    def add(u, factor, v):
        return {j: (u[j] if j in u else 0.0) + (factor * v[j] if j in v else 0.0) for j in sorted({*u, *v})}

    d, r, x = {0: 1.0}, {first: 1.0}, {}
    norm_now = gram[first, first]
    for step in range(steps):
        inverse_now = jnp.where(norm_now > 1e-37, 1.0 / norm_now, 0.0)
        image = image_of(d)
        energy = product(d, image)
        size = jnp.where(energy > 0, jnp.minimum(norm_now / energy, 1.0), 0.0)
        x = add(x, size, d)
        if last and step == steps - 1:
            break
        r = add(r, -size, image)
        norm_next = jnp.maximum(product(r, r), 0.0)
        d = add(r, norm_next * inverse_now, d)
        norm_now = norm_next
    return x, r, d


def packed(tall):
    upper_half = lax.broadcasted_iota(jnp.int32, (8, 128), 0) < 4
    return jnp.concatenate([tall[8:16], jnp.where(upper_half, tall[16:24], tall[0:8])], axis=0)


def operator(source, target, quarter_mask, columns, shift, rows, loaded, odd, pack=False, folded=None, group=8):
    lane = lax.broadcasted_iota(jnp.int32, (rows, 128), 1)
    if folded is not None:
        line, last_row = folded
        is_last = lax.broadcasted_iota(jnp.int32, (rows, 128), 0) == last_row
    cut = packed if pack else lambda value: value[0:rows]

    steps = columns // (group * 128)

    def body(step, carry):
        chunk = lax.rem(steps + 2 - step, steps) if odd else lax.rem(step + 1, steps)
        at = pl.multiple_of(chunk * (group * 128), 128)
        held, ahead, behind = {}, {}, {}
        for k in range(group + 2):
            held[k] = source[0:loaded, pl.ds(at + 128 * k, 128)]
            ahead[k] = pltpu.roll(cut(held[k]), 127, 1)
            behind[k] = pltpu.roll(cut(held[k]), 1, 1)
            if k < 2:
                continue
            here = held[k - 1]
            east = jnp.where(lane == 127, ahead[k], ahead[k - 1])
            west = jnp.where(lane == 0, behind[k - 2], behind[k - 1])
            north = cut(pltpu.roll(here, loaded - 1, 0))
            south = cut(pltpu.roll(here, 1, 0))
            if folded is not None:
                north = jnp.where(is_last, line[pl.ds(chunk * group + k - 2, 1), :], north)
            here = cut(here)
            beside = (north + south) + (east + west)
            value = (1.0 - 0.25 * shift) * here if shift else here
            value = value - quarter_mask[0:rows, pl.ds(at + 128 * (k - 2), 128)] * beside
            target[0:rows, pl.ds(at + 128 * (k - 1), 128)] = value
        return carry

    lax.fori_loop(0, steps, body, 0, unroll=True)
    wrap(target, rows, columns)


def wrap(target, rows, columns):
    target[0:rows, 0:PAD] = target[0:rows, columns : columns + PAD]
    target[0:rows, columns + PAD : columns + 2 * PAD] = target[0:rows, PAD : 2 * PAD]


def kernel(
    background, norm_factor, v_diffusivity, h_diffusivity, sea_mask, fold_order,
    solved_out, other_out,
    bg, nf, vd, mask_in, fold_in, scaled, rhs, solved, inverse, below, upper,
    field, quarter_mask, packed_mask, masked, v_chain, v_more, second_basis,
    partner_row, partner_lane, lines, folded_p, message, received, result,
    load_sem, there_send, there_recv, back_send, back_recv,
    halo_send, halo_recv, mask_send, mask_recv, sum_send, sum_recv, last_send, last_recv, last_local,
):
    tile, lev, var = (lax.axis_index(a) for a in ("tile", "lev", "var"))
    tiles, levels = lax.axis_size("tile"), lax.axis_size("lev")
    columns = bg.shape[1]
    part = columns // levels
    top = tiles - 1
    blocks = columns // 128
    f32 = jnp.float32

    loads = [
        pltpu.make_async_copy(source, target, load_sem.at[i])
        for i, (source, target) in enumerate(
            ((background, bg), (norm_factor, nf), (sea_mask, mask_in), (v_diffusivity, vd), (fold_order, fold_in))
        )
    ]
    for load in loads[:2]:
        load.start()
    barrier = pltpu.get_barrier_semaphore()
    bits = (lax.rem(lev, 2), lax.rem(lev // 2, 2), lev // 4)

    def peer_level(d):
        return sum(
            (1 - bit if d >> place & 1 else bit) * (1 << place) for place, bit in enumerate(bits)
        )

    peers = [peer_level(d) for d in range(levels)]

    def greet_tile(d, carry):
        pl.semaphore_signal(barrier, inc=1, device_id={"tile": lax.rem(tile + d, tiles)}, device_id_type=MESH)
        return carry

    for d in range(1, levels):
        pl.semaphore_signal(barrier, inc=1, device_id={"lev": peers[d]}, device_id_type=MESH)
    pl.semaphore_signal(barrier, inc=1, device_id={"var": 1 - var}, device_id_type=MESH)
    lax.fori_loop(1, tiles, greet_tile, 0, unroll=True)
    for load in loads[2:]:
        load.start()
    loads[0].wait()
    loads[1].wait()
    scaled[...] = nf[...] * bg[...]
    pl.semaphore_wait(barrier, (levels - 1) + (tiles - 1) + 1)

    for d in reversed(range(1, levels)):
        pltpu.make_async_remote_copy(
            src_ref=scaled.at[:, pl.ds(pl.multiple_of(peers[d] * part, part), part)],
            dst_ref=rhs.at[lev],
            send_sem=there_send,
            recv_sem=there_recv,
            device_id={"lev": peers[d]},
            device_id_type=MESH,
        ).start()
    rhs[lev] = scaled[:, pl.ds(pl.multiple_of(lev * part, part), part)]

    sides = ((8, 16, 0, 1), (8, 16, 16, -1), (14, 16, 30, 2), (8, 10, 24, -2))

    def reached(distance):
        return tile + distance <= top if distance > 0 else tile + distance >= 0

    def halo_copies(buffer, send, recv, at, width):
        for side, (low, high, land, distance) in enumerate(sides):

            @pl.when(reached(distance))
            def _(side=side, low=low, high=high, land=land, distance=distance):
                pltpu.make_async_remote_copy(
                    src_ref=buffer.at[low:high, pl.ds(at, width)],
                    dst_ref=buffer.at[land : land + high - low, pl.ds(at, width)],
                    send_sem=send.at[side],
                    recv_sem=recv.at[side],
                    device_id={"tile": tile + distance},
                    device_id_type=MESH,
                ).start()

    def halo_wait(buffer, sem, receive):
        for side, (low, high, land, distance) in enumerate(sides):

            @pl.when(reached(-distance if receive else distance))
            def _(side=side, low=low, high=high, land=land):
                at = slice(land, land + high - low) if receive else slice(low, high)
                pltpu.make_async_copy(buffer.at[at, :], buffer.at[at, :], sem.at[side]).wait()

    loads[2].wait()
    quarter_mask[OWN, :] = 0.25 * mask_in[...].astype(f32)
    halo_copies(quarter_mask, mask_send, mask_recv, 0, columns)
    for low, high, land, distance in sides:

        @pl.when(jnp.logical_not(reached(-distance)))
        def _(land=land, rows=high - low):
            for buffer in (field, quarter_mask):
                buffer[land : land + rows, :] = jnp.zeros((rows, columns), f32)

    @pl.when(tile == top)
    def _():
        for chain in v_chain[1:]:
            chain[16:24, :] = jnp.zeros((8, chain.shape[1]), f32)

    loads[3].wait()
    above = jnp.zeros((ROWS, part), f32)
    upper_now = above
    for level in range(levels):
        coefficient = vd[level]
        inv = 1.0 / (1.0 + above + coefficient + above * upper_now)
        inverse[level] = inv
        below[level] = above * inv
        upper_now = -coefficient * inv
        upper[level] = upper_now
        above = coefficient

    loads[4].wait()

    @pl.when(tile >= top - 1)
    def _():
        order = fold_in[...]
        lane = lax.broadcasted_iota(jnp.int32, (1, columns), 1)
        mate = jnp.where(lane % 2 == 0, pltpu.roll(order, columns - 1, 1), pltpu.roll(order, 1, 1))
        row_hot = lax.broadcasted_iota(jnp.int32, (blocks, columns), 0) == order // 128
        lane_hot = lax.broadcasted_iota(jnp.int32, (128, columns), 0) == order % 128
        high = jnp.where(row_hot, (mate // 64).astype(f32), 0.0)
        low = jnp.where(row_hot, (mate % 64).astype(f32), 0.0)
        left = jnp.concatenate([high, low], axis=0).astype(jnp.bfloat16)
        right = jnp.where(lane_hot, 1.0, 0.0).astype(jnp.bfloat16)
        found = lax.dot_general(left, right, (((1,), (1,)), ((), ())), preferred_element_type=f32)
        partner = 64 * found[:blocks].astype(jnp.int32) + found[blocks:].astype(jnp.int32)
        partner_row[...] = partner // 128
        partner_lane[...] = partner % 128

    pltpu.make_async_copy(rhs.at[0 : levels - 1], rhs.at[0 : levels - 1], there_recv).wait()
    reduced = jnp.zeros((ROWS, part), f32)
    for level in range(levels):
        reduced = rhs[level] * inverse[level] + below[level] * reduced
        solved[level] = reduced
    value = jnp.zeros((ROWS, part), f32)
    for level in reversed(range(levels)):
        value = solved[level] - upper[level] * value
        solved[level] = value

    my_columns = pl.multiple_of(lev * part, part)

    for d in reversed(range(1, levels)):
        pltpu.make_async_remote_copy(
            src_ref=solved.at[peers[d]],
            dst_ref=field.at[OWN, pl.ds(my_columns, part)],
            send_sem=back_send,
            recv_sem=back_recv.at[d],
            device_id={"lev": peers[d]},
            device_id_type=MESH,
        ).start()
    field[OWN, pl.ds(my_columns, part)] = solved[lev]
    for d in range(1, levels):
        at = pl.multiple_of(peers[d] * part, part)
        here = field.at[OWN, pl.ds(at, part)]
        pltpu.make_async_copy(here, here, back_recv.at[d]).wait()
        if d % 2 == 1:
            at = pl.multiple_of(peers[d] // 2 * (2 * part), 2 * part)
            halo_copies(field, halo_send, halo_recv, at, 2 * part)

    def fold(buffer, last_row, folded):
        def repeat(block, carry):
            at = pl.multiple_of(PAD + block * 128, 128)
            lines[block] = jnp.broadcast_to(buffer[last_row : last_row + 1, pl.ds(at, 128)], (8, 128))
            return carry

        lax.fori_loop(0, blocks, repeat, 0, unroll=True)
        for q in range(blocks // 8):
            rows = slice(8 * q, 8 * q + 8)
            at_lane, at_row = partner_lane[rows, :], partner_row[rows, :]

            def pick(block, now, at_lane=at_lane, at_row=at_row):
                moved = jnp.take_along_axis(lines[block], at_lane, axis=1, mode="promise_in_bounds")
                return jnp.where(at_row == block, moved, now)

            folded[rows, :] = lax.fori_loop(0, blocks, pick, jnp.zeros((8, 128), f32), unroll=True)

    is_top = tile == top

    first, second = ROUNDS
    halo_wait(quarter_mask, mask_recv, True)

    def pack_mask(block, carry):
        at = pl.multiple_of(block * 128, 128)
        packed_mask[:, pl.ds(at, 128)] = packed(quarter_mask[0:24, pl.ds(at, 128)])
        return carry

    lax.fori_loop(0, blocks, pack_mask, 0, unroll=True)
    halo_wait(field, halo_recv, True)

    def apply_mask(block, carry):
        at = pl.multiple_of(block * 128, 128)
        masked[:, pl.ds(at + PAD, 128)] = (4.0 * quarter_mask[:, pl.ds(at, 128)]) * field[:, pl.ds(at, 128)]
        return carry

    lax.fori_loop(0, blocks, apply_mask, 0, unroll=True)
    wrap(masked, 32, columns)
    def first_chain(strip):
        source = masked
        for j in range(first):
            folded, rows = None, 24
            if strip == "top":
                fold(source, 15, folded_p)
                folded, rows = (folded_p, 15), 16
            elif strip == "next" and j < 2:
                fold(source, 23, folded_p)
                folded = (folded_p, 23)
            if j == 0:
                rows = 32
            operator(
                source, v_chain[j], quarter_mask, columns, SHIFTS[j], rows, 32 if j < 2 else rows, j % 2, folded=folded
            )
            source = v_chain[j]
        message[0] = gram_message([of(field, OWN, 0)] + [of(v, OWN, PAD) for v in v_chain], pairs_of((first + 1,), False), columns)

    def of(buffer, rows, pad):
        return lambda block: buffer[rows, pl.ds(pl.multiple_of(block * 128 + pad, 128), 128)]

    across = 8
    run, place = tile // across, lax.rem(tile, across)
    away = sorted(
        ((i, j) for i in range(tiles // across) for j in range(across) if i or j),
        key=lambda at: -min(at[0], tiles // across - at[0]) - min(at[1], across - at[1]),
    )
    others = [
        across * lax.rem(run + i, tiles // across) + lax.rem(place + j, across) for i, j in away
    ]

    def reduce_over_tiles(index):
        for to in others:
            pltpu.make_async_remote_copy(
                src_ref=message.at[index],
                dst_ref=received.at[index, tile],
                send_sem=sum_send.at[index],
                recv_sem=sum_recv.at[index],
                device_id={"tile": to},
                device_id_type=MESH,
            ).start()

    def sum_over_tiles(index):
        all_others = received.at[index, 0 : tiles - 1]
        pltpu.make_async_copy(all_others, all_others, sum_recv.at[index]).wait()
        return jnp.sum(received[index], axis=0)

    pl.when(is_top)(functools.partial(first_chain, "top"))
    pl.when(tile == top - 1)(functools.partial(first_chain, "next"))
    pl.when(tile < top - 1)(functools.partial(first_chain, "other"))
    received[0, tile] = message[0]
    reduce_over_tiles(0)

    def more_chain(at_top):
        source = v_chain[-1]
        for j in range(second):
            if at_top:
                fold(source, 15 if j == 0 else 7, folded_p)
            operator(
                source, v_more[j], packed_mask, columns, SHIFTS[j], 8 if j == second - 1 else 16,
                24 if j == 0 else 16, 1 - j % 2, pack=j == 0, folded=(folded_p, 7) if at_top else None,
            )
            source = v_more[j]

    pl.when(is_top)(functools.partial(more_chain, True))
    pl.when(jnp.logical_not(is_top))(functools.partial(more_chain, False))
    strip_rows = slice(0, 8)
    v_basis = [of(field, OWN, 0)] + [of(v, OWN, PAD) for v in v_chain] + [of(v, strip_rows, PAD) for v in v_more]

    diffusivity = h_diffusivity[0, 0]
    x_first, r_next, d_next = coefficient_cg(sum_over_tiles(0), (first + 1,), diffusivity, first, False)

    all_shifts = SHIFTS[:first] + SHIFTS[:second]

    def chain_numbers(numbers, length):
        chain = [numbers]
        for j in range(length):
            parts = {}
            for i, value in chain[-1].items():
                parts.setdefault(i + 1, []).append(value)
                if all_shifts[i] != SHIFTS[j]:
                    parts.setdefault(i, []).append((0.25 * (all_shifts[i] - SHIFTS[j])) * value)
            chain.append({i: sum(terms) for i, terms in sorted(parts.items())})
        return chain

    numbers = chain_numbers(d_next, second) + chain_numbers(r_next, second - 1)
    basis = [of(one, strip_rows, 0) for one in second_basis]

    def combine(block, carry):
        at = pl.multiple_of(block * 128, 128)
        held = [v(block) for v in v_basis]
        for one, terms in zip(second_basis, numbers):
            one[:, pl.ds(at, 128)] = tree_sum(terms[i] * held[i] for i in terms)
        return carry

    lax.fori_loop(0, blocks, combine, 0, unroll=True)
    message[1] = gram_message(basis, pairs_of((second + 1, second), True), columns)
    received[1, tile] = message[1]
    reduce_over_tiles(1)
    def part_one(block, carry):
        at = pl.multiple_of(block * 128, 128)
        result[:, pl.ds(at, 128)] = tree_sum(x_first[j] * v_basis[j](block) for j in x_first)
        return carry

    lax.fori_loop(0, blocks, part_one, 0, unroll=True)
    x_second, _, _ = coefficient_cg(sum_over_tiles(1), (second + 1, second), diffusivity, second, True)

    pieces = 4
    width = columns // pieces
    for piece in range(pieces):

        def part_two(block, carry, piece=piece):
            block = block + piece * (width // 128)
            at = pl.multiple_of(block * 128, 128)
            result[:, pl.ds(at, 128)] += tree_sum(x_second[j] * basis[j](block) for j in x_second)
            return carry

        lax.fori_loop(0, width // 128, part_two, 0, unroll=True)
        here = slice(piece * width, piece * width + width)
        pltpu.make_async_remote_copy(
            src_ref=result.at[:, here],
            dst_ref=other_out.at[:, here],
            send_sem=last_send,
            recv_sem=last_recv,
            device_id={"var": 1 - var},
            device_id_type=MESH,
        ).start()
    keep = pltpu.make_async_copy(result, solved_out, last_local)
    keep.start()

    def sent(buffer, sem):
        pltpu.make_async_copy(buffer, buffer, sem).wait()

    sent(rhs.at[0 : levels - 1], there_send)
    sent(rhs.at[0 : levels - 1], back_send)
    halo_wait(quarter_mask, mask_send, False)
    halo_wait(field, halo_send, False)
    for index in range(2):
        sent(received.at[index, 0 : tiles - 1], sum_send.at[index])
    keep.wait()
    sent(result, last_send)
    pltpu.make_async_copy(other_out, other_out, last_recv).wait()


def per_device(
    background, norm_factor, v_diffusivity, h_diffusivity, sea_mask, fold_order, coupling
):
    rows, columns = background.shape[2:]
    levels, tiles = lax.axis_size("lev"), lax.axis_size("tile")
    part = columns // levels
    f32 = jnp.float32
    strip = jax.ShapeDtypeStruct((rows, columns), f32)
    vmem = pltpu.VMEM
    tall = vmem((32, columns), f32)

    def padded(height):
        return vmem((height, columns + 2 * PAD), f32)

    first, second = ROUNDS
    blocks = columns // 128
    dma = pltpu.SemaphoreType.DMA
    in_hbm = functools.partial(pltpu.with_memory_space_constraint, memory_space=pltpu.HBM)
    solved, other = pl.pallas_call(
        kernel,
        out_shape=(strip, strip),
        in_specs=[pl.BlockSpec(memory_space=pl.ANY)] * 3
        + [pl.BlockSpec(memory_space=pltpu.SMEM)]
        + [pl.BlockSpec(memory_space=pl.ANY)] * 2,
        out_specs=(pl.BlockSpec(memory_space=pl.ANY),) * 2,
        scratch_shapes=[
            vmem((rows, columns), f32),
            vmem((rows, columns), f32),
            vmem((levels, rows, part), f32),
            vmem((rows, columns), jnp.int32),
            vmem((1, columns), jnp.int32),
            vmem((rows, columns), f32),
            vmem((levels, rows, part), f32),
            vmem((levels, rows, part), f32),
            vmem((levels, rows, part), f32),
            vmem((levels, rows, part), f32),
            vmem((levels, rows, part), f32),
            tall,
            tall,
            vmem((16, columns), f32),
            padded(32),
            [padded(32 if j == 0 else 24) for j in range(first)],
            [padded(16)] * second,
            [vmem((rows, columns), f32)] * (2 * second + 1),
            vmem((blocks, 128), jnp.int32),
            vmem((blocks, 128), jnp.int32),
            vmem((blocks, 8, 128), f32),
            vmem((blocks, 128), f32),
            vmem((2, 1, 128), f32),
            vmem((2, tiles, 1, 128), f32),
            vmem((rows, columns), f32),
            dma((5,)),
            dma,
            dma,
            dma,
            dma((levels,)),
            dma((4,)),
            dma((4,)),
            dma((4,)),
            dma((4,)),
            dma((2,)),
            dma((2,)),
            dma,
            dma,
            dma,
        ],
        compiler_params=pltpu.CompilerParams(
            collective_id=0, has_side_effects=True, vmem_limit_bytes=40 * 2**20
        ),
    )(
        in_hbm(background.reshape(rows, columns)),
        in_hbm(norm_factor.reshape(rows, columns)),
        in_hbm(v_diffusivity.reshape(levels, rows, part)),
        h_diffusivity,
        in_hbm(sea_mask.reshape(rows, columns)),
        in_hbm(fold_order.reshape(1, columns)),
    )
    return (solved + coupling[0, 0] * other)[None, None]


def solution(mesh):
    placed = (
        P("var", "lev", "tile", None),
        P("var", "lev", "tile", None),
        P("var", None, "tile", "lev"),
        P("var", "lev"),
        P("lev", "tile", None),
        P(),
        P("var", "lev", "tile", None),
    )
    return jax.shard_map(
        per_device,
        mesh=mesh,
        in_specs=placed,
        out_specs=P("var", "lev", "tile", None),
        check_vma=False,
    )
```

```python
import functools

import jax
import jax.numpy as jnp
from jax import lax
from jax.experimental import pallas as pl
from jax.experimental.pallas import tpu as pltpu
from jax.sharding import PartitionSpec as P

MESH = pl.DeviceIdType.MESH
ROUNDS = (5, 5)
SHIFTS = (0.0, 5.0, 2.0, 7.0, 0.5)
ROWS = 8
PAD = 128
OWN = slice(8, 16)


def tree_sum(terms):
    terms = list(terms)
    while len(terms) > 1:
        terms = [sum(terms[i : i + 2]) for i in range(0, len(terms), 2)]
    return terms[0]


def pairs_of(chains, last):
    count = sum(chains)
    ends = {sum(chains[: i + 1]) - 1 for i in range(len(chains))} if last else set()
    return [(i, j) for i in range(count) for j in range(i, count) if not (i in ends and j in ends)]


def gram_message(vectors, pairs, columns):
    lane = lax.broadcasted_iota(jnp.int32, (8, 128), 1)
    message = jnp.zeros((8, 128), jnp.float32)
    for at in range(0, len(pairs), 28):
        group = pairs[at : at + 28]
        used = sorted({i for pair in group for i in pair})

        def body(block, sums, group=group, used=used):
            held = {i: vectors[i](block) for i in used}
            return tuple(total + held[i] * held[j] for total, (i, j) in zip(sums, group))

        zeros = tuple(jnp.zeros((8, 128), jnp.float32) for _ in group)
        sums = lax.fori_loop(0, columns // 128, body, zeros, unroll=True)
        for place, total in enumerate(sums):
            message = jnp.where(lane == at + place, jnp.sum(total, axis=1, keepdims=True), message)
    return jnp.sum(message, axis=0, keepdims=True)


def coefficient_cg(totals, chains, diffusivity, steps, last):
    count = sum(chains)
    first = count - chains[-1]
    totals = jnp.broadcast_to(totals, (8, 128))
    gram = {}
    for place, (i, j) in enumerate(pairs_of(chains, last)):
        gram[i, j] = gram[j, i] = jnp.broadcast_to(totals[:, place : place + 1], (8, 128))
    same, start = {}, 0
    for length in chains:
        for j in range(length - 1):
            same[start + j] = 1.0 + diffusivity * SHIFTS[j]
        start += length
    up = 4.0 * diffusivity

    def image_of(d):
        parts = {}
        for j, value in d.items():
            parts.setdefault(j, []).append(same[j] * value)
            parts.setdefault(j + 1, []).append(up * value)
        return {j: sum(terms) for j, terms in sorted(parts.items())}

    def product(u, v):
        return tree_sum(u[i] * tree_sum(gram[i, j] * v[j] for j in v) for i in u)

    def add(u, factor, v):
        return {j: (u[j] if j in u else 0.0) + (factor * v[j] if j in v else 0.0) for j in sorted({*u, *v})}

    d, r, x = {0: 1.0}, {first: 1.0}, {}
    norm_now = gram[first, first]
    for step in range(steps):
        inverse_now = jnp.where(norm_now > 1e-37, 1.0 / norm_now, 0.0)
        image = image_of(d)
        energy = product(d, image)
        size = jnp.where(energy > 0, jnp.minimum(norm_now / energy, 1.0), 0.0)
        x = add(x, size, d)
        if last and step == steps - 1:
            break
        r = add(r, -size, image)
        norm_next = jnp.maximum(product(r, r), 0.0)
        d = add(r, norm_next * inverse_now, d)
        norm_now = norm_next
    return x, r, d


def packed(tall):
    upper_half = lax.broadcasted_iota(jnp.int32, (8, 128), 0) < 4
    return jnp.concatenate([tall[8:16], jnp.where(upper_half, tall[16:24], tall[0:8])], axis=0)


def operator(source, target, quarter_mask, columns, shift, rows, loaded, pack=False, folded=None, group=8):
    lane = lax.broadcasted_iota(jnp.int32, (rows, 128), 1)
    if folded is not None:
        line, last_row = folded
        is_last = lax.broadcasted_iota(jnp.int32, (rows, 128), 0) == last_row
    cut = packed if pack else lambda value: value[0:rows]

    def body(chunk, carry):
        at = pl.multiple_of(chunk * (group * 128), 128)
        held, ahead, behind = {}, {}, {}
        for k in range(group + 2):
            held[k] = source[0:loaded, pl.ds(at + 128 * k, 128)]
            ahead[k] = pltpu.roll(cut(held[k]), 127, 1)
            behind[k] = pltpu.roll(cut(held[k]), 1, 1)
            if k < 2:
                continue
            here = held[k - 1]
            east = jnp.where(lane == 127, ahead[k], ahead[k - 1])
            west = jnp.where(lane == 0, behind[k - 2], behind[k - 1])
            north = cut(pltpu.roll(here, loaded - 1, 0))
            south = cut(pltpu.roll(here, 1, 0))
            if folded is not None:
                north = jnp.where(is_last, line[pl.ds(chunk * group + k - 2, 1), :], north)
            here = cut(here)
            beside = (north + south) + (east + west)
            value = (1.0 - 0.25 * shift) * here if shift else here
            value = value - quarter_mask[0:rows, pl.ds(at + 128 * (k - 2), 128)] * beside
            target[0:rows, pl.ds(at + 128 * (k - 1), 128)] = value
        return carry

    lax.fori_loop(0, columns // (group * 128), body, 0, unroll=True)
    wrap(target, rows, columns)


def wrap(target, rows, columns):
    target[0:rows, 0:PAD] = target[0:rows, columns : columns + PAD]
    target[0:rows, columns + PAD : columns + 2 * PAD] = target[0:rows, PAD : 2 * PAD]


def kernel(
    background, norm_factor, v_diffusivity, h_diffusivity, sea_mask, fold_order,
    solved_out, other_out,
    bg, nf, vd, mask_in, fold_in, scaled, rhs, solved, inverse, below, upper,
    field, quarter_mask, packed_mask, masked, v_chain, v_more, second_basis,
    partner_row, partner_lane, lines, folded_p, message, received, result,
    load_sem, there_send, there_recv, back_send, back_recv,
    halo_send, halo_recv, mask_send, mask_recv, sum_send, sum_recv, last_send, last_recv, last_local,
):
    tile, lev, var = (lax.axis_index(a) for a in ("tile", "lev", "var"))
    tiles, levels = lax.axis_size("tile"), lax.axis_size("lev")
    columns = bg.shape[1]
    part = columns // levels
    top = tiles - 1
    blocks = columns // 128
    f32 = jnp.float32

    loads = [
        pltpu.make_async_copy(source, target, load_sem.at[i])
        for i, (source, target) in enumerate(
            ((background, bg), (norm_factor, nf), (sea_mask, mask_in), (v_diffusivity, vd), (fold_order, fold_in))
        )
    ]
    for load in loads[:2]:
        load.start()
    barrier = pltpu.get_barrier_semaphore()
    bits = (lax.rem(lev, 2), lax.rem(lev // 2, 2), lev // 4)

    def peer_level(d):
        return sum(
            (1 - bit if d >> place & 1 else bit) * (1 << place) for place, bit in enumerate(bits)
        )

    peers = [peer_level(d) for d in range(levels)]

    def greet_tile(d, carry):
        pl.semaphore_signal(barrier, inc=1, device_id={"tile": lax.rem(tile + d, tiles)}, device_id_type=MESH)
        return carry

    for d in range(1, levels):
        pl.semaphore_signal(barrier, inc=1, device_id={"lev": peers[d]}, device_id_type=MESH)
    pl.semaphore_signal(barrier, inc=1, device_id={"var": 1 - var}, device_id_type=MESH)
    lax.fori_loop(1, tiles, greet_tile, 0, unroll=True)
    for load in loads[2:]:
        load.start()
    loads[0].wait()
    loads[1].wait()
    scaled[...] = nf[...] * bg[...]
    pl.semaphore_wait(barrier, (levels - 1) + (tiles - 1) + 1)

    for d in reversed(range(1, levels)):
        pltpu.make_async_remote_copy(
            src_ref=scaled.at[:, pl.ds(pl.multiple_of(peers[d] * part, part), part)],
            dst_ref=rhs.at[lev],
            send_sem=there_send,
            recv_sem=there_recv,
            device_id={"lev": peers[d]},
            device_id_type=MESH,
        ).start()
    rhs[lev] = scaled[:, pl.ds(pl.multiple_of(lev * part, part), part)]

    sides = ((8, 16, 0, 1), (8, 16, 16, -1), (14, 16, 30, 2), (8, 10, 24, -2))

    def reached(distance):
        return tile + distance <= top if distance > 0 else tile + distance >= 0

    def halo_copies(buffer, send, recv, at, width):
        for side, (low, high, land, distance) in enumerate(sides):

            @pl.when(reached(distance))
            def _(side=side, low=low, high=high, land=land, distance=distance):
                pltpu.make_async_remote_copy(
                    src_ref=buffer.at[low:high, pl.ds(at, width)],
                    dst_ref=buffer.at[land : land + high - low, pl.ds(at, width)],
                    send_sem=send.at[side],
                    recv_sem=recv.at[side],
                    device_id={"tile": tile + distance},
                    device_id_type=MESH,
                ).start()

    def halo_wait(buffer, sem, receive):
        for side, (low, high, land, distance) in enumerate(sides):

            @pl.when(reached(-distance if receive else distance))
            def _(side=side, low=low, high=high, land=land):
                at = slice(land, land + high - low) if receive else slice(low, high)
                pltpu.make_async_copy(buffer.at[at, :], buffer.at[at, :], sem.at[side]).wait()

    loads[2].wait()
    quarter_mask[OWN, :] = 0.25 * mask_in[...].astype(f32)
    halo_copies(quarter_mask, mask_send, mask_recv, 0, columns)
    for low, high, land, distance in sides:

        @pl.when(jnp.logical_not(reached(-distance)))
        def _(land=land, rows=high - low):
            for buffer in (field, quarter_mask):
                buffer[land : land + rows, :] = jnp.zeros((rows, columns), f32)

    @pl.when(tile == top)
    def _():
        for chain in v_chain[1:]:
            chain[16:24, :] = jnp.zeros((8, chain.shape[1]), f32)

    loads[3].wait()
    above = jnp.zeros((ROWS, part), f32)
    upper_now = above
    for level in range(levels):
        coefficient = vd[level]
        inv = 1.0 / (1.0 + above + coefficient + above * upper_now)
        inverse[level] = inv
        below[level] = above * inv
        upper_now = -coefficient * inv
        upper[level] = upper_now
        above = coefficient

    loads[4].wait()

    @pl.when(tile >= top - 1)
    def _():
        order = fold_in[...]
        lane = lax.broadcasted_iota(jnp.int32, (1, columns), 1)
        mate = jnp.where(lane % 2 == 0, pltpu.roll(order, columns - 1, 1), pltpu.roll(order, 1, 1))
        row_hot = lax.broadcasted_iota(jnp.int32, (blocks, columns), 0) == order // 128
        lane_hot = lax.broadcasted_iota(jnp.int32, (128, columns), 0) == order % 128
        high = jnp.where(row_hot, (mate // 64).astype(f32), 0.0)
        low = jnp.where(row_hot, (mate % 64).astype(f32), 0.0)
        left = jnp.concatenate([high, low], axis=0).astype(jnp.bfloat16)
        right = jnp.where(lane_hot, 1.0, 0.0).astype(jnp.bfloat16)
        found = lax.dot_general(left, right, (((1,), (1,)), ((), ())), preferred_element_type=f32)
        partner = 64 * found[:blocks].astype(jnp.int32) + found[blocks:].astype(jnp.int32)
        partner_row[...] = partner // 128
        partner_lane[...] = partner % 128

    pltpu.make_async_copy(rhs.at[0 : levels - 1], rhs.at[0 : levels - 1], there_recv).wait()
    reduced = jnp.zeros((ROWS, part), f32)
    for level in range(levels):
        reduced = rhs[level] * inverse[level] + below[level] * reduced
        solved[level] = reduced
    value = jnp.zeros((ROWS, part), f32)
    for level in reversed(range(levels)):
        value = solved[level] - upper[level] * value
        solved[level] = value

    my_columns = pl.multiple_of(lev * part, part)

    for d in reversed(range(1, levels)):
        pltpu.make_async_remote_copy(
            src_ref=solved.at[peers[d]],
            dst_ref=field.at[OWN, pl.ds(my_columns, part)],
            send_sem=back_send,
            recv_sem=back_recv.at[d],
            device_id={"lev": peers[d]},
            device_id_type=MESH,
        ).start()
    field[OWN, pl.ds(my_columns, part)] = solved[lev]
    for d in range(1, levels):
        at = pl.multiple_of(peers[d] * part, part)
        here = field.at[OWN, pl.ds(at, part)]
        pltpu.make_async_copy(here, here, back_recv.at[d]).wait()
        if d >= levels - 2:
            halo_copies(field, halo_send, halo_recv, at, part)
        elif d % 2 == 1:
            at = pl.multiple_of(peers[d] // 2 * (2 * part), 2 * part)
            halo_copies(field, halo_send, halo_recv, at, 2 * part)

    def fold(buffer, last_row, folded):
        def repeat(block, carry):
            at = pl.multiple_of(PAD + block * 128, 128)
            lines[block] = jnp.broadcast_to(buffer[last_row : last_row + 1, pl.ds(at, 128)], (8, 128))
            return carry

        lax.fori_loop(0, blocks, repeat, 0, unroll=True)
        for q in range(blocks // 8):
            rows = slice(8 * q, 8 * q + 8)
            at_lane, at_row = partner_lane[rows, :], partner_row[rows, :]

            def pick(block, now, at_lane=at_lane, at_row=at_row):
                moved = jnp.take_along_axis(lines[block], at_lane, axis=1, mode="promise_in_bounds")
                return jnp.where(at_row == block, moved, now)

            folded[rows, :] = lax.fori_loop(0, blocks, pick, jnp.zeros((8, 128), f32), unroll=True)

    is_top = tile == top

    first, second = ROUNDS
    halo_wait(quarter_mask, mask_recv, True)

    def pack_mask(block, carry):
        at = pl.multiple_of(block * 128, 128)
        packed_mask[:, pl.ds(at, 128)] = packed(quarter_mask[0:24, pl.ds(at, 128)])
        return carry

    lax.fori_loop(0, blocks, pack_mask, 0, unroll=True)
    halo_wait(field, halo_recv, True)

    def apply_mask(block, carry):
        at = pl.multiple_of(block * 128, 128)
        masked[:, pl.ds(at + PAD, 128)] = (4.0 * quarter_mask[:, pl.ds(at, 128)]) * field[:, pl.ds(at, 128)]
        return carry

    lax.fori_loop(0, blocks, apply_mask, 0, unroll=True)
    wrap(masked, 32, columns)
    def first_chain(strip):
        source = masked
        for j in range(first):
            folded, rows = None, 24
            if strip == "top":
                fold(source, 15, folded_p)
                folded, rows = (folded_p, 15), 16
            elif strip == "next" and j < 2:
                fold(source, 23, folded_p)
                folded = (folded_p, 23)
            if j == 0:
                rows = 32
            operator(
                source, v_chain[j], quarter_mask, columns, SHIFTS[j], rows, 32 if j < 2 else rows, folded=folded
            )
            source = v_chain[j]
        message[0] = gram_message([of(field, OWN, 0)] + [of(v, OWN, PAD) for v in v_chain], pairs_of((first + 1,), False), columns)

    def of(buffer, rows, pad):
        return lambda block: buffer[rows, pl.ds(pl.multiple_of(block * 128 + pad, 128), 128)]

    across = 8
    run, place = tile // across, lax.rem(tile, across)
    away = sorted(
        ((i, j) for i in range(tiles // across) for j in range(across) if i or j),
        key=lambda at: -min(at[0], tiles // across - at[0]) - min(at[1], across - at[1]),
    )
    others = [
        across * lax.rem(run + i, tiles // across) + lax.rem(place + j, across) for i, j in away
    ]

    def reduce_over_tiles(index):
        for to in others:
            pltpu.make_async_remote_copy(
                src_ref=message.at[index],
                dst_ref=received.at[index, tile],
                send_sem=sum_send.at[index],
                recv_sem=sum_recv.at[index],
                device_id={"tile": to},
                device_id_type=MESH,
            ).start()

    def sum_over_tiles(index):
        all_others = received.at[index, 0 : tiles - 1]
        pltpu.make_async_copy(all_others, all_others, sum_recv.at[index]).wait()
        return jnp.sum(received[index], axis=0)

    pl.when(is_top)(functools.partial(first_chain, "top"))
    pl.when(tile == top - 1)(functools.partial(first_chain, "next"))
    pl.when(tile < top - 1)(functools.partial(first_chain, "other"))
    received[0, tile] = message[0]
    reduce_over_tiles(0)

    def more_chain(at_top):
        source = v_chain[-1]
        for j in range(second):
            if at_top:
                fold(source, 15 if j == 0 else 7, folded_p)
            operator(
                source, v_more[j], packed_mask, columns, SHIFTS[j], 8 if j == second - 1 else 16,
                24 if j == 0 else 16, pack=j == 0, folded=(folded_p, 7) if at_top else None,
            )
            source = v_more[j]

    pl.when(is_top)(functools.partial(more_chain, True))
    pl.when(jnp.logical_not(is_top))(functools.partial(more_chain, False))
    strip_rows = slice(0, 8)
    v_basis = [of(field, OWN, 0)] + [of(v, OWN, PAD) for v in v_chain] + [of(v, strip_rows, PAD) for v in v_more]

    diffusivity = h_diffusivity[0, 0]
    x_first, r_next, d_next = coefficient_cg(sum_over_tiles(0), (first + 1,), diffusivity, first, False)

    all_shifts = SHIFTS[:first] + SHIFTS[:second]

    def chain_numbers(numbers, length):
        chain = [numbers]
        for j in range(length):
            parts = {}
            for i, value in chain[-1].items():
                parts.setdefault(i + 1, []).append(value)
                if all_shifts[i] != SHIFTS[j]:
                    parts.setdefault(i, []).append((0.25 * (all_shifts[i] - SHIFTS[j])) * value)
            chain.append({i: sum(terms) for i, terms in sorted(parts.items())})
        return chain

    numbers = chain_numbers(d_next, second) + chain_numbers(r_next, second - 1)
    basis = [of(one, strip_rows, 0) for one in second_basis]

    def combine(block, carry):
        at = pl.multiple_of(block * 128, 128)
        held = [v(block) for v in v_basis]
        for one, terms in zip(second_basis, numbers):
            one[:, pl.ds(at, 128)] = tree_sum(terms[i] * held[i] for i in terms)
        return carry

    lax.fori_loop(0, blocks, combine, 0, unroll=True)
    message[1] = gram_message(basis, pairs_of((second + 1, second), True), columns)
    received[1, tile] = message[1]
    reduce_over_tiles(1)
    def part_one(block, carry):
        at = pl.multiple_of(block * 128, 128)
        result[:, pl.ds(at, 128)] = tree_sum(x_first[j] * v_basis[j](block) for j in x_first)
        return carry

    lax.fori_loop(0, blocks, part_one, 0, unroll=True)
    x_second, _, _ = coefficient_cg(sum_over_tiles(1), (second + 1, second), diffusivity, second, True)

    pieces = 4
    width = columns // pieces
    for piece in range(pieces):

        def part_two(block, carry, piece=piece):
            block = block + piece * (width // 128)
            at = pl.multiple_of(block * 128, 128)
            result[:, pl.ds(at, 128)] += tree_sum(x_second[j] * basis[j](block) for j in x_second)
            return carry

        lax.fori_loop(0, width // 128, part_two, 0, unroll=True)
        here = slice(piece * width, piece * width + width)
        pltpu.make_async_remote_copy(
            src_ref=result.at[:, here],
            dst_ref=other_out.at[:, here],
            send_sem=last_send,
            recv_sem=last_recv,
            device_id={"var": 1 - var},
            device_id_type=MESH,
        ).start()
    keep = pltpu.make_async_copy(result, solved_out, last_local)
    keep.start()

    def sent(buffer, sem):
        pltpu.make_async_copy(buffer, buffer, sem).wait()

    sent(rhs.at[0 : levels - 1], there_send)
    sent(rhs.at[0 : levels - 1], back_send)
    halo_wait(quarter_mask, mask_send, False)
    halo_wait(field, halo_send, False)
    for index in range(2):
        sent(received.at[index, 0 : tiles - 1], sum_send.at[index])
    keep.wait()
    sent(result, last_send)
    pltpu.make_async_copy(other_out, other_out, last_recv).wait()


def per_device(
    background, norm_factor, v_diffusivity, h_diffusivity, sea_mask, fold_order, coupling
):
    rows, columns = background.shape[2:]
    levels, tiles = lax.axis_size("lev"), lax.axis_size("tile")
    part = columns // levels
    f32 = jnp.float32
    strip = jax.ShapeDtypeStruct((rows, columns), f32)
    vmem = pltpu.VMEM
    tall = vmem((32, columns), f32)

    def padded(height):
        return vmem((height, columns + 2 * PAD), f32)

    first, second = ROUNDS
    blocks = columns // 128
    dma = pltpu.SemaphoreType.DMA
    in_hbm = functools.partial(pltpu.with_memory_space_constraint, memory_space=pltpu.HBM)
    solved, other = pl.pallas_call(
        kernel,
        out_shape=(strip, strip),
        in_specs=[pl.BlockSpec(memory_space=pl.ANY)] * 3
        + [pl.BlockSpec(memory_space=pltpu.SMEM)]
        + [pl.BlockSpec(memory_space=pl.ANY)] * 2,
        out_specs=(pl.BlockSpec(memory_space=pl.ANY),) * 2,
        scratch_shapes=[
            vmem((rows, columns), f32),
            vmem((rows, columns), f32),
            vmem((levels, rows, part), f32),
            vmem((rows, columns), jnp.int32),
            vmem((1, columns), jnp.int32),
            vmem((rows, columns), f32),
            vmem((levels, rows, part), f32),
            vmem((levels, rows, part), f32),
            vmem((levels, rows, part), f32),
            vmem((levels, rows, part), f32),
            vmem((levels, rows, part), f32),
            tall,
            tall,
            vmem((16, columns), f32),
            padded(32),
            [padded(32 if j == 0 else 24) for j in range(first)],
            [padded(16)] * second,
            [vmem((rows, columns), f32)] * (2 * second + 1),
            vmem((blocks, 128), jnp.int32),
            vmem((blocks, 128), jnp.int32),
            vmem((blocks, 8, 128), f32),
            vmem((blocks, 128), f32),
            vmem((2, 1, 128), f32),
            vmem((2, tiles, 1, 128), f32),
            vmem((rows, columns), f32),
            dma((5,)),
            dma,
            dma,
            dma,
            dma((levels,)),
            dma((4,)),
            dma((4,)),
            dma((4,)),
            dma((4,)),
            dma((2,)),
            dma((2,)),
            dma,
            dma,
            dma,
        ],
        compiler_params=pltpu.CompilerParams(
            collective_id=0, has_side_effects=True, vmem_limit_bytes=40 * 2**20
        ),
    )(
        in_hbm(background.reshape(rows, columns)),
        in_hbm(norm_factor.reshape(rows, columns)),
        in_hbm(v_diffusivity.reshape(levels, rows, part)),
        h_diffusivity,
        in_hbm(sea_mask.reshape(rows, columns)),
        in_hbm(fold_order.reshape(1, columns)),
    )
    return (solved + coupling[0, 0] * other)[None, None]


def solution(mesh):
    placed = (
        P("var", "lev", "tile", None),
        P("var", "lev", "tile", None),
        P("var", None, "tile", "lev"),
        P("var", "lev"),
        P("lev", "tile", None),
        P(),
        P("var", "lev", "tile", None),
    )
    return jax.shard_map(
        per_device,
        mesh=mesh,
        in_specs=placed,
        out_specs=P("var", "lev", "tile", None),
        check_vma=False,
    )
```
